256 devices in a mesh: seq: 32 (over y, z_lo, core), fsdp: 8 (over x, z_hi).
Axes of the slice: x: 4, y: 4, z: 8 (z_hi: 2, z_lo: 4; z = z_hi * 4 + z_lo), core: 2. Of those that a mesh axis runs over, the one named last changes fastest.
Arguments:
- queries: bfloat16 [8, 16384, 1024], P('fsdp', 'seq'), may hold values from -10.5 to 10.5
- key_vectors: bfloat16 [8, 16384, 1024], P('fsdp', 'seq'), may hold values from -10.5 to 10.5
- value_vectors: bfloat16 [8, 16384, 1024], P('fsdp', 'seq'), may hold values from -6 to 6
- grad_mixed: bfloat16 [8, 16384, 2048], P('fsdp', 'seq'), may hold values from -24 to 24
- out_weight: bfloat16 [1024, 2048], P('fsdp'), may hold values from -0.1875 to 0.1875
- head_phase: int32 [8], replicated, may hold values from 0 to 3
- segments_short: int32 [15], replicated, may hold values from 1 to 2048, 16384 in all
- segments_long: int32 [3], replicated, may hold values from 1 to 8192, as said below
Outputs:
- grad_query: bfloat16 [8, 16384, 1024], P('fsdp', 'seq')
- grad_key: bfloat16 [8, 16384, 1024], P('fsdp', 'seq')
- grad_value: bfloat16 [8, 16384, 1024], P('fsdp', 'seq')
The draws below stay inside these ranges and needn't reach their ends.
Inputs may be any that keep to these rules, and one draw needn't show every extreme that they name: `segments_long`: lengths that sum to 16384; the last of them is 8192, the others are shorter.
All inputs are finite; a program needn't handle non-finite values.
Results may differ from the reference program's by a relative error of at most 0.0095.
Values may be sent and summed in bfloat16 or wider, within the bound.
A program may use at most 256 MiB of HBM per device.

```python
import math
import jax
import jax.numpy as jnp
import numpy as np
from jax import lax

D = 2048
HEADS = 8
HS = 128
TOK_DEV = 512
SEG_SHORT = 2048
SEG_LONG = 8192
GROUPS = 8
L = 16384
REACH_SHORT = 4
REACH_LONG = 16
NSEG_SHORT = 15
NSEG_LONG = 3
N_SEQ = 32


def draw_queries(key, part):
    drawn = jnp.clip(jax.random.normal(jax.random.fold_in(key, 21), (GROUPS, L, HEADS * HS), jnp.float32), -6.0, 6.0)
    return drawn.astype(jnp.bfloat16)


def draw_key_vectors(key, part):
    drawn = jnp.clip(jax.random.normal(jax.random.fold_in(key, 22), (GROUPS, L, HEADS * HS), jnp.float32), -6.0, 6.0)
    return drawn.astype(jnp.bfloat16)


def split_lengths(key, total, count):
    base = total // count
    extra = total % count
    places = jnp.arange(count, dtype=jnp.int32)
    pieces = base + (places < extra).astype(jnp.int32)
    if count > 1:
        room = max(min(base - 1, SEG_LONG - base - 2), 0)
        moves = jax.random.randint(key, (count - 1,), 0, room + 1, dtype=jnp.int32)
        zero_one = jnp.zeros((1,), jnp.int32)
        pieces = pieces + jnp.concatenate([moves, zero_one]) - jnp.concatenate([zero_one, moves])
    return pieces.astype(jnp.int32)


def draw_segments_long(key, part):
    if NSEG_LONG == 1:
        return jnp.full((1,), L, jnp.int32)
    before = split_lengths(jax.random.fold_in(key, 32), L - SEG_LONG, NSEG_LONG - 1)
    return jnp.concatenate([before, jnp.full((1,), SEG_LONG, jnp.int32)]).astype(jnp.int32)


def plant(result, own_key, least, high):
    longest = result.shape.index(max(result.shape))
    spots = []
    for shift in (0, 1):
        where = [jax.random.randint(jax.random.fold_in(own_key, axis), (), 0, length) for axis, length in enumerate(result.shape)]
        where[longest] = (where[longest] + shift) % result.shape[longest]
        spots.append(tuple(where))
    return result.at[spots[0]].set(least).at[spots[1]].set(high)


def level_of(stream_key, extent, shards, low, largest):
    loudness, own = 1.0, jax.random.fold_in(stream_key, 6)
    for dim, blocks in shards:
        heights = jnp.exp(jax.random.uniform(jax.random.fold_in(own, dim), (blocks,), jnp.float32, low / len(shards), largest / len(shards)))
        loudness = loudness * jnp.repeat(heights, extent[dim] // blocks).reshape([-1 if axis == dim else 1 for axis in range(len(extent))])
    return loudness


def length_profile(amount, total, most, lean):
    loads = [(1 << 20) // math.isqrt(rank ** lean) + 1 for rank in range(2, amount + 1)]
    rest, given = total - most - (amount - 1), [1] * (amount - 1)
    while rest > 0:
        free = [i for i in range(amount - 1) if given[i] < most]
        mass, budget = sum([loads[i] for i in free]), rest
        for i in free:
            more = min(most - given[i], max(1, budget * loads[i] // mass), rest)
            given[i] = given[i] + more
            rest = rest - more
    return np.array([most] + given)


def ragged_sizes(key, count, total, most, skew):
    if count == 2:
        one = jax.random.randint(key, (), max(1, total - most), min(most, total - 1) + 1)
        return jnp.stack([one, total - one])
    tallies = jnp.asarray(length_profile(count, total, most, skew), jnp.int32)
    twos = (count - 1) // 2
    source_of, sink = tallies[1:1 + 2 * twos:2], tallies[2:2 + 2 * twos:2]
    room = jnp.minimum(source_of - 1, most - sink)
    shifted = jax.random.randint(jax.random.fold_in(key, 1), (twos,), 0, 1 << 20) % (room + 1)
    tallies = tallies.at[1:1 + 2 * twos:2].set(source_of - shifted).at[2:2 + 2 * twos:2].set(sink + shifted)
    return tallies[jax.random.permutation(jax.random.fold_in(key, 2), count)]


def noise(own_key, dims, scale, limit, cuts=(), kind=jnp.bfloat16):
    drawn = scale * jax.random.normal(own_key, dims, jnp.float32)
    if cuts:
        drawn = drawn * level_of(own_key, dims, cuts, -0.22, 0.18)
    return jnp.clip(drawn, -limit, limit).astype(kind)


def setup_inputs(seed: int = 0) -> dict:
    key_list = jax.random.split(jax.random.key(seed), 9)
    queries = draw_queries(jax.random.fold_in(key_list[8], 71), 0)
    key_vectors = draw_key_vectors(jax.random.fold_in(key_list[8], 71), 0)
    value_vectors = noise(key_list[2], (GROUPS, L, HEADS * HS), 1.0, 6.0, ((0, 8), (1, 32)))
    grad_mixed = noise(key_list[3], (GROUPS, L, D), 4.0, 24.0, ((0, 8), (1, 32)))
    out_weight = noise(key_list[4], (HEADS * HS, D), (HEADS * HS) ** -0.5, 0.1875, ((0, 8),))
    head_phase = plant(jax.random.randint(key_list[5], (HEADS,), 0, 4), jax.random.fold_in(key_list[5], 1), 0, 3).astype(jnp.int32)
    segments_short = ragged_sizes(key_list[6], NSEG_SHORT, L, SEG_SHORT, 2).astype(jnp.int32)
    segments_long = draw_segments_long(jax.random.fold_in(key_list[8], 71), 0)
    return dict(queries=queries, key_vectors=key_vectors, value_vectors=value_vectors, grad_mixed=grad_mixed, out_weight=out_weight, head_phase=head_phase, segments_short=segments_short, segments_long=segments_long)


VERY_NEGATIVE = -1e+30

def take_half(tensor, parity):
    layout = tensor.shape
    paired = tensor.reshape(layout[:-3] + (layout[-3] // 2, 2) + layout[-2:])
    return jnp.where((parity == 0)[:, None], paired[..., 0, :, :], paired[..., 1, :, :])

def put_half(tensor, parity):
    zero_fill = jnp.zeros_like(tensor)
    first_half = jnp.where((parity == 0)[:, None], tensor, zero_fill)
    second_half = jnp.where((parity == 1)[:, None], tensor, zero_fill)
    stacked = jnp.stack([first_half, second_half], axis=-3)
    return stacked.reshape(tensor.shape[:-3] + (2 * tensor.shape[-3],) + tensor.shape[-2:])

def stat_half(tensor, parity):
    paired = tensor.reshape(tensor.shape[0], tensor.shape[1] // 2, 2)
    return jnp.where((parity == 0)[:, None], paired[:, :, 0], paired[:, :, 1])

def stat_put(tensor, parity, fill_value):
    filler = jnp.full_like(tensor, fill_value)
    first_half = jnp.where((parity == 0)[:, None], tensor, filler)
    second_half = jnp.where((parity == 1)[:, None], tensor, filler)
    return jnp.stack([first_half, second_half], axis=-1).reshape(tensor.shape[0], 2 * tensor.shape[1])

def segment_of(positions, lengths):
    seg_ends = jnp.cumsum(lengths).astype(jnp.int32)
    return lax.optimization_barrier(jnp.sum((positions[..., None] >= seg_ends).astype(jnp.int32), axis=-1))

def row_positions(shard_index, tok_dev, stride, offset, row_count):
    return shard_index * tok_dev + stride * jnp.arange(row_count, dtype=jnp.int32)[None, :] + offset[:, None]

def pair_mask(query_pos, key_pos, lengths):
    query_seg = segment_of(query_pos, lengths)
    key_seg = segment_of(key_pos, lengths)
    causal = key_pos[:, None, :] <= query_pos[:, :, None]
    same_seg = key_seg[:, None, :] == query_seg[:, :, None]
    return causal & same_seg & (key_pos[:, None, :] >= 0)

def product(pattern, left_operand, right_operand):
    return jnp.einsum(pattern, left_operand.astype(jnp.float32), right_operand.astype(jnp.float32))

def unguarded(is_live, compute, shapes):
    return compute()

def shard_grads(shard_index, query_rows, grad_rows, near_window, far_window, head_phase, segments_short, segments_long, guard_fn, product_fn):
    rows_short, head_count, head_width = query_rows.shape
    tok_dev = 2 * rows_short
    score_scale = 1.0 / math.sqrt(head_width)
    par_short = head_phase % 2
    par_long = head_phase // 2
    query_long = take_half(query_rows, par_long)
    grad_long = take_half(grad_rows, par_long)
    levels = [(query_rows, grad_rows, near_window, 2, par_short, segments_short), (query_long, grad_long, far_window, 4, head_phase, segments_long)]
    stored = []
    peak_list = []
    for query_here, grad_here, window, stride, offset, lengths in levels:
        row_count = query_here.shape[0]
        query_pos = row_positions(shard_index, tok_dev, stride, offset, row_count)
        blocks = []
        top_here = jnp.full((head_count, row_count), VERY_NEGATIVE, jnp.float32)
        for distance in range(len(window)):
            key_pos = row_positions(shard_index - distance, tok_dev, stride, offset, row_count)
            live_pairs = pair_mask(query_pos, key_pos, lengths)

            def score_block(query_here=query_here, key_here=window[distance][0]):
                return (product_fn('qhd,khd->hqk', query_here, key_here) * score_scale,)
            raw_scores = guard_fn(jnp.any(live_pairs), score_block, ((head_count, row_count, row_count),))[0]
            scores = jnp.where(live_pairs, raw_scores, VERY_NEGATIVE)
            top_here = jnp.maximum(top_here, lax.optimization_barrier(jnp.max(scores, axis=-1)))
            blocks.append((live_pairs, scores))
        stored.append(blocks)
        peak_list.append(top_here)
    top_short = jnp.maximum(peak_list[0], stat_put(peak_list[1], par_long, VERY_NEGATIVE))
    level_tops = [top_short, stat_half(top_short, par_long)]
    totals = []
    numerators = []
    for level_index, (query_here, grad_here, window, stride, offset, lengths) in enumerate(levels):
        row_count = query_here.shape[0]
        total_here = jnp.zeros((head_count, row_count), jnp.float32)
        numer_here = jnp.zeros((row_count, head_count, head_width), jnp.float32)
        for distance, (live_pairs, scores) in enumerate(stored[level_index]):
            weights = jnp.where(live_pairs, jnp.exp(scores - level_tops[level_index][:, :, None]), 0.0)
            total_here = total_here + lax.optimization_barrier(jnp.sum(weights, axis=-1))

            def weight_block(weights=weights, value_here=window[distance][1]):
                return (product_fn('hqk,khd->qhd', weights.astype(jnp.bfloat16), value_here),)
            numer_here = numer_here + guard_fn(jnp.any(live_pairs), weight_block, ((row_count, head_count, head_width),))[0]
        totals.append(total_here)
        numerators.append(numer_here)
    denominator = totals[0] + stat_put(totals[1], par_long, 0.0)
    attended = (numerators[0] + put_half(numerators[1], par_long)) / jnp.transpose(denominator)[:, :, None]
    delta_rows = jnp.transpose(lax.optimization_barrier(jnp.sum(grad_rows.astype(jnp.float32) * attended, axis=-1)))
    inverse = 1.0 / denominator
    level_inverse = [inverse, stat_half(inverse, par_long)]
    level_delta = [delta_rows, stat_half(delta_rows, par_long)]
    grad_levels = []
    part_levels = []
    for level_index, (query_here, grad_here, window, stride, offset, lengths) in enumerate(levels):
        row_count = query_here.shape[0]
        grad_sum = jnp.zeros((row_count, head_count, head_width), jnp.float32)
        part_list = []
        for distance, (live_pairs, scores) in enumerate(stored[level_index]):

            def backward_block(live_pairs=live_pairs, scores=scores, key_here=window[distance][0], value_here=window[distance][1], query_here=query_here, grad_here=grad_here, top_here=level_tops[level_index], inverse_here=level_inverse[level_index], delta_here=level_delta[level_index]):
                probability = jnp.where(live_pairs, jnp.exp(scores - top_here[:, :, None]), 0.0) * inverse_here[:, :, None]
                grad_probs = product_fn('qhd,khd->hqk', grad_here, value_here)
                grad_scores = (probability * (grad_probs - delta_here[:, :, None])).astype(jnp.bfloat16)
                return (product_fn('hqk,khd->qhd', grad_scores, key_here) * score_scale, product_fn('hqk,qhd->khd', grad_scores, query_here) * score_scale, product_fn('hqk,qhd->khd', probability.astype(jnp.bfloat16), grad_here))
            shapes = ((row_count, head_count, head_width),) * 3
            add_query, part_key, part_value = guard_fn(jnp.any(live_pairs), backward_block, shapes)
            grad_sum = grad_sum + add_query
            part_list.append((part_key, part_value))
        grad_levels.append(grad_sum)
        part_levels.append(part_list)
    grad_query = grad_levels[0] + put_half(grad_levels[1], par_long)
    near_parts = []
    for distance in range(len(near_window)):
        key_part = part_levels[0][distance][0] + put_half(part_levels[1][distance][0], par_long)
        value_part = part_levels[0][distance][1] + put_half(part_levels[1][distance][1], par_long)
        near_parts.append(jnp.stack([key_part, value_part]).astype(jnp.bfloat16))
    far_parts = [jnp.stack([part_levels[1][distance][0], part_levels[1][distance][1]]).astype(jnp.bfloat16) for distance in range(len(near_window), len(far_window))]
    return (grad_query, near_parts, far_parts)

def one_sequence(queries, key_vectors, value_vectors, grad_out, head_phase, segments_short, segments_long):
    par_short = head_phase % 2
    par_long = head_phase // 2
    rows_short = TOK_DEV // 2
    rows_long = TOK_DEV // 4
    query_all = take_half(queries.reshape(L, HEADS, HS), par_short)
    grad_all = take_half(grad_out.reshape(L, HEADS, HS), par_short)
    pair_short = jnp.stack([take_half(key_vectors.reshape(L, HEADS, HS), par_short), take_half(value_vectors.reshape(L, HEADS, HS), par_short)])
    pair_long = take_half(pair_short, par_long)
    padded_short = jnp.pad(pair_short, ((0, 0), (REACH_LONG * rows_short, 0), (0, 0), (0, 0)))
    padded_long = jnp.pad(pair_long, ((0, 0), (REACH_LONG * rows_long, 0), (0, 0), (0, 0)))

    def per_shard(accumulated, shard_index):
        query_rows = lax.dynamic_slice_in_dim(query_all, shard_index * rows_short, rows_short, 0)
        grad_rows = lax.dynamic_slice_in_dim(grad_all, shard_index * rows_short, rows_short, 0)
        near_window = [lax.dynamic_slice_in_dim(padded_short, (shard_index - distance + REACH_LONG) * rows_short, rows_short, 1) for distance in range(REACH_SHORT + 1)]
        far_window = [lax.dynamic_slice_in_dim(padded_long, (shard_index - distance + REACH_LONG) * rows_long, rows_long, 1) for distance in range(REACH_LONG + 1)]
        grad_query, near_parts, far_parts = shard_grads(shard_index, query_rows, grad_rows, near_window, far_window, head_phase, segments_short, segments_long, unguarded, product)
        for distance in range(REACH_SHORT + 1):
            place_at = (shard_index - distance + REACH_LONG) * rows_short
            current = lax.dynamic_slice_in_dim(accumulated, place_at, rows_short, 1)
            accumulated = lax.dynamic_update_slice_in_dim(accumulated, current + near_parts[distance].astype(jnp.float32), place_at, 1)
        for distance in range(REACH_SHORT + 1, REACH_LONG + 1):
            place_at = (shard_index - distance + REACH_LONG) * rows_short
            current = lax.dynamic_slice_in_dim(accumulated, place_at, rows_short, 1)
            spread = put_half(far_parts[distance - REACH_SHORT - 1].astype(jnp.float32), par_long)
            accumulated = lax.dynamic_update_slice_in_dim(accumulated, current + spread, place_at, 1)
        return (accumulated, grad_query)
    accumulated = jnp.zeros((2, (N_SEQ + REACH_LONG) * rows_short, HEADS, HS), jnp.float32)
    accumulated, grad_queries = lax.scan(per_shard, accumulated, jnp.arange(N_SEQ, dtype=jnp.int32))
    grad_query_rows = grad_queries.reshape(L // 2, HEADS, HS).astype(jnp.bfloat16)
    final_pair = accumulated[:, REACH_LONG * rows_short:].astype(jnp.bfloat16)
    grad_query = put_half(grad_query_rows, par_short).reshape(L, HEADS * HS)
    grad_key = put_half(final_pair[0], par_short).reshape(L, HEADS * HS)
    grad_value = put_half(final_pair[1], par_short).reshape(L, HEADS * HS)
    return (grad_query, grad_key, grad_value)

def reference(queries, key_vectors, value_vectors, grad_mixed, out_weight, head_phase, segments_short, segments_long):

    def per_sequence(seq_index):
        grad_out = jnp.dot(grad_mixed[seq_index], jnp.transpose(out_weight), preferred_element_type=jnp.float32).astype(jnp.bfloat16)
        return one_sequence(queries[seq_index], key_vectors[seq_index], value_vectors[seq_index], grad_out, head_phase, segments_short, segments_long)
    results = lax.map(per_sequence, jnp.arange(GROUPS, dtype=jnp.int32))
    return (results[0], results[1], results[2])
```

```python
import functools
import math

import jax
import jax.numpy as jnp
from jax import lax
from jax.experimental import pallas as pl
from jax.experimental.pallas import tpu as pltpu
from jax.sharding import PartitionSpec as P

HEADS = 8
HS = 128
TOK = 512
ROWS = 256
LROWS = 128
RING = 8
ROW_LINES = 4
NEG = -1e30
SCALE = 1.0 / math.sqrt(HS)
NT = (((1,), (1,)), ((), ()))
NN = (((1,), (0,)), ((), ()))
TN = (((0,), (0,)), ((), ()))
VMEM_LIMIT = 56 * 1024 * 1024


def dot(a, b, dims):
    return lax.dot_general(a, b, dims, preferred_element_type=jnp.float32)


def token_of(row, phase):
    other = jnp.where(phase < 2, phase + 2, phase - 2)
    return 4 * (row & (LROWS - 1)) + jnp.where(row < LROWS, phase, other)


def pick_matrix(phase):
    row = lax.broadcasted_iota(jnp.int32, (ROWS, TOK), 0)
    tok = lax.broadcasted_iota(jnp.int32, (ROWS, TOK), 1)
    return (tok == token_of(row, phase)).astype(jnp.float32).astype(jnp.bfloat16)


def spread_matrix(phase):
    row = lax.broadcasted_iota(jnp.int32, (TOK, ROWS), 1)
    tok = lax.broadcasted_iota(jnp.int32, (TOK, ROWS), 0)
    return (tok == token_of(row, phase)).astype(jnp.float32).astype(jnp.bfloat16)


def place():
    me = lax.axis_index("seq")
    return me, me // RING, lax.rem(me, RING)


def greet(line, pos, with_lines):
    barrier = pltpu.get_barrier_semaphore()
    for o in range(1, RING):
        pl.semaphore_signal(
            barrier, inc=1, device_id={"seq": line * RING + lax.rem(pos + o, RING)}
        )
    if with_lines:
        for o in (1, ROW_LINES - 1):
            pl.semaphore_signal(
                barrier, inc=1, device_id={"seq": lax.rem(line + o, ROW_LINES) * RING + pos}
            )
    pl.semaphore_wait(barrier, RING - 1 + (2 if with_lines else 0))


def send_qkv(
    phase_ref, q_ref, k_ref, v_ref, qo_ref, kvo_ref, stage, send_sem, recv_sem, hsend, hrecv
):
    me, line, pos = place()
    greet(line, pos, True)

    def packed(h):
        pick = pick_matrix(phase_ref[h])
        cols = pl.ds(pl.multiple_of(h * HS, HS), HS)
        return [dot(pick, ref[:, cols], NN).astype(jnp.bfloat16) for ref in (q_ref, k_ref, v_ref)]

    def to_peer(o, what):
        peer = line * RING + lax.rem(pos + o, RING)
        if what == 0:
            src, dst = stage.at[o, 0], qo_ref.at[pos]
        else:
            src, dst = stage.at[o, pl.ds(1, 2)], kvo_ref.at[RING + pos]
        return pltpu.make_async_remote_copy(
            src_ref=src,
            dst_ref=dst,
            send_sem=send_sem.at[what, o],
            recv_sem=recv_sem.at[what, o],
            device_id={"seq": peer},
        )

    def far(s):
        return pltpu.make_async_remote_copy(
            src_ref=kvo_ref.at[RING + s],
            dst_ref=kvo_ref.at[s],
            send_sem=hsend.at[s],
            recv_sem=hrecv.at[s],
            device_id={"seq": me + RING},
        )

    def far_long(s):
        return pltpu.make_async_remote_copy(
            src_ref=kvo_ref.at[RING + s, :, pl.ds(0, LROWS)],
            dst_ref=kvo_ref.at[s, :, pl.ds(0, LROWS)],
            send_sem=hsend.at[s],
            recv_sem=hrecv.at[s],
            device_id={"seq": me + RING},
        )

    def start(o, _):
        for i, rows in enumerate(packed(lax.rem(pos + o, RING))):
            stage[o, i] = rows
        to_peer(o, 1).start()
        to_peer(o, 0).start()
        return 0

    lax.fori_loop(1, RING, start, 0)
    own = packed(pos)
    qo_ref[pos] = own[0]
    kvo_ref[RING + pos, 0] = own[1]
    kvo_ref[RING + pos, 1] = own[2]

    def forward(o, _):
        s = lax.rem(pos + RING - o, RING)

        @pl.when(o > 0)
        def _():
            to_peer(o, 1).wait_recv()

        @pl.when((line < ROW_LINES - 1) & (s >= RING // 2))
        def _():
            far(s).start()

        @pl.when((lax.rem(line, 2) == 0) & (s < RING // 2))
        def _():
            far_long(s).start()

        return 0

    lax.fori_loop(0, RING, forward, 0)

    def finish(o, _):
        to_peer(o, 0).wait_recv()
        to_peer(o, 0).wait_send()
        to_peer(o, 1).wait_send()
        return 0

    lax.fori_loop(1, RING, finish, 0)

    def finish_far(s, _):
        @pl.when((line < ROW_LINES - 1) & (s >= RING // 2))
        def _():
            far(s).wait_send()

        @pl.when((lax.rem(line, 2) == 0) & (s < RING // 2))
        def _():
            far_long(s).wait_send()

        @pl.when((line > 0) & (s >= RING // 2))
        def _():
            far(s).wait_recv()

        @pl.when((lax.rem(line, 2) == 1) & (s < RING // 2))
        def _():
            far_long(s).wait_recv()

        return 0

    lax.fori_loop(0, RING, finish_far, 0)


def send_grad(phase_ref, g_ref, w_ref, out_ref, stage, send_sem, recv_sem):
    me, line, pos = place()
    greet(line, pos, False)

    def packed(h):
        rows = pl.ds(pl.multiple_of(h * HS, HS), HS)
        full = dot(g_ref[...], w_ref[rows, :], NT).astype(jnp.bfloat16)
        return dot(pick_matrix(phase_ref[h]), full, NN).astype(jnp.bfloat16)

    def to_peer(o):
        return pltpu.make_async_remote_copy(
            src_ref=stage.at[o],
            dst_ref=out_ref.at[pos],
            send_sem=send_sem.at[o],
            recv_sem=recv_sem.at[o],
            device_id={"seq": line * RING + lax.rem(pos + o, RING)},
        )

    def start(o, _):
        stage[o] = packed(lax.rem(pos + o, RING))
        to_peer(o).start()
        return 0

    lax.fori_loop(1, RING, start, 0)
    out_ref[pos] = packed(pos)

    def finish(o, _):
        to_peer(o).wait_recv()
        to_peer(o).wait_send()
        return 0

    lax.fori_loop(1, RING, finish, 0)


def attend(sc_ref, q_ref, kv_ref, do_ref, dq_ref, own_ref, far_ref, acc, s_sc, dp_sc, sl_sc, dpl_sc):
    phase = sc_ref[0]
    seq_start = sc_ref[1]
    acc[...] = jnp.zeros_like(acc)

    def low_of(tok, first, count):
        low = jnp.full_like(tok, seq_start)
        for n in range(count):
            end = sc_ref[first + n]
            low = jnp.where(tok >= end, jnp.maximum(low, end), low)
        return low

    def scalar_low(tok, first, count):
        low = seq_start
        for n in range(count):
            end = sc_ref[first + n]
            low = jnp.where(tok >= end, jnp.maximum(low, end), low)
        return low

    n_short, n_long = 15, 3
    key_off = token_of(lax.broadcasted_iota(jnp.int32, (ROWS, 1), 0), phase)
    lrow = lax.broadcasted_iota(jnp.int32, (4 * LROWS, 1), 0)
    long_off = (lrow // LROWS) * TOK + 4 * (lrow & (LROWS - 1)) + phase
    query_off = token_of(lax.broadcasted_iota(jnp.int32, (1, ROWS), 1), phase)

    def block(i, _):
        g = RING + i
        q = q_ref[i]
        do = do_ref[i]
        ql, dol = q[:LROWS], do[:LROWS]
        tok = g * TOK + query_off
        tokl = tok[:, :LROWS]
        low_s = low_of(tok, 2, n_short)
        low_l = low_of(tokl, 2 + n_short, n_long)
        first_s = scalar_low(g * TOK, 2, n_short) // TOK
        first_l = scalar_low(g * TOK, 2 + n_short, n_long) // (4 * TOK)
        first_s = jnp.maximum(first_s, g - 4)
        last_l = g // 4 + 1

        def long_kv(c, which):
            return kv_ref[pl.ds(4 * c, 4), which, pl.ds(0, LROWS), :].reshape(4 * LROWS, HS)

        def score(j, m):
            s = dot(kv_ref[j, 0], q, NT)
            u = j * TOK + key_off
            s = jnp.where((u >= low_s) & (u <= tok), s, NEG)
            s_sc[j - g + 4] = s
            return jnp.maximum(m, jnp.max(s, axis=0, keepdims=True))

        m = lax.fori_loop(first_s, g + 1, score, jnp.full((1, ROWS), NEG, jnp.float32))

        def score_long(c, m):
            s = dot(long_kv(c, 0), ql, NT)
            u = c * (4 * TOK) + long_off
            s = jnp.where((u >= low_l) & (u <= tokl), s, NEG)
            sl_sc[c] = s
            return jnp.maximum(m, jnp.max(s, axis=0, keepdims=True))

        ml = lax.fori_loop(first_l, last_l, score_long, m[:, :LROWS])
        m = jnp.concatenate([ml, m[:, LROWS:]], axis=1)

        def weigh(j, carry):
            l, d = carry
            p = jnp.exp((s_sc[j - g + 4] - m) * SCALE)
            dp = dot(kv_ref[j, 1], do, NT)
            s_sc[j - g + 4] = p
            dp_sc[j - g + 4] = dp
            return (
                l + jnp.sum(p, axis=0, keepdims=True),
                d + jnp.sum(p * dp, axis=0, keepdims=True),
            )

        zero = jnp.zeros((1, ROWS), jnp.float32)
        l, d = lax.fori_loop(first_s, g + 1, weigh, (zero, zero))

        def weigh_long(c, carry):
            l, d = carry
            p = jnp.exp((sl_sc[c] - ml) * SCALE)
            dp = dot(long_kv(c, 1), dol, NT)
            sl_sc[c] = p
            dpl_sc[c] = dp
            return (
                l + jnp.sum(p, axis=0, keepdims=True),
                d + jnp.sum(p * dp, axis=0, keepdims=True),
            )

        ll, dl = lax.fori_loop(first_l, last_l, weigh_long, (l[:, :LROWS], d[:, :LROWS]))
        l = jnp.concatenate([ll, l[:, LROWS:]], axis=1)
        d = jnp.concatenate([dl, d[:, LROWS:]], axis=1)
        inv = 1.0 / l
        delta = d * inv
        invl, deltal = inv[:, :LROWS], delta[:, :LROWS]

        def back(j, dqt):
            pr = s_sc[j - g + 4] * inv
            ds = (pr * (dp_sc[j - g + 4] - delta)).astype(jnp.bfloat16)
            acc[j, 1] += dot(pr.astype(jnp.bfloat16), do, NN)
            acc[j, 0] += dot(ds, q, NN)
            return dqt + dot(kv_ref[j, 0], ds, TN)

        dqt = lax.fori_loop(first_s, g + 1, back, jnp.zeros((HS, ROWS), jnp.float32))

        def back_long(c, dqt):
            pr = sl_sc[c] * invl
            ds = (pr * (dpl_sc[c] - deltal)).astype(jnp.bfloat16)
            dv = dot(pr.astype(jnp.bfloat16), dol, NN)
            dk = dot(ds, ql, NN)
            acc[pl.ds(4 * c, 4), 1, pl.ds(0, LROWS), :] += dv.reshape(4, LROWS, HS)
            acc[pl.ds(4 * c, 4), 0, pl.ds(0, LROWS), :] += dk.reshape(4, LROWS, HS)
            return dqt + dot(long_kv(c, 0), ds, TN)

        dqlt = lax.fori_loop(first_l, last_l, back_long, dqt[:, :LROWS])
        dq_ref[i, pl.ds(0, LROWS), :] = (dqlt.T * SCALE).astype(jnp.bfloat16)
        dq_ref[i, pl.ds(LROWS, LROWS), :] = (dqt[:, LROWS:].T * SCALE).astype(jnp.bfloat16)
        return 0

    lax.fori_loop(0, RING, block, 0)

    def emit(b, _):
        far_ref[b, 0] = (acc[b, 0] * SCALE).astype(jnp.bfloat16)
        far_ref[b, 1] = acc[b, 1].astype(jnp.bfloat16)
        own_ref[b, 0] = acc[RING + b, 0] * SCALE
        own_ref[b, 1] = acc[RING + b, 1]
        return 0

    lax.fori_loop(0, RING, emit, 0)


def give_back(
    phase_ref,
    dq_ref,
    own_ref,
    far_ref,
    gq_ref,
    gk_ref,
    gv_ref,
    stage,
    near,
    got_q,
    got_kv,
    send_sem,
    recv_sem,
    hsend,
    hrecv,
):
    me, line, pos = place()
    greet(line, pos, True)

    def far(s):
        return pltpu.make_async_remote_copy(
            src_ref=far_ref.at[s],
            dst_ref=near.at[s],
            send_sem=hsend.at[s],
            recv_sem=hrecv.at[s],
            device_id={"seq": me - RING},
        )

    def far_long(s):
        return pltpu.make_async_remote_copy(
            src_ref=far_ref.at[s, :, pl.ds(0, LROWS)],
            dst_ref=near.at[s, :, pl.ds(0, LROWS)],
            send_sem=hsend.at[s],
            recv_sem=hrecv.at[s],
            device_id={"seq": me - RING},
        )

    def home(o, what):
        s = lax.rem(pos + o, RING)
        if what == 0:
            src, dst = dq_ref.at[s], got_q.at[pos]
        else:
            src, dst = stage.at[s], got_kv.at[pos]
        return pltpu.make_async_remote_copy(
            src_ref=src,
            dst_ref=dst,
            send_sem=send_sem.at[what, o],
            recv_sem=recv_sem.at[what, o],
            device_id={"seq": line * RING + s},
        )

    def start_far(o, _):
        s = lax.rem(pos + o, RING)

        @pl.when((line > 0) & (s >= RING // 2))
        def _():
            far(s).start()

        @pl.when((lax.rem(line, 2) == 1) & (s < RING // 2))
        def _():
            far_long(s).start()

        return 0

    lax.fori_loop(1, RING + 1, start_far, 0)

    def start_q(o, _):
        home(o, 0).start()
        return 0

    lax.fori_loop(1, RING, start_q, 0)
    got_q[pos] = dq_ref[pos]

    def start_kv(o, _):
        s = lax.rem(pos + o, RING)
        full = (line < ROW_LINES - 1) & (s >= RING // 2)
        half = (lax.rem(line, 2) == 0) & (s < RING // 2)

        @pl.when(full)
        def _():
            far(s).wait_recv()
            stage[s] = (own_ref[s] + near[s].astype(jnp.float32)).astype(jnp.bfloat16)

        @pl.when(half)
        def _():
            far_long(s).wait_recv()
            stage[s, :, pl.ds(0, LROWS)] = (
                own_ref[s, :, pl.ds(0, LROWS)] + near[s, :, pl.ds(0, LROWS)].astype(jnp.float32)
            ).astype(jnp.bfloat16)
            stage[s, :, pl.ds(LROWS, LROWS)] = own_ref[s, :, pl.ds(LROWS, LROWS)].astype(
                jnp.bfloat16
            )

        @pl.when(jnp.logical_not(full | half))
        def _():
            stage[s] = own_ref[s].astype(jnp.bfloat16)

        @pl.when(o < RING)
        def _():
            home(o, 1).start()

        return 0

    lax.fori_loop(1, RING + 1, start_kv, 0)
    got_kv[pos] = stage[pos]

    def unpack(o, _):
        h = lax.rem(pos + RING - o, RING)

        @pl.when(o > 0)
        def _():
            home(o, 0).wait_recv()
            home(o, 1).wait_recv()

        spread = spread_matrix(phase_ref[h])
        cols = pl.ds(pl.multiple_of(h * HS, HS), HS)
        gq_ref[:, cols] = dot(spread, got_q[h], NN).astype(jnp.bfloat16)
        gk_ref[:, cols] = dot(spread, got_kv[h, 0], NN).astype(jnp.bfloat16)
        gv_ref[:, cols] = dot(spread, got_kv[h, 1], NN).astype(jnp.bfloat16)
        return 0

    lax.fori_loop(0, RING, unpack, 0)

    def finish(o, _):
        home(o, 0).wait_send()
        home(o, 1).wait_send()
        return 0

    lax.fori_loop(1, RING, finish, 0)

    def finish_far(s, _):
        @pl.when((line > 0) & (s >= RING // 2))
        def _():
            far(s).wait_send()

        @pl.when((lax.rem(line, 2) == 1) & (s < RING // 2))
        def _():
            far_long(s).wait_send()

        return 0

    lax.fori_loop(0, RING, finish_far, 0)


VM = pl.BlockSpec(memory_space=pltpu.VMEM)
SM = pl.BlockSpec(memory_space=pltpu.SMEM)
DMA = pltpu.SemaphoreType.DMA
BF = jnp.bfloat16


def shaped(*dims, dtype=BF):
    return jax.ShapeDtypeStruct(dims, dtype)


def shards(q, k, v, grad_mixed, out_weight, head_phase, segments_short, segments_long):
    me = lax.axis_index("seq")
    line, pos = me // RING, lax.rem(me, RING)
    weight = lax.all_gather(out_weight, "fsdp", axis=0, tiled=True)

    q_rows, kv_rows = pl.pallas_call(
        send_qkv,
        out_shape=(shaped(RING, ROWS, HS), shaped(2 * RING, 2, ROWS, HS)),
        in_specs=[SM, VM, VM, VM],
        out_specs=(VM, VM),
        scratch_shapes=[
            pltpu.VMEM((RING, 3, ROWS, HS), BF),
            DMA((2, RING)),
            DMA((2, RING)),
            DMA((RING,)),
            DMA((RING,)),
        ],
        compiler_params=pltpu.CompilerParams(
            collective_id=0, has_side_effects=True, vmem_limit_bytes=VMEM_LIMIT
        ),
        name="send_qkv",
    )(head_phase, q[0], k[0], v[0])

    do_rows = pl.pallas_call(
        send_grad,
        out_shape=shaped(RING, ROWS, HS),
        in_specs=[SM, VM, VM],
        out_specs=VM,
        scratch_shapes=[pltpu.VMEM((RING, ROWS, HS), BF), DMA((RING,)), DMA((RING,))],
        compiler_params=pltpu.CompilerParams(
            collective_id=1, has_side_effects=True, vmem_limit_bytes=VMEM_LIMIT
        ),
        name="send_grad",
    )(head_phase, grad_mixed[0], weight)

    origin = (line - 1) * (RING * TOK)

    def ends(lengths):
        n = lengths.shape[0]
        tri = jnp.arange(n)[None, :] <= jnp.arange(n)[:, None]
        return jnp.sum(jnp.where(tri, lengths[None, :], 0), axis=1) - origin

    phase_here = jnp.sum(jnp.where(jnp.arange(HEADS) == pos, head_phase, 0))
    scalars = jnp.concatenate(
        [jnp.stack([phase_here, -origin]), ends(segments_short), ends(segments_long)]
    ).astype(jnp.int32)
    dq_rows, own, far = pl.pallas_call(
        attend,
        out_shape=(
            shaped(RING, ROWS, HS),
            shaped(RING, 2, ROWS, HS, dtype=jnp.float32),
            shaped(RING, 2, ROWS, HS),
        ),
        in_specs=[SM, VM, VM, VM],
        out_specs=(VM, VM, VM),
        scratch_shapes=[
            pltpu.VMEM((2 * RING, 2, ROWS, HS), jnp.float32),
            pltpu.VMEM((5, ROWS, ROWS), jnp.float32),
            pltpu.VMEM((5, ROWS, ROWS), jnp.float32),
            pltpu.VMEM((4, 4 * LROWS, LROWS), jnp.float32),
            pltpu.VMEM((4, 4 * LROWS, LROWS), jnp.float32),
        ],
        compiler_params=pltpu.CompilerParams(vmem_limit_bytes=VMEM_LIMIT),
        name="attend",
    )(scalars, q_rows, kv_rows, do_rows)

    gq, gk, gv = pl.pallas_call(
        give_back,
        out_shape=(shaped(TOK, HEADS * HS),) * 3,
        in_specs=[SM, VM, VM, VM],
        out_specs=(VM,) * 3,
        scratch_shapes=[
            pltpu.VMEM((RING, 2, ROWS, HS), BF),
            pltpu.VMEM((RING, 2, ROWS, HS), BF),
            pltpu.VMEM((RING, ROWS, HS), BF),
            pltpu.VMEM((RING, 2, ROWS, HS), BF),
            DMA((2, RING)),
            DMA((2, RING)),
            DMA((RING,)),
            DMA((RING,)),
        ],
        compiler_params=pltpu.CompilerParams(
            collective_id=2, has_side_effects=True, vmem_limit_bytes=VMEM_LIMIT
        ),
        name="give_back",
    )(head_phase, dq_rows, own, far)
    return gq[None], gk[None], gv[None]


def solution(mesh):
    placed = (
        P("fsdp", "seq", None),
        P("fsdp", "seq", None),
        P("fsdp", "seq", None),
        P("fsdp", "seq", None),
        P("fsdp", None),
        P(),
        P(),
        P(),
    )
    return jax.shard_map(
        shards,
        mesh=mesh,
        in_specs=placed,
        out_specs=(P("fsdp", "seq", None), P("fsdp", "seq", None), P("fsdp", "seq", None)),
        check_vma=False,
    )
```

```python
import functools
import math

import jax
import jax.numpy as jnp
from jax import lax
from jax.experimental import pallas as pl
from jax.experimental.pallas import tpu as pltpu
from jax.sharding import PartitionSpec as P

HEADS = 8
HS = 128
TOK = 512
ROWS = 256
LROWS = 128
RING = 8
ROW_LINES = 4
XS = 4
NEG = -1e30
SCALE = 1.0 / math.sqrt(HS)
NT = (((1,), (1,)), ((), ()))
NN = (((1,), (0,)), ((), ()))
TN = (((0,), (0,)), ((), ()))
VMEM_LIMIT = 56 * 1024 * 1024


def dot(a, b, dims):
    return lax.dot_general(a, b, dims, preferred_element_type=jnp.float32)


def token_of(row, phase):
    other = jnp.where(phase < 2, phase + 2, phase - 2)
    return 4 * (row & (LROWS - 1)) + jnp.where(row < LROWS, phase, other)


def pick_matrix(phase):
    row = lax.broadcasted_iota(jnp.int32, (ROWS, TOK), 0)
    tok = lax.broadcasted_iota(jnp.int32, (ROWS, TOK), 1)
    return (tok == token_of(row, phase)).astype(jnp.float32).astype(jnp.bfloat16)


def spread_matrix(phase):
    row = lax.broadcasted_iota(jnp.int32, (TOK, ROWS), 1)
    tok = lax.broadcasted_iota(jnp.int32, (TOK, ROWS), 0)
    return (tok == token_of(row, phase)).astype(jnp.float32).astype(jnp.bfloat16)


def place():
    me = lax.axis_index("seq")
    return me, me // RING, lax.rem(me, RING)


def greet(line, pos, columns, gather):
    barrier = pltpu.get_barrier_semaphore()
    for o in range(1, RING):
        pl.semaphore_signal(
            barrier, inc=1, device_id={"seq": line * RING + lax.rem(pos + o, RING)}
        )
    for o in columns:
        pl.semaphore_signal(
            barrier, inc=1, device_id={"seq": lax.rem(line + o, ROW_LINES) * RING + pos}
        )
    total = RING - 1 + len(columns)
    if gather:
        f = lax.axis_index("fsdp")
        x, hi = f // 2, lax.rem(f, 2)
        pl.semaphore_signal(barrier, inc=1, device_id={"fsdp": 2 * x + 1 - hi})
        for o in range(1, XS):
            pl.semaphore_signal(barrier, inc=1, device_id={"fsdp": 2 * lax.rem(x + o, XS) + hi})
        total += XS
    pl.semaphore_wait(barrier, total)


def send_all(
    phase_ref,
    q_ref,
    k_ref,
    v_ref,
    g_ref,
    w_ref,
    qo_ref,
    kvo_ref,
    do_ref,
    stage,
    gstage,
    w_all,
    send_sem,
    recv_sem,
    hsend,
    hrecv,
    gsend,
    grecv,
    zsend,
    zrecv,
    ysend,
    yrecv,
    xsend,
    xrecv,
    csend,
    crecv,
):
    me, line, pos = place()
    core = lax.rem(me, 2)
    f = lax.axis_index("fsdp")
    x, hi = f // 2, lax.rem(f, 2)
    mate = 2 * x + 1 - hi
    greet(line, pos, (1, 2, 3), True)
    half = pl.ds(pl.multiple_of(core * 64, 64), 64)
    piece = pl.ds(pl.multiple_of(core * 64 + line * 16, 16), 16)

    to_mate = pltpu.make_async_remote_copy(
        src_ref=w_ref.at[piece],
        dst_ref=w_all.at[f, piece],
        send_sem=zsend,
        recv_sem=zrecv,
        device_id={"fsdp": mate},
    )

    def along_y(o):
        return pltpu.make_async_remote_copy(
            src_ref=w_all.at[mate, piece],
            dst_ref=w_all.at[mate, piece],
            send_sem=ysend.at[o],
            recv_sem=yrecv.at[o],
            device_id={"seq": lax.rem(line + o, ROW_LINES) * RING + pos},
        )

    def along_x(j, own):
        m = jnp.maximum(j - 2, 0)
        src = w_ref.at[half] if own else w_all.at[mate, half]
        return pltpu.make_async_remote_copy(
            src_ref=src,
            dst_ref=w_all.at[f if own else mate, half],
            send_sem=xsend.at[j],
            recv_sem=xrecv.at[j],
            device_id={"fsdp": 2 * lax.rem(x + lax.rem(m, 3) + 1, XS) + hi},
        )

    def slot(j):
        m = jnp.maximum(j - 2, 0)
        other = 2 * lax.rem(x + XS - 1 - lax.rem(m, 3), XS) + jnp.where(m < 3, hi, 1 - hi)
        return jnp.where(j == 0, f, jnp.where(j == 1, mate, other))

    def to_core(j):
        return pltpu.make_async_remote_copy(
            src_ref=w_all.at[slot(j), half],
            dst_ref=w_all.at[slot(j), half],
            send_sem=csend.at[j],
            recv_sem=crecv.at[j],
            device_id={"seq": me + 1 - 2 * core},
        )

    to_mate.start()
    for j in range(2, 5):
        along_x(j, True).start()

    def packed(h):
        pick = pick_matrix(phase_ref[h])
        cols = pl.ds(pl.multiple_of(h * HS, HS), HS)
        return [dot(pick, ref[:, cols], NN).astype(jnp.bfloat16) for ref in (q_ref, k_ref, v_ref)]

    def to_peer(o, what):
        peer = line * RING + lax.rem(pos + o, RING)
        if what == 0:
            src, dst = stage.at[o, 0], qo_ref.at[pos]
        else:
            src, dst = stage.at[o, pl.ds(1, 2)], kvo_ref.at[RING + pos]
        return pltpu.make_async_remote_copy(
            src_ref=src,
            dst_ref=dst,
            send_sem=send_sem.at[what, o],
            recv_sem=recv_sem.at[what, o],
            device_id={"seq": peer},
        )

    def far(s):
        return pltpu.make_async_remote_copy(
            src_ref=kvo_ref.at[RING + s],
            dst_ref=kvo_ref.at[s],
            send_sem=hsend.at[s],
            recv_sem=hrecv.at[s],
            device_id={"seq": me + RING},
        )

    def far_long(s):
        return pltpu.make_async_remote_copy(
            src_ref=kvo_ref.at[RING + s, :, pl.ds(0, LROWS)],
            dst_ref=kvo_ref.at[s, :, pl.ds(0, LROWS)],
            send_sem=hsend.at[s],
            recv_sem=hrecv.at[s],
            device_id={"seq": me + RING},
        )

    def start(o, _):
        for i, rows in enumerate(packed(lax.rem(pos + o, RING))):
            stage[o, i] = rows
        to_peer(o, 1).start()
        to_peer(o, 0).start()
        return 0

    lax.fori_loop(1, RING, start, 0)

    to_mate.wait_recv()
    for o in range(1, ROW_LINES):
        along_y(o).start()
    own = packed(pos)
    qo_ref[pos] = own[0]
    kvo_ref[RING + pos, 0] = own[1]
    kvo_ref[RING + pos, 1] = own[2]
    w_all[f] = w_ref[...]
    for o in range(1, ROW_LINES):
        along_y(o).wait_recv()
    for j in range(5, 8):
        along_x(j, False).start()
    to_core(1).start()

    def to_head(j, h):
        return pltpu.make_async_remote_copy(
            src_ref=gstage.at[j],
            dst_ref=do_ref.at[pos],
            send_sem=gsend.at[j],
            recv_sem=grecv.at[pos],
            device_id={"seq": line * RING + h},
        )

    def grad_head(j, _):
        h = slot(j)

        @pl.when((j >= 1) & (j < RING - 1))
        def _():
            along_x(j + 1, True).wait_recv()
            to_core(j + 1).start()

        @pl.when(j >= 1)
        def _():
            to_core(j).wait_recv()

        full = dot(g_ref[...], w_all[h], NT).astype(jnp.bfloat16)
        rows = dot(pick_matrix(phase_ref[h]), full, NN).astype(jnp.bfloat16)

        @pl.when(h == pos)
        def _():
            do_ref[pos] = rows

        @pl.when(h != pos)
        def _():
            gstage[j] = rows
            to_head(j, h).start()

        return 0

    lax.fori_loop(0, RING, grad_head, 0)

    def forward(o, _):
        s = lax.rem(pos + RING - o, RING)

        @pl.when(o > 0)
        def _():
            to_peer(o, 1).wait_recv()

        @pl.when((line < ROW_LINES - 1) & (s >= RING // 2))
        def _():
            far(s).start()

        @pl.when((lax.rem(line, 2) == 0) & (s < RING // 2))
        def _():
            far_long(s).start()

        return 0

    lax.fori_loop(0, RING, forward, 0)

    def finish(o, _):
        to_peer(o, 0).wait_recv()
        to_peer(o, 0).wait_send()
        to_peer(o, 1).wait_send()
        return 0

    lax.fori_loop(1, RING, finish, 0)

    def finish_grad(j, _):
        h = slot(j)

        @pl.when(h != pos)
        def _():
            to_head(j, h).wait_send()

        @pl.when(j != pos)
        def _():
            pltpu.make_async_remote_copy(
                src_ref=gstage.at[j],
                dst_ref=do_ref.at[j],
                send_sem=gsend.at[j],
                recv_sem=grecv.at[j],
                device_id={"seq": line * RING + lax.rem(pos + 1, RING)},
            ).wait_recv()

        return 0

    lax.fori_loop(0, RING, finish_grad, 0)

    def finish_far(s, _):
        @pl.when((line < ROW_LINES - 1) & (s >= RING // 2))
        def _():
            far(s).wait_send()

        @pl.when((lax.rem(line, 2) == 0) & (s < RING // 2))
        def _():
            far_long(s).wait_send()

        @pl.when((line > 0) & (s >= RING // 2))
        def _():
            far(s).wait_recv()

        @pl.when((lax.rem(line, 2) == 1) & (s < RING // 2))
        def _():
            far_long(s).wait_recv()

        return 0

    lax.fori_loop(0, RING, finish_far, 0)
    to_mate.wait_send()
    for o in range(1, ROW_LINES):
        along_y(o).wait_send()
    for j in range(2, 8):
        along_x(j, True).wait_send()
    for j in range(1, 8):
        to_core(j).wait_send()


def attend(sc_ref, q_ref, kv_ref, do_ref, dq_ref, own_ref, far_ref, acc, s_sc, dp_sc, sl_sc, dpl_sc):
    phase = sc_ref[0]
    seq_start = sc_ref[1]
    acc[...] = jnp.zeros_like(acc)

    def low_of(tok, first, count):
        low = jnp.full_like(tok, seq_start)
        for n in range(count):
            end = sc_ref[first + n]
            low = jnp.where(tok >= end, jnp.maximum(low, end), low)
        return low

    def scalar_low(tok, first, count):
        low = seq_start
        for n in range(count):
            end = sc_ref[first + n]
            low = jnp.where(tok >= end, jnp.maximum(low, end), low)
        return low

    n_short, n_long = 15, 3
    key_off = token_of(lax.broadcasted_iota(jnp.int32, (ROWS, 1), 0), phase)
    lrow = lax.broadcasted_iota(jnp.int32, (4 * LROWS, 1), 0)
    long_off = (lrow // LROWS) * TOK + 4 * (lrow & (LROWS - 1)) + phase
    query_off = token_of(lax.broadcasted_iota(jnp.int32, (1, ROWS), 1), phase)

    def block(i, _):
        g = RING + i
        q = q_ref[i]
        do = do_ref[i]
        ql, dol = q[:LROWS], do[:LROWS]
        tok = g * TOK + query_off
        tokl = tok[:, :LROWS]
        low_s = low_of(tok, 2, n_short)
        low_l = low_of(tokl, 2 + n_short, n_long)
        first_s = scalar_low(g * TOK, 2, n_short) // TOK
        first_l = scalar_low(g * TOK, 2 + n_short, n_long) // (4 * TOK)
        first_s = jnp.maximum(first_s, g - 4)
        last_l = g // 4 + 1

        def long_kv(c, which):
            return kv_ref[pl.ds(4 * c, 4), which, pl.ds(0, LROWS), :].reshape(4 * LROWS, HS)

        def score(j, m):
            s = dot(kv_ref[j, 0], q, NT)
            u = j * TOK + key_off
            s = jnp.where((u >= low_s) & (u <= tok), s, NEG)
            s_sc[j - g + 4] = s
            return jnp.maximum(m, jnp.max(s, axis=0, keepdims=True))

        m = lax.fori_loop(first_s, g + 1, score, jnp.full((1, ROWS), NEG, jnp.float32))

        def score_long(c, m):
            s = dot(long_kv(c, 0), ql, NT)
            u = c * (4 * TOK) + long_off
            s = jnp.where((u >= low_l) & (u <= tokl), s, NEG)
            sl_sc[c] = s
            return jnp.maximum(m, jnp.max(s, axis=0, keepdims=True))

        ml = lax.fori_loop(first_l, last_l, score_long, m[:, :LROWS])
        m = jnp.concatenate([ml, m[:, LROWS:]], axis=1)

        def weigh(j, carry):
            l, d = carry
            p = jnp.exp((s_sc[j - g + 4] - m) * SCALE)
            dp = dot(kv_ref[j, 1], do, NT)
            s_sc[j - g + 4] = p
            dp_sc[j - g + 4] = dp
            return (
                l + jnp.sum(p, axis=0, keepdims=True),
                d + jnp.sum(p * dp, axis=0, keepdims=True),
            )

        zero = jnp.zeros((1, ROWS), jnp.float32)
        l, d = lax.fori_loop(first_s, g + 1, weigh, (zero, zero))

        def weigh_long(c, carry):
            l, d = carry
            p = jnp.exp((sl_sc[c] - ml) * SCALE)
            dp = dot(long_kv(c, 1), dol, NT)
            sl_sc[c] = p
            dpl_sc[c] = dp
            return (
                l + jnp.sum(p, axis=0, keepdims=True),
                d + jnp.sum(p * dp, axis=0, keepdims=True),
            )

        ll, dl = lax.fori_loop(first_l, last_l, weigh_long, (l[:, :LROWS], d[:, :LROWS]))
        l = jnp.concatenate([ll, l[:, LROWS:]], axis=1)
        d = jnp.concatenate([dl, d[:, LROWS:]], axis=1)
        inv = 1.0 / l
        delta = d * inv
        invl, deltal = inv[:, :LROWS], delta[:, :LROWS]

        def back(j, dqt):
            pr = s_sc[j - g + 4] * inv
            ds = (pr * (dp_sc[j - g + 4] - delta)).astype(jnp.bfloat16)
            acc[j, 1] += dot(pr.astype(jnp.bfloat16), do, NN)
            acc[j, 0] += dot(ds, q, NN)
            return dqt + dot(kv_ref[j, 0], ds, TN)

        dqt = lax.fori_loop(first_s, g + 1, back, jnp.zeros((HS, ROWS), jnp.float32))

        def back_long(c, dqt):
            pr = sl_sc[c] * invl
            ds = (pr * (dpl_sc[c] - deltal)).astype(jnp.bfloat16)
            dv = dot(pr.astype(jnp.bfloat16), dol, NN)
            dk = dot(ds, ql, NN)
            acc[pl.ds(4 * c, 4), 1, pl.ds(0, LROWS), :] += dv.reshape(4, LROWS, HS)
            acc[pl.ds(4 * c, 4), 0, pl.ds(0, LROWS), :] += dk.reshape(4, LROWS, HS)
            return dqt + dot(long_kv(c, 0), ds, TN)

        dqlt = lax.fori_loop(first_l, last_l, back_long, dqt[:, :LROWS])
        dq_ref[i, pl.ds(0, LROWS), :] = (dqlt.T * SCALE).astype(jnp.bfloat16)
        dq_ref[i, pl.ds(LROWS, LROWS), :] = (dqt[:, LROWS:].T * SCALE).astype(jnp.bfloat16)
        return 0

    lax.fori_loop(0, RING, block, 0)

    def emit(b, _):
        far_ref[b, 0] = (acc[b, 0] * SCALE).astype(jnp.bfloat16)
        far_ref[b, 1] = acc[b, 1].astype(jnp.bfloat16)
        own_ref[b, 0] = acc[RING + b, 0] * SCALE
        own_ref[b, 1] = acc[RING + b, 1]
        return 0

    lax.fori_loop(0, RING, emit, 0)


def give_back(
    phase_ref,
    dq_ref,
    own_ref,
    far_ref,
    gq_ref,
    gk_ref,
    gv_ref,
    stage,
    near,
    got_q,
    got_kv,
    send_sem,
    recv_sem,
    hsend,
    hrecv,
):
    me, line, pos = place()
    greet(line, pos, (1, 3), False)

    def far(s):
        return pltpu.make_async_remote_copy(
            src_ref=far_ref.at[s],
            dst_ref=near.at[s],
            send_sem=hsend.at[s],
            recv_sem=hrecv.at[s],
            device_id={"seq": me - RING},
        )

    def far_long(s):
        return pltpu.make_async_remote_copy(
            src_ref=far_ref.at[s, :, pl.ds(0, LROWS)],
            dst_ref=near.at[s, :, pl.ds(0, LROWS)],
            send_sem=hsend.at[s],
            recv_sem=hrecv.at[s],
            device_id={"seq": me - RING},
        )

    def home(o, what):
        s = lax.rem(pos + o, RING)
        if what == 0:
            src, dst = dq_ref.at[s], got_q.at[pos]
        else:
            src, dst = stage.at[s], got_kv.at[pos]
        return pltpu.make_async_remote_copy(
            src_ref=src,
            dst_ref=dst,
            send_sem=send_sem.at[what, o],
            recv_sem=recv_sem.at[what, o],
            device_id={"seq": line * RING + s},
        )

    def start_far(o, _):
        s = lax.rem(pos + o, RING)

        @pl.when((line > 0) & (s >= RING // 2))
        def _():
            far(s).start()

        @pl.when((lax.rem(line, 2) == 1) & (s < RING // 2))
        def _():
            far_long(s).start()

        return 0

    lax.fori_loop(1, RING + 1, start_far, 0)

    def start_q(o, _):
        home(o, 0).start()
        return 0

    lax.fori_loop(1, RING, start_q, 0)
    got_q[pos] = dq_ref[pos]

    def start_kv(o, _):
        s = lax.rem(pos + o, RING)
        full = (line < ROW_LINES - 1) & (s >= RING // 2)
        half = (lax.rem(line, 2) == 0) & (s < RING // 2)

        @pl.when(full)
        def _():
            far(s).wait_recv()
            stage[s] = (own_ref[s] + near[s].astype(jnp.float32)).astype(jnp.bfloat16)

        @pl.when(half)
        def _():
            far_long(s).wait_recv()
            stage[s, :, pl.ds(0, LROWS)] = (
                own_ref[s, :, pl.ds(0, LROWS)] + near[s, :, pl.ds(0, LROWS)].astype(jnp.float32)
            ).astype(jnp.bfloat16)
            stage[s, :, pl.ds(LROWS, LROWS)] = own_ref[s, :, pl.ds(LROWS, LROWS)].astype(
                jnp.bfloat16
            )

        @pl.when(jnp.logical_not(full | half))
        def _():
            stage[s] = own_ref[s].astype(jnp.bfloat16)

        @pl.when(o < RING)
        def _():
            home(o, 1).start()

        return 0

    lax.fori_loop(1, RING + 1, start_kv, 0)
    got_kv[pos] = stage[pos]

    def unpack(o, _):
        h = lax.rem(pos + RING - o, RING)

        @pl.when(o > 0)
        def _():
            home(o, 0).wait_recv()
            home(o, 1).wait_recv()

        spread = spread_matrix(phase_ref[h])
        cols = pl.ds(pl.multiple_of(h * HS, HS), HS)
        gq_ref[:, cols] = dot(spread, got_q[h], NN).astype(jnp.bfloat16)
        gk_ref[:, cols] = dot(spread, got_kv[h, 0], NN).astype(jnp.bfloat16)
        gv_ref[:, cols] = dot(spread, got_kv[h, 1], NN).astype(jnp.bfloat16)
        return 0

    lax.fori_loop(0, RING, unpack, 0)

    def finish(o, _):
        home(o, 0).wait_send()
        home(o, 1).wait_send()
        return 0

    lax.fori_loop(1, RING, finish, 0)

    def finish_far(s, _):
        @pl.when((line > 0) & (s >= RING // 2))
        def _():
            far(s).wait_send()

        @pl.when((lax.rem(line, 2) == 1) & (s < RING // 2))
        def _():
            far_long(s).wait_send()

        return 0

    lax.fori_loop(0, RING, finish_far, 0)


VM = pl.BlockSpec(memory_space=pltpu.VMEM)
SM = pl.BlockSpec(memory_space=pltpu.SMEM)
DMA = pltpu.SemaphoreType.DMA
BF = jnp.bfloat16


def shaped(*dims, dtype=BF):
    return jax.ShapeDtypeStruct(dims, dtype)


def shards(q, k, v, grad_mixed, out_weight, head_phase, segments_short, segments_long):
    me = lax.axis_index("seq")
    line, pos = me // RING, lax.rem(me, RING)
    q_rows, kv_rows, do_rows = pl.pallas_call(
        send_all,
        out_shape=(
            shaped(RING, ROWS, HS),
            shaped(2 * RING, 2, ROWS, HS),
            shaped(RING, ROWS, HS),
        ),
        in_specs=[SM, VM, VM, VM, VM, VM],
        out_specs=(VM, VM, VM),
        scratch_shapes=[
            pltpu.VMEM((RING, 3, ROWS, HS), BF),
            pltpu.VMEM((RING, ROWS, HS), BF),
            pltpu.VMEM((HEADS, HS, grad_mixed.shape[2]), BF),
            DMA((2, RING)),
            DMA((2, RING)),
            DMA((RING,)),
            DMA((RING,)),
            DMA((RING,)),
            DMA((RING,)),
            DMA,
            DMA,
            DMA((ROW_LINES,)),
            DMA((ROW_LINES,)),
            DMA((RING,)),
            DMA((RING,)),
            DMA((RING,)),
            DMA((RING,)),
        ],
        compiler_params=pltpu.CompilerParams(
            collective_id=0, has_side_effects=True, vmem_limit_bytes=VMEM_LIMIT
        ),
        name="send_all",
    )(head_phase, q[0], k[0], v[0], grad_mixed[0], out_weight)

    origin = (line - 1) * (RING * TOK)

    def ends(lengths):
        n = lengths.shape[0]
        tri = jnp.arange(n)[None, :] <= jnp.arange(n)[:, None]
        return jnp.sum(jnp.where(tri, lengths[None, :], 0), axis=1) - origin

    phase_here = jnp.sum(jnp.where(jnp.arange(HEADS) == pos, head_phase, 0))
    scalars = jnp.concatenate(
        [jnp.stack([phase_here, -origin]), ends(segments_short), ends(segments_long)]
    ).astype(jnp.int32)
    dq_rows, own, far = pl.pallas_call(
        attend,
        out_shape=(
            shaped(RING, ROWS, HS),
            shaped(RING, 2, ROWS, HS, dtype=jnp.float32),
            shaped(RING, 2, ROWS, HS),
        ),
        in_specs=[SM, VM, VM, VM],
        out_specs=(VM, VM, VM),
        scratch_shapes=[
            pltpu.VMEM((2 * RING, 2, ROWS, HS), jnp.float32),
            pltpu.VMEM((5, ROWS, ROWS), jnp.float32),
            pltpu.VMEM((5, ROWS, ROWS), jnp.float32),
            pltpu.VMEM((4, 4 * LROWS, LROWS), jnp.float32),
            pltpu.VMEM((4, 4 * LROWS, LROWS), jnp.float32),
        ],
        compiler_params=pltpu.CompilerParams(vmem_limit_bytes=VMEM_LIMIT),
        name="attend",
    )(scalars, q_rows, kv_rows, do_rows)

    gq, gk, gv = pl.pallas_call(
        give_back,
        out_shape=(shaped(TOK, HEADS * HS),) * 3,
        in_specs=[SM, VM, VM, VM],
        out_specs=(VM,) * 3,
        scratch_shapes=[
            pltpu.VMEM((RING, 2, ROWS, HS), BF),
            pltpu.VMEM((RING, 2, ROWS, HS), BF),
            pltpu.VMEM((RING, ROWS, HS), BF),
            pltpu.VMEM((RING, 2, ROWS, HS), BF),
            DMA((2, RING)),
            DMA((2, RING)),
            DMA((RING,)),
            DMA((RING,)),
        ],
        compiler_params=pltpu.CompilerParams(
            collective_id=1, has_side_effects=True, vmem_limit_bytes=VMEM_LIMIT
        ),
        name="give_back",
    )(head_phase, dq_rows, own, far)
    return gq[None], gk[None], gv[None]


def solution(mesh):
    placed = (
        P("fsdp", "seq", None),
        P("fsdp", "seq", None),
        P("fsdp", "seq", None),
        P("fsdp", "seq", None),
        P("fsdp", None),
        P(),
        P(),
        P(),
    )
    return jax.shard_map(
        shards,
        mesh=mesh,
        in_specs=placed,
        out_specs=(P("fsdp", "seq", None), P("fsdp", "seq", None), P("fsdp", "seq", None)),
        check_vma=False,
    )
```

```python
import functools
import math

import jax
import jax.numpy as jnp
from jax import lax
from jax.experimental import pallas as pl
from jax.experimental.pallas import tpu as pltpu
from jax.sharding import PartitionSpec as P

HEADS = 8
HS = 128
TOK = 512
ROWS = 256
LROWS = 128
RING = 8
ROW_LINES = 4
XS = 4
PAIRS = 4
NEAR = 5
SHORT_TILES = RING * NEAR
TILES = SHORT_TILES + 2 * PAIRS * PAIRS
NEG = -1e30
SCALE = 1.0 / math.sqrt(HS)
NT = (((1,), (1,)), ((), ()))
NN = (((1,), (0,)), ((), ()))
TN = (((0,), (0,)), ((), ()))
VMEM_LIMIT = 60 * 1024 * 1024


def dot(a, b, dims):
    return lax.dot_general(a, b, dims, preferred_element_type=jnp.float32)


def token_of(row, phase):
    other = jnp.where(phase < 2, phase + 2, phase - 2)
    return 4 * (row & (LROWS - 1)) + jnp.where(row < LROWS, phase, other)


def pick_matrix(phase):
    row = lax.broadcasted_iota(jnp.int32, (ROWS, TOK), 0)
    tok = lax.broadcasted_iota(jnp.int32, (ROWS, TOK), 1)
    return (tok == token_of(row, phase)).astype(jnp.float32).astype(jnp.bfloat16)


def spread_matrix(phase):
    row = lax.broadcasted_iota(jnp.int32, (TOK, ROWS), 1)
    tok = lax.broadcasted_iota(jnp.int32, (TOK, ROWS), 0)
    return (tok == token_of(row, phase)).astype(jnp.float32).astype(jnp.bfloat16)


def place():
    me = lax.axis_index("seq")
    return me, me // RING, lax.rem(me, RING)


def greet(line, pos, columns, gather):
    barrier = pltpu.get_barrier_semaphore()
    for o in range(1, RING):
        pl.semaphore_signal(
            barrier, inc=1, device_id={"seq": line * RING + lax.rem(pos + o, RING)}
        )
    for o in columns:
        pl.semaphore_signal(
            barrier, inc=1, device_id={"seq": lax.rem(line + o, ROW_LINES) * RING + pos}
        )
    total = RING - 1 + len(columns)
    if gather:
        f = lax.axis_index("fsdp")
        x, hi = f // 2, lax.rem(f, 2)
        pl.semaphore_signal(barrier, inc=1, device_id={"fsdp": 2 * x + 1 - hi})
        for o in range(1, XS):
            pl.semaphore_signal(barrier, inc=1, device_id={"fsdp": 2 * lax.rem(x + o, XS) + hi})
        total += XS
    pl.semaphore_wait(barrier, total)


def send_all(
    phase_ref,
    q_ref,
    k_ref,
    v_ref,
    g_ref,
    w_ref,
    qo_ref,
    kvo_ref,
    do_ref,
    stage,
    gstage,
    w_all,
    send_sem,
    recv_sem,
    hsend,
    hrecv,
    gsend,
    grecv,
    zsend,
    zrecv,
    ysend,
    yrecv,
    xsend,
    xrecv,
    csend,
    crecv,
):
    me, line, pos = place()
    core = lax.rem(me, 2)
    f = lax.axis_index("fsdp")
    x, hi = f // 2, lax.rem(f, 2)
    mate = 2 * x + 1 - hi
    greet(line, pos, (1, 2, 3), True)
    half = pl.ds(pl.multiple_of(core * 64, 64), 64)
    piece = pl.ds(pl.multiple_of(core * 64 + line * 16, 16), 16)

    to_mate = pltpu.make_async_remote_copy(
        src_ref=w_ref.at[piece],
        dst_ref=w_all.at[f, piece],
        send_sem=zsend,
        recv_sem=zrecv,
        device_id={"fsdp": mate},
    )

    def along_y(o):
        return pltpu.make_async_remote_copy(
            src_ref=w_all.at[mate, piece],
            dst_ref=w_all.at[mate, piece],
            send_sem=ysend.at[o],
            recv_sem=yrecv.at[o],
            device_id={"seq": lax.rem(line + o, ROW_LINES) * RING + pos},
        )

    def along_x(j, own):
        m = jnp.maximum(j - 2, 0)
        src = w_ref.at[half] if own else w_all.at[mate, half]
        return pltpu.make_async_remote_copy(
            src_ref=src,
            dst_ref=w_all.at[f if own else mate, half],
            send_sem=xsend.at[j],
            recv_sem=xrecv.at[j],
            device_id={"fsdp": 2 * lax.rem(x + lax.rem(m, 3) + 1, XS) + hi},
        )

    def slot(j):
        m = jnp.maximum(j - 2, 0)
        other = 2 * lax.rem(x + XS - 1 - lax.rem(m, 3), XS) + jnp.where(m < 3, hi, 1 - hi)
        return jnp.where(j == 0, f, jnp.where(j == 1, mate, other))

    def to_core(j):
        return pltpu.make_async_remote_copy(
            src_ref=w_all.at[slot(j), half],
            dst_ref=w_all.at[slot(j), half],
            send_sem=csend.at[j],
            recv_sem=crecv.at[j],
            device_id={"seq": me + 1 - 2 * core},
        )

    to_mate.start()
    for j in range(2, 5):
        along_x(j, True).start()

    def packed(h):
        pick = pick_matrix(phase_ref[h])
        cols = pl.ds(pl.multiple_of(h * HS, HS), HS)
        return [dot(pick, ref[:, cols], NN).astype(jnp.bfloat16) for ref in (q_ref, k_ref, v_ref)]

    def to_peer(o, what):
        peer = line * RING + lax.rem(pos + o, RING)
        if what == 0:
            src, dst = stage.at[o, 0], qo_ref.at[pos]
        else:
            src, dst = stage.at[o, pl.ds(1, 2)], kvo_ref.at[RING + pos]
        return pltpu.make_async_remote_copy(
            src_ref=src,
            dst_ref=dst,
            send_sem=send_sem.at[what, o],
            recv_sem=recv_sem.at[what, o],
            device_id={"seq": peer},
        )

    def far(s):
        return pltpu.make_async_remote_copy(
            src_ref=kvo_ref.at[RING + s],
            dst_ref=kvo_ref.at[s],
            send_sem=hsend.at[s],
            recv_sem=hrecv.at[s],
            device_id={"seq": me + RING},
        )

    def far_long(s):
        return pltpu.make_async_remote_copy(
            src_ref=kvo_ref.at[RING + s, :, pl.ds(0, LROWS)],
            dst_ref=kvo_ref.at[s, :, pl.ds(0, LROWS)],
            send_sem=hsend.at[s],
            recv_sem=hrecv.at[s],
            device_id={"seq": me + RING},
        )

    def start(o, _):
        for i, rows in enumerate(packed(lax.rem(pos + o, RING))):
            stage[o, i] = rows
        to_peer(o, 1).start()
        to_peer(o, 0).start()
        return 0

    lax.fori_loop(1, RING, start, 0)

    to_mate.wait_recv()
    for o in range(1, ROW_LINES):
        along_y(o).start()
    own = packed(pos)
    qo_ref[pos] = own[0]
    kvo_ref[RING + pos, 0] = own[1]
    kvo_ref[RING + pos, 1] = own[2]
    w_all[f] = w_ref[...]
    for o in range(1, ROW_LINES):
        along_y(o).wait_recv()
    for j in range(5, 8):
        along_x(j, False).start()
    to_core(1).start()

    def to_head(j, h):
        return pltpu.make_async_remote_copy(
            src_ref=gstage.at[j],
            dst_ref=do_ref.at[pos],
            send_sem=gsend.at[j],
            recv_sem=grecv.at[pos],
            device_id={"seq": line * RING + h},
        )

    def grad_head(j, _):
        h = slot(j)

        @pl.when((j >= 1) & (j < RING - 1))
        def _():
            along_x(j + 1, True).wait_recv()
            to_core(j + 1).start()

        @pl.when(j >= 1)
        def _():
            to_core(j).wait_recv()

        full = dot(g_ref[...], w_all[h], NT).astype(jnp.bfloat16)
        rows = dot(pick_matrix(phase_ref[h]), full, NN).astype(jnp.bfloat16)

        @pl.when(h == pos)
        def _():
            do_ref[pos] = rows

        @pl.when(h != pos)
        def _():
            gstage[j] = rows
            to_head(j, h).start()

        return 0

    lax.fori_loop(0, RING, grad_head, 0)

    def forward(o, _):
        s = lax.rem(pos + RING - o, RING)

        @pl.when(o > 0)
        def _():
            to_peer(o, 1).wait_recv()

        @pl.when((line < ROW_LINES - 1) & (s >= RING // 2))
        def _():
            far(s).start()

        @pl.when((lax.rem(line, 2) == 0) & (s < RING // 2))
        def _():
            far_long(s).start()

        return 0

    lax.fori_loop(0, RING, forward, 0)

    def finish(o, _):
        to_peer(o, 0).wait_recv()
        to_peer(o, 0).wait_send()
        to_peer(o, 1).wait_send()
        return 0

    lax.fori_loop(1, RING, finish, 0)

    def finish_grad(j, _):
        h = slot(j)

        @pl.when(h != pos)
        def _():
            to_head(j, h).wait_send()

        @pl.when(j != pos)
        def _():
            pltpu.make_async_remote_copy(
                src_ref=gstage.at[j],
                dst_ref=do_ref.at[j],
                send_sem=gsend.at[j],
                recv_sem=grecv.at[j],
                device_id={"seq": line * RING + lax.rem(pos + 1, RING)},
            ).wait_recv()

        return 0

    lax.fori_loop(0, RING, finish_grad, 0)

    def finish_far(s, _):
        @pl.when((line < ROW_LINES - 1) & (s >= RING // 2))
        def _():
            far(s).wait_send()

        @pl.when((lax.rem(line, 2) == 0) & (s < RING // 2))
        def _():
            far_long(s).wait_send()

        @pl.when((line > 0) & (s >= RING // 2))
        def _():
            far(s).wait_recv()

        @pl.when((lax.rem(line, 2) == 1) & (s < RING // 2))
        def _():
            far_long(s).wait_recv()

        return 0

    lax.fori_loop(0, RING, finish_far, 0)
    to_mate.wait_send()
    for o in range(1, ROW_LINES):
        along_y(o).wait_send()
    for j in range(2, 8):
        along_x(j, True).wait_send()
    for j in range(1, 8):
        to_core(j).wait_send()


def attend_back(
    phase_ref,
    short_ref,
    long_ref,
    q_ref,
    kv_ref,
    do_ref,
    gq_ref,
    gk_ref,
    gv_ref,
    kt_ref,
    lkv_ref,
    lkt_ref,
    lq_ref,
    off_ref,
    rows_ref,
    p_ref,
    dp_ref,
    st_ref,
    delta_ref,
    acc,
    dq_acc,
    far_stage,
    near,
    dq_stage,
    stage,
    got_q,
    got_kv,
    send_sem,
    recv_sem,
    hsend,
    hrecv,
):
    me, line, pos = place()
    odd = lax.rem(line, 2)
    greet(line, pos, (1, 3), False)
    phase = phase_ref[pos]
    origin = (line - 1) * (RING * TOK)

    def far(s):
        return pltpu.make_async_remote_copy(
            src_ref=far_stage.at[s],
            dst_ref=near.at[s],
            send_sem=hsend.at[s],
            recv_sem=hrecv.at[s],
            device_id={"seq": me - RING},
        )

    def far_long(s):
        return pltpu.make_async_remote_copy(
            src_ref=far_stage.at[s, :, pl.ds(0, LROWS)],
            dst_ref=near.at[s, :, pl.ds(0, LROWS)],
            send_sem=hsend.at[s],
            recv_sem=hrecv.at[s],
            device_id={"seq": me - RING},
        )

    def home(s, what):
        if what == 0:
            src, dst = dq_stage.at[s], got_q.at[pos]
        else:
            src, dst = stage.at[s], got_kv.at[pos]
        return pltpu.make_async_remote_copy(
            src_ref=src,
            dst_ref=dst,
            send_sem=send_sem.at[what, s],
            recv_sem=recv_sem.at[what, pos],
            device_id={"seq": line * RING + s},
        )

    def landed(s, what):
        dst = got_q.at[s] if what == 0 else got_kv.at[s]
        src = dq_stage.at[s] if what == 0 else stage.at[s]
        return pltpu.make_async_remote_copy(
            src_ref=src,
            dst_ref=dst,
            send_sem=send_sem.at[what, s],
            recv_sem=recv_sem.at[what, s],
            device_id={"seq": line * RING + lax.rem(pos + 1, RING)},
        )

    row = lax.broadcasted_iota(jnp.int32, (ROWS, LROWS), 0)
    off_ref[0] = token_of(row, phase)
    off_ref[1] = (row // LROWS) * TOK + 4 * (row & (LROWS - 1)) + phase

    def low_of(tok, lengths, count):
        low = jnp.full_like(tok, -origin)
        end = -origin
        for n in range(count):
            end = end + lengths[n]
            low = jnp.where(tok >= end, jnp.maximum(low, end), low)
        return low

    lane = lax.broadcasted_iota(jnp.int32, (1, ROWS), 1)
    query_off = token_of(lane, phase)
    pair_off = (lane // LROWS) * TOK + 4 * (lane & (LROWS - 1)) + phase

    def prepare_query(i, _):
        tok = (RING + i) * TOK + query_off
        rows_ref[i, pl.ds(0, 1), :] = tok
        rows_ref[i, pl.ds(1, 1), :] = low_of(tok, short_ref, 15)
        return 0

    lax.fori_loop(0, RING, prepare_query, 0)

    def prepare_pair(ii, _):
        tok = (RING + 2 * ii) * TOK + pair_off
        rows_ref[RING + ii, pl.ds(0, 1), :] = tok
        rows_ref[RING + ii, pl.ds(1, 1), :] = low_of(tok, long_ref, 3)
        for e in range(2):
            lq_ref[ii, 0, pl.ds(e * LROWS, LROWS), :] = q_ref[2 * ii + e, pl.ds(0, LROWS), :]
            lq_ref[ii, 1, pl.ds(e * LROWS, LROWS), :] = do_ref[2 * ii + e, pl.ds(0, LROWS), :]
        return 0

    lax.fori_loop(0, PAIRS, prepare_pair, 0)

    first_block = jnp.where(line > 0, RING // 2, RING)
    first_pair = jnp.where(odd == 1, 0, PAIRS)

    def prepare_key(g, _):
        kt_ref[g] = kv_ref[g, 0].T
        return 0

    lax.fori_loop(first_block, 2 * RING, prepare_key, 0)

    def prepare_key_pair(kp, _):
        for e in range(2):
            for w in range(2):
                lkv_ref[kp, w, pl.ds(e * LROWS, LROWS), :] = kv_ref[
                    2 * kp + e, w, pl.ds(0, LROWS), :
                ]
        lkt_ref[kp] = lkv_ref[kp, 0].T
        return 0

    lax.fori_loop(first_pair, 2 * PAIRS, prepare_key_pair, 0)

    st_ref[:, pl.ds(0, 1), :] = jnp.full((TILES, 1, ROWS), NEG, jnp.float32)
    st_ref[:, pl.ds(1, 3), :] = jnp.zeros((TILES, 3, ROWS), jnp.float32)
    acc[...] = jnp.zeros_like(acc)
    dq_acc[...] = jnp.zeros_like(dq_acc)

    def tile(t, k, v, q, do, kind, tok, low):
        off = off_ref[kind]
        off = jnp.concatenate([off, off], axis=1)
        s = dot(k, q, NT)
        s = jnp.where((off >= low) & (off <= tok), s, NEG)
        m = jnp.max(s, axis=0, keepdims=True)
        p = jnp.exp((s - m) * SCALE)
        dp = dot(v, do, NT)
        p_ref[t] = p
        dp_ref[t] = dp
        st_ref[t, pl.ds(0, 1), :] = m
        st_ref[t, pl.ds(1, 1), :] = jnp.sum(p, axis=0, keepdims=True)
        st_ref[t, pl.ds(2, 1), :] = jnp.sum(p * dp, axis=0, keepdims=True)

    def score_query(i, _):
        tok = rows_ref[i, pl.ds(0, 1), :]
        low = rows_ref[i, pl.ds(1, 1), :]

        def one(g, _):
            tile(
                i * NEAR + RING + i - g,
                kv_ref[g, 0],
                kv_ref[g, 1],
                q_ref[i],
                do_ref[i],
                0,
                tok - g * TOK,
                low - g * TOK,
            )
            return 0

        lax.fori_loop(jnp.maximum(RING + i - (NEAR - 1), first_block), RING + i + 1, one, 0)
        return 0

    lax.fori_loop(0, RING, score_query, 0)

    def score_pair(ii, _):
        tok = rows_ref[RING + ii, pl.ds(0, 1), :]
        low = rows_ref[RING + ii, pl.ds(1, 1), :]

        def one(kp, _):
            tile(
                SHORT_TILES + ii * 2 * PAIRS + kp,
                lkv_ref[kp, 0],
                lkv_ref[kp, 1],
                lq_ref[ii, 0],
                lq_ref[ii, 1],
                1,
                tok - kp * (2 * TOK),
                low - kp * (2 * TOK),
            )
            return 0

        lax.fori_loop(first_pair, PAIRS + ii + 1, one, 0)
        return 0

    lax.fori_loop(0, PAIRS, score_pair, 0)

    def join(ii, _):
        base = SHORT_TILES + ii * 2 * PAIRS
        lst = [st_ref[base + c] for c in range(2 * PAIRS)]
        tops, invs, deltas = [], [], []
        for e in range(2):
            i = 2 * ii + e
            sst = [st_ref[i * NEAR + c] for c in range(NEAR)]
            here = slice(e * LROWS, (e + 1) * LROWS)
            m = functools.reduce(jnp.maximum, [a[0:1] for a in sst])
            ml = functools.reduce(jnp.maximum, [a[0:1, here] for a in lst], m[:, :LROWS])
            m = jnp.concatenate([ml, m[:, LROWS:]], axis=1)
            w = [jnp.exp((a[0:1] - m) * SCALE) for a in sst]
            wl = [jnp.exp((a[0:1, here] - ml) * SCALE) for a in lst]
            l = sum(x * a[1:2] for x, a in zip(w, sst))
            d = sum(x * a[2:3] for x, a in zip(w, sst))
            ll = sum((x * a[1:2, here] for x, a in zip(wl, lst)), l[:, :LROWS])
            dl = sum((x * a[2:3, here] for x, a in zip(wl, lst)), d[:, :LROWS])
            l = jnp.concatenate([ll, l[:, LROWS:]], axis=1)
            d = jnp.concatenate([dl, d[:, LROWS:]], axis=1)
            inv = 1.0 / l
            delta_ref[i, pl.ds(0, 1), :] = d * inv
            for c in range(NEAR):
                st_ref[i * NEAR + c, pl.ds(3, 1), :] = w[c] * inv
            tops.append(ml)
            invs.append(inv[:, :LROWS])
            deltas.append((d * inv)[:, :LROWS])
        ml = jnp.concatenate(tops, axis=1)
        il = jnp.concatenate(invs, axis=1)
        delta_ref[RING + ii, pl.ds(0, 1), :] = jnp.concatenate(deltas, axis=1)
        for c in range(2 * PAIRS):
            st_ref[base + c, pl.ds(3, 1), :] = jnp.exp((lst[c][0:1] - ml) * SCALE) * il
        return 0

    lax.fori_loop(0, PAIRS, join, 0)

    def back(t, q, do, kt, delta):
        pr = p_ref[t] * st_ref[t, pl.ds(3, 1), :]
        ds = (pr * (dp_ref[t] - delta)).astype(jnp.bfloat16)
        return dot(ds, q, NN), dot(pr.astype(jnp.bfloat16), do, NN), dot(kt, ds, NN)

    def back_pair(kp, first):
        def one(ii, _):
            dk, dv, dq = back(
                SHORT_TILES + ii * 2 * PAIRS + kp,
                lq_ref[ii, 0],
                lq_ref[ii, 1],
                lkt_ref[kp],
                delta_ref[RING + ii, pl.ds(0, 1), :],
            )
            for e in range(2):
                part = slice(e * LROWS, (e + 1) * LROWS)
                acc[2 * kp + e, 0, pl.ds(0, LROWS), :] += dk[part]
                acc[2 * kp + e, 1, pl.ds(0, LROWS), :] += dv[part]
                dq_acc[2 * ii + e, :, pl.ds(0, LROWS)] += dq[:, part]
            return 0

        lax.fori_loop(first, PAIRS, one, 0)

    def back_block(g, first, last):
        def one(i, _):
            dk, dv, dq = back(
                i * NEAR + RING + i - g,
                q_ref[i],
                do_ref[i],
                kt_ref[g],
                delta_ref[i, pl.ds(0, 1), :],
            )
            acc[g, 0] += dk
            acc[g, 1] += dv
            dq_acc[i] += dq
            return 0

        lax.fori_loop(first, last, one, 0)

    def far_pair(kp, _):
        @pl.when(odd == 1)
        def _():
            back_pair(kp, 0)

        for e in range(2):
            g = 2 * kp + e

            @pl.when(kp >= PAIRS // 2)
            def _(g=g):
                back_block(g, 0, g - (RING - NEAR))

            far_stage[g, 0] = (acc[g, 0] * SCALE).astype(jnp.bfloat16)
            far_stage[g, 1] = acc[g, 1].astype(jnp.bfloat16)

            @pl.when(kp >= PAIRS // 2)
            def _(g=g):
                far(g).start()

            @pl.when(kp < PAIRS // 2)
            def _(g=g):
                far_long(g).start()

        return 0

    first_far = jnp.where(odd == 1, 0, jnp.where(line > 0, PAIRS // 2, PAIRS))
    lax.fori_loop(first_far, PAIRS, far_pair, 0)

    def own_pair(kp, _):
        back_pair(PAIRS + kp, kp)
        for e in range(2):
            b = 2 * kp + e
            back_block(RING + b, b, jnp.minimum(b + NEAR, RING))
            dq_stage[b] = (dq_acc[b].T * SCALE).astype(jnp.bfloat16)

            @pl.when(b != pos)
            def _(b=b):
                home(b, 0).start()

        for e in range(2):
            b = 2 * kp + e
            full = (line < ROW_LINES - 1) & (b >= RING // 2)
            half = (odd == 0) & (b < RING // 2)

            @pl.when(full)
            def _(b=b):
                far(b).wait_recv()

            @pl.when(half)
            def _(b=b):
                far_long(b).wait_recv()
                near[b, :, pl.ds(LROWS, LROWS)] = jnp.zeros((2, LROWS, HS), jnp.bfloat16)

            @pl.when(jnp.logical_not(full | half))
            def _(b=b):
                near[b] = jnp.zeros((2, ROWS, HS), jnp.bfloat16)

            stage[b, 0] = (acc[RING + b, 0] * SCALE + near[b, 0].astype(jnp.float32)).astype(
                jnp.bfloat16
            )
            stage[b, 1] = (acc[RING + b, 1] + near[b, 1].astype(jnp.float32)).astype(jnp.bfloat16)

            @pl.when(b != pos)
            def _(b=b):
                home(b, 1).start()

        return 0

    lax.fori_loop(0, PAIRS, own_pair, 0)
    got_q[pos] = dq_stage[pos]
    got_kv[pos] = stage[pos]

    def unpack(o, _):
        h = lax.rem(pos + RING - o, RING)

        @pl.when(o > 0)
        def _():
            landed(h, 0).wait_recv()
            landed(h, 1).wait_recv()

        spread = spread_matrix(phase_ref[h])
        cols = pl.ds(pl.multiple_of(h * HS, HS), HS)
        gq_ref[:, cols] = dot(spread, got_q[h], NN).astype(jnp.bfloat16)
        gk_ref[:, cols] = dot(spread, got_kv[h, 0], NN).astype(jnp.bfloat16)
        gv_ref[:, cols] = dot(spread, got_kv[h, 1], NN).astype(jnp.bfloat16)
        return 0

    lax.fori_loop(0, RING, unpack, 0)

    def finish(o, _):
        s = lax.rem(pos + o, RING)
        home(s, 0).wait_send()
        home(s, 1).wait_send()
        return 0

    lax.fori_loop(1, RING, finish, 0)

    def finish_far(s, _):
        @pl.when((line > 0) & (s >= RING // 2))
        def _():
            far(s).wait_send()

        @pl.when((odd == 1) & (s < RING // 2))
        def _():
            far_long(s).wait_send()

        return 0

    lax.fori_loop(0, RING, finish_far, 0)


VM = pl.BlockSpec(memory_space=pltpu.VMEM)
SM = pl.BlockSpec(memory_space=pltpu.SMEM)
DMA = pltpu.SemaphoreType.DMA
BF = jnp.bfloat16


def shaped(*dims, dtype=BF):
    return jax.ShapeDtypeStruct(dims, dtype)


def shards(q, k, v, grad_mixed, out_weight, head_phase, segments_short, segments_long):
    me = lax.axis_index("seq")
    line, pos = me // RING, lax.rem(me, RING)
    q_rows, kv_rows, do_rows = pl.pallas_call(
        send_all,
        out_shape=(
            shaped(RING, ROWS, HS),
            shaped(2 * RING, 2, ROWS, HS),
            shaped(RING, ROWS, HS),
        ),
        in_specs=[SM, VM, VM, VM, VM, VM],
        out_specs=(VM, VM, VM),
        scratch_shapes=[
            pltpu.VMEM((RING, 3, ROWS, HS), BF),
            pltpu.VMEM((RING, ROWS, HS), BF),
            pltpu.VMEM((HEADS, HS, grad_mixed.shape[2]), BF),
            DMA((2, RING)),
            DMA((2, RING)),
            DMA((RING,)),
            DMA((RING,)),
            DMA((RING,)),
            DMA((RING,)),
            DMA,
            DMA,
            DMA((ROW_LINES,)),
            DMA((ROW_LINES,)),
            DMA((RING,)),
            DMA((RING,)),
            DMA((RING,)),
            DMA((RING,)),
        ],
        compiler_params=pltpu.CompilerParams(
            collective_id=0, has_side_effects=True, vmem_limit_bytes=VMEM_LIMIT
        ),
        name="send_all",
    )(head_phase, q[0], k[0], v[0], grad_mixed[0], out_weight)

    gq, gk, gv = pl.pallas_call(
        attend_back,
        out_shape=(shaped(TOK, HEADS * HS),) * 3,
        in_specs=[SM, SM, SM, VM, VM, VM],
        out_specs=(VM,) * 3,
        scratch_shapes=[
            pltpu.VMEM((2 * RING, HS, ROWS), BF),
            pltpu.VMEM((2 * PAIRS, 2, ROWS, HS), BF),
            pltpu.VMEM((2 * PAIRS, HS, ROWS), BF),
            pltpu.VMEM((PAIRS, 2, ROWS, HS), BF),
            pltpu.VMEM((2, ROWS, LROWS), jnp.int32),
            pltpu.VMEM((RING + PAIRS, 8, ROWS), jnp.int32),
            pltpu.VMEM((TILES, ROWS, ROWS), jnp.float32),
            pltpu.VMEM((TILES, ROWS, ROWS), jnp.float32),
            pltpu.VMEM((TILES, 8, ROWS), jnp.float32),
            pltpu.VMEM((RING + PAIRS, 8, ROWS), jnp.float32),
            pltpu.VMEM((2 * RING, 2, ROWS, HS), jnp.float32),
            pltpu.VMEM((RING, HS, ROWS), jnp.float32),
            pltpu.VMEM((RING, 2, ROWS, HS), BF),
            pltpu.VMEM((RING, 2, ROWS, HS), BF),
            pltpu.VMEM((RING, ROWS, HS), BF),
            pltpu.VMEM((RING, 2, ROWS, HS), BF),
            pltpu.VMEM((RING, ROWS, HS), BF),
            pltpu.VMEM((RING, 2, ROWS, HS), BF),
            DMA((2, RING)),
            DMA((2, RING)),
            DMA((RING,)),
            DMA((RING,)),
        ],
        compiler_params=pltpu.CompilerParams(
            collective_id=1, has_side_effects=True, vmem_limit_bytes=VMEM_LIMIT
        ),
        name="attend_back",
    )(head_phase, segments_short, segments_long, q_rows, kv_rows, do_rows)
    return gq[None], gk[None], gv[None]


def solution(mesh):
    placed = (
        P("fsdp", "seq", None),
        P("fsdp", "seq", None),
        P("fsdp", "seq", None),
        P("fsdp", "seq", None),
        P("fsdp", None),
        P(),
        P(),
        P(),
    )
    return jax.shard_map(
        shards,
        mesh=mesh,
        in_specs=placed,
        out_specs=(P("fsdp", "seq", None), P("fsdp", "seq", None), P("fsdp", "seq", None)),
        check_vma=False,
    )
```

```python
import functools
import math

import jax
import jax.numpy as jnp
from jax import lax
from jax.experimental import pallas as pl
from jax.experimental.pallas import tpu as pltpu
from jax.sharding import PartitionSpec as P

HEADS = 8
HS = 128
TOK = 512
ROWS = 256
LROWS = 128
RING = 8
ROW_LINES = 4
XS = 4
PAIRS = 4
NEAR = 5
STATS = RING + PAIRS * PAIRS
NEG = -1e30
SCALE = 1.0 / math.sqrt(HS)
EXP_SCALE = SCALE * math.log2(math.e)
NT = (((1,), (1,)), ((), ()))
NN = (((1,), (0,)), ((), ()))
TN = (((0,), (0,)), ((), ()))
VMEM_LIMIT = 60 * 1024 * 1024


def dot(a, b, dims):
    return lax.dot_general(a, b, dims, preferred_element_type=jnp.float32)


def token_of(row, phase):
    other = jnp.where(phase < 2, phase + 2, phase - 2)
    return 4 * (row & (LROWS - 1)) + jnp.where(row < LROWS, phase, other)


def pick_matrix(phase):
    row = lax.broadcasted_iota(jnp.int32, (ROWS, TOK), 0)
    tok = lax.broadcasted_iota(jnp.int32, (ROWS, TOK), 1)
    return (tok == token_of(row, phase)).astype(jnp.float32).astype(jnp.bfloat16)


def spread_matrix(phase):
    row = lax.broadcasted_iota(jnp.int32, (TOK, ROWS), 1)
    tok = lax.broadcasted_iota(jnp.int32, (TOK, ROWS), 0)
    return (tok == token_of(row, phase)).astype(jnp.float32).astype(jnp.bfloat16)


def place():
    me = lax.axis_index("seq")
    return me, me // RING, lax.rem(me, RING)


def greet(line, pos, columns, gather):
    barrier = pltpu.get_barrier_semaphore()
    for o in range(1, RING):
        pl.semaphore_signal(
            barrier, inc=1, device_id={"seq": line * RING + lax.rem(pos + o, RING)}
        )
    for o in columns:
        pl.semaphore_signal(
            barrier, inc=1, device_id={"seq": lax.rem(line + o, ROW_LINES) * RING + pos}
        )
    total = RING - 1 + len(columns)
    if gather:
        f = lax.axis_index("fsdp")
        x, hi = f // 2, lax.rem(f, 2)
        pl.semaphore_signal(barrier, inc=1, device_id={"fsdp": 2 * x + 1 - hi})
        for o in range(1, XS):
            pl.semaphore_signal(barrier, inc=1, device_id={"fsdp": 2 * lax.rem(x + o, XS) + hi})
        total += XS
    pl.semaphore_wait(barrier, total)


def layer(
    phase_ref,
    short_ref,
    long_ref,
    q_ref,
    k_ref,
    v_ref,
    g_ref,
    w_ref,
    gq_ref,
    gk_ref,
    gv_ref,
    stage,
    gstage,
    w_all,
    qo_ref,
    kvo_ref,
    do_ref,
    kt_ref,
    lkv_ref,
    lkt_ref,
    lq_ref,
    off_ref,
    rows_ref,
    s_ref,
    p_ref,
    lp_ref,
    o_ref,
    lo_ref,
    st_ref,
    delta_ref,
    acc,
    dq_acc,
    far_stage,
    near,
    dq_stage,
    kv_stage,
    got_q,
    got_kv,
    send_sem,
    recv_sem,
    hsend,
    hrecv,
    gsend,
    grecv,
    zsend,
    zrecv,
    ysend,
    yrecv,
    xsend,
    xrecv,
    csend,
    crecv,
    bsend,
    brecv,
    fsend,
    frecv,
):
    me, line, pos = place()
    core = lax.rem(me, 2)
    f = lax.axis_index("fsdp")
    x, hi = f // 2, lax.rem(f, 2)
    mate = 2 * x + 1 - hi
    greet(line, pos, (1, 2, 3), True)
    half = pl.ds(pl.multiple_of(core * 64, 64), 64)
    piece = pl.ds(pl.multiple_of(core * 64 + line * 16, 16), 16)

    to_mate = pltpu.make_async_remote_copy(
        src_ref=w_ref.at[piece],
        dst_ref=w_all.at[f, piece],
        send_sem=zsend,
        recv_sem=zrecv,
        device_id={"fsdp": mate},
    )

    def along_y(o):
        return pltpu.make_async_remote_copy(
            src_ref=w_all.at[mate, piece],
            dst_ref=w_all.at[mate, piece],
            send_sem=ysend.at[o],
            recv_sem=yrecv.at[o],
            device_id={"seq": lax.rem(line + o, ROW_LINES) * RING + pos},
        )

    def along_x(j, own):
        m = jnp.maximum(j - 2, 0)
        src = w_ref.at[half] if own else w_all.at[mate, half]
        return pltpu.make_async_remote_copy(
            src_ref=src,
            dst_ref=w_all.at[f if own else mate, half],
            send_sem=xsend.at[j],
            recv_sem=xrecv.at[j],
            device_id={"fsdp": 2 * lax.rem(x + lax.rem(m, 3) + 1, XS) + hi},
        )

    def slot(j):
        m = jnp.maximum(j - 2, 0)
        other = 2 * lax.rem(x + XS - 1 - lax.rem(m, 3), XS) + jnp.where(m < 3, hi, 1 - hi)
        return jnp.where(j == 0, f, jnp.where(j == 1, mate, other))

    def to_core(j):
        return pltpu.make_async_remote_copy(
            src_ref=w_all.at[slot(j), half],
            dst_ref=w_all.at[slot(j), half],
            send_sem=csend.at[j],
            recv_sem=crecv.at[j],
            device_id={"seq": me + 1 - 2 * core},
        )

    to_mate.start()
    for j in range(2, 5):
        along_x(j, True).start()

    def packed(h):
        pick = pick_matrix(phase_ref[h])
        cols = pl.ds(pl.multiple_of(h * HS, HS), HS)
        return [dot(pick, ref[:, cols], NN).astype(jnp.bfloat16) for ref in (q_ref, k_ref, v_ref)]

    def to_peer(o, what):
        peer = line * RING + lax.rem(pos + o, RING)
        if what == 0:
            src, dst = stage.at[o, 0], qo_ref.at[pos]
        else:
            src, dst = stage.at[o, pl.ds(1, 2)], kvo_ref.at[RING + pos]
        return pltpu.make_async_remote_copy(
            src_ref=src,
            dst_ref=dst,
            send_sem=send_sem.at[what, o],
            recv_sem=recv_sem.at[what, o],
            device_id={"seq": peer},
        )

    def far(s):
        return pltpu.make_async_remote_copy(
            src_ref=kvo_ref.at[RING + s],
            dst_ref=kvo_ref.at[s],
            send_sem=hsend.at[s],
            recv_sem=hrecv.at[s],
            device_id={"seq": me + RING},
        )

    def far_long(s):
        return pltpu.make_async_remote_copy(
            src_ref=kvo_ref.at[RING + s, :, pl.ds(0, LROWS)],
            dst_ref=kvo_ref.at[s, :, pl.ds(0, LROWS)],
            send_sem=hsend.at[s],
            recv_sem=hrecv.at[s],
            device_id={"seq": me + RING},
        )

    def start(o, _):
        for i, rows in enumerate(packed(lax.rem(pos + o, RING))):
            stage[o, i] = rows
        to_peer(o, 1).start()
        to_peer(o, 0).start()
        return 0

    lax.fori_loop(1, RING, start, 0)

    to_mate.wait_recv()
    for o in range(1, ROW_LINES):
        along_y(o).start()
    own = packed(pos)
    qo_ref[pos] = own[0]
    kvo_ref[RING + pos, 0] = own[1]
    kvo_ref[RING + pos, 1] = own[2]
    w_all[f] = w_ref[...]
    for o in range(1, ROW_LINES):
        along_y(o).wait_recv()
    for j in range(5, 8):
        along_x(j, False).start()
    to_core(1).start()

    def to_head(j, h):
        return pltpu.make_async_remote_copy(
            src_ref=gstage.at[j],
            dst_ref=do_ref.at[pos],
            send_sem=gsend.at[j],
            recv_sem=grecv.at[pos],
            device_id={"seq": line * RING + h},
        )

    def grad_head(j, _):
        h = slot(j)

        @pl.when((j >= 1) & (j < RING - 1))
        def _():
            along_x(j + 1, True).wait_recv()
            to_core(j + 1).start()

        @pl.when(j >= 1)
        def _():
            to_core(j).wait_recv()

        full = dot(g_ref[...], w_all[h], NT).astype(jnp.bfloat16)
        rows = dot(pick_matrix(phase_ref[h]), full, NN).astype(jnp.bfloat16)

        @pl.when(h == pos)
        def _():
            do_ref[pos] = rows

        @pl.when(h != pos)
        def _():
            gstage[j] = rows
            to_head(j, h).start()

        return 0

    lax.fori_loop(0, RING, grad_head, 0)

    def forward(o, _):
        s = lax.rem(pos + RING - o, RING)

        @pl.when(o > 0)
        def _():
            to_peer(o, 1).wait_recv()

        @pl.when((line < ROW_LINES - 1) & (s >= RING // 2))
        def _():
            far(s).start()

        @pl.when((lax.rem(line, 2) == 0) & (s < RING // 2))
        def _():
            far_long(s).start()

        return 0

    lax.fori_loop(0, RING, forward, 0)


    phase = phase_ref[pos]
    odd = lax.rem(line, 2)
    origin = (line - 1) * (RING * TOK)
    row = lax.broadcasted_iota(jnp.int32, (ROWS, LROWS), 0)
    off_ref[0] = token_of(row, phase)
    off_ref[1] = (row // LROWS) * TOK + 4 * (row & (LROWS - 1)) + phase

    def low_of(tok, lengths, count):
        low = jnp.full_like(tok, -origin)
        end = -origin
        for n in range(count):
            end = end + lengths[n]
            low = jnp.where(tok >= end, jnp.maximum(low, end), low)
        return low

    lane = lax.broadcasted_iota(jnp.int32, (1, ROWS), 1)
    query_off = token_of(lane, phase)
    pair_off = (lane // LROWS) * TOK + 4 * (lane & (LROWS - 1)) + phase

    def prepare_query(i, _):
        tok = (RING + i) * TOK + query_off
        rows_ref[i, pl.ds(0, 1), :] = tok
        rows_ref[i, pl.ds(1, 1), :] = low_of(tok, short_ref, short_ref.shape[0])
        return 0

    lax.fori_loop(0, RING, prepare_query, 0)

    def prepare_pair(ii, _):
        tok = (RING + 2 * ii) * TOK + pair_off
        rows_ref[RING + ii, pl.ds(0, 1), :] = tok
        rows_ref[RING + ii, pl.ds(1, 1), :] = low_of(tok, long_ref, long_ref.shape[0])
        return 0

    lax.fori_loop(0, PAIRS, prepare_pair, 0)

    st_ref[:, pl.ds(0, 1), :] = jnp.full((STATS, 1, ROWS), NEG, jnp.float32)
    st_ref[:, pl.ds(1, 3), :] = jnp.zeros((STATS, 3, ROWS), jnp.float32)
    acc[...] = jnp.zeros_like(acc)
    dq_acc[...] = jnp.zeros_like(dq_acc)
    lo_ref[...] = jnp.zeros_like(lo_ref)

    @pl.when(line == 0)
    def _():
        kvo_ref[pl.ds(0, RING)] = jnp.zeros((RING, 2, ROWS, HS), jnp.bfloat16)

    def got_query(o, _):
        to_peer(o, 0).wait_recv()
        return 0

    lax.fori_loop(1, RING, got_query, 0)

    def prepare_key(g, _):
        kt_ref[g, 0] = kvo_ref[g, 0].T
        kt_ref[g, 1] = kvo_ref[g, 1].T
        return 0

    def prepare_key_pair(kp, _):
        for e in range(2):
            for w in range(2):
                lkv_ref[kp, w, pl.ds(e * LROWS, LROWS), :] = kvo_ref[
                    2 * kp + e, w, pl.ds(0, LROWS), :
                ]
        cols = pl.ds(pl.multiple_of(lax.rem(kp, 2) * ROWS, ROWS), ROWS)
        lkt_ref[kp // 2, 0, :, cols] = lkv_ref[kp, 0].T
        lkt_ref[kp // 2, 1, :, cols] = lkv_ref[kp, 1].T
        return 0

    def prepare_long_query(ii, _):
        for e in range(2):
            lq_ref[ii, 0, pl.ds(e * LROWS, LROWS), :] = qo_ref[2 * ii + e, pl.ds(0, LROWS), :]
        return 0

    lax.fori_loop(0, PAIRS, prepare_long_query, 0)
    lax.fori_loop(RING, 2 * RING, prepare_key, 0)
    lax.fori_loop(PAIRS, 2 * PAIRS, prepare_key_pair, 0)

    def strip(i, _):
        tok = rows_ref[i, pl.ds(0, 1), :]
        low = rows_ref[i, pl.ds(1, 1), :]
        q = qo_ref[i]
        off = jnp.concatenate([off_ref[0], off_ref[0]], axis=1)
        tops = []
        for d in range(NEAR):
            g = RING + i - d
            s = dot(kvo_ref[g, 0], q, NT)
            live = off >= low - g * TOK
            if d == 0:
                live = live & (off <= tok - g * TOK)
            s = jnp.where(live, s, NEG)
            s_ref[d] = s
            tops.append(jnp.max(s, axis=0, keepdims=True))
        m = functools.reduce(jnp.maximum, tops)
        l, o = jnp.zeros((1, ROWS), jnp.float32), jnp.zeros((HS, ROWS), jnp.float32)
        for d in range(NEAR):
            p = jnp.exp2((s_ref[d] - m) * EXP_SCALE)
            l = l + jnp.sum(p, axis=0, keepdims=True)
            w = p.astype(jnp.bfloat16)
            p_ref[i, d] = w
            o = o + dot(kt_ref[RING + i - d, 1], w, NN)
        st_ref[i, pl.ds(0, 1), :] = m
        st_ref[i, pl.ds(1, 1), :] = l
        o_ref[i] = o
        return 0

    def chunk(ii, c):
        tok = rows_ref[RING + ii, pl.ds(0, 1), :]
        low = rows_ref[RING + ii, pl.ds(1, 1), :]
        q = lq_ref[ii, 0]
        off = jnp.concatenate([off_ref[1], off_ref[1]], axis=1)
        scores = []
        for e in range(2):
            kp = 2 * c + e
            s = dot(lkv_ref[kp, 0], q, NT)
            at = kp * (2 * TOK)
            scores.append(jnp.where((off >= low - at) & (off <= tok - at), s, NEG))
        m = jnp.maximum(*[jnp.max(s, axis=0, keepdims=True) for s in scores])
        l = jnp.zeros((1, ROWS), jnp.float32)
        parts = []
        for e in range(2):
            p = jnp.exp2((scores[e] - m) * EXP_SCALE)
            l = l + jnp.sum(p, axis=0, keepdims=True)
            w = p.astype(jnp.bfloat16)
            lp_ref[ii, 2 * c + e] = w
            parts.append(w)
        t = RING + ii * PAIRS + c
        st_ref[t, pl.ds(0, 1), :] = m
        st_ref[t, pl.ds(1, 1), :] = l
        lo_ref[ii, c] = dot(lkt_ref[c, 1], jnp.concatenate(parts, axis=0), NN)

    def own_chunks(ii, _):
        chunk(ii, 2)

        @pl.when(ii >= 2)
        def _():
            chunk(ii, 3)

        return 0

    lax.fori_loop(0, PAIRS, own_chunks, 0)
    lax.fori_loop(RING // 2, RING, strip, 0)

    def got_far(s, _):
        @pl.when((line > 0) & (s >= RING // 2))
        def _():
            far(s).wait_recv()

        @pl.when((odd == 1) & (s < RING // 2))
        def _():
            far_long(s).wait_recv()

        return 0

    lax.fori_loop(0, RING, got_far, 0)
    lax.fori_loop(RING // 2, RING, prepare_key, 0)
    lax.fori_loop(0, RING // 2, strip, 0)

    @pl.when(odd == 1)
    def _():
        lax.fori_loop(0, PAIRS, prepare_key_pair, 0)

        def far_chunks(n, _):
            chunk(n // 2, lax.rem(n, 2))
            return 0

        lax.fori_loop(0, 2 * PAIRS, far_chunks, 0)

    def got_grad(j, _):
        @pl.when(j != pos)
        def _():
            pltpu.make_async_remote_copy(
                src_ref=gstage.at[j],
                dst_ref=do_ref.at[j],
                send_sem=gsend.at[j],
                recv_sem=grecv.at[j],
                device_id={"seq": line * RING + lax.rem(pos + 1, RING)},
            ).wait_recv()

        return 0

    lax.fori_loop(0, RING, got_grad, 0)

    def join(ii, _):
        base = RING + ii * PAIRS
        lst = [st_ref[base + c] for c in range(PAIRS)]
        tops, invs, deltas = [], [], []
        for e in range(2):
            i = 2 * ii + e
            lq_ref[ii, 1, pl.ds(e * LROWS, LROWS), :] = do_ref[i, pl.ds(0, LROWS), :]
            here = slice(e * LROWS, (e + 1) * LROWS)
            m = st_ref[i, pl.ds(0, 1), :]
            ml = functools.reduce(jnp.maximum, [a[0:1, here] for a in lst], m[:, :LROWS])
            w = jnp.exp2((m - jnp.concatenate([ml, m[:, LROWS:]], axis=1)) * EXP_SCALE)
            wl = [jnp.exp2((a[0:1, here] - ml) * EXP_SCALE) for a in lst]
            l = w * st_ref[i, pl.ds(1, 1), :]
            ll = sum((x * a[1:2, here] for x, a in zip(wl, lst)), l[:, :LROWS])
            inv = 1.0 / jnp.concatenate([ll, l[:, LROWS:]], axis=1)
            o = o_ref[i] * w
            ol = o[:, :LROWS]
            for c in range(PAIRS):
                ol = ol + lo_ref[ii, c, :, here] * wl[c]
            o = jnp.concatenate([ol, o[:, LROWS:]], axis=1)
            gt = do_ref[i].T.astype(jnp.float32)
            delta = jnp.sum(gt * (o * inv), axis=0, keepdims=True)
            delta_ref[i, pl.ds(0, 1), :] = delta
            st_ref[i, pl.ds(3, 1), :] = w * inv
            tops.append(ml)
            invs.append(inv[:, :LROWS])
            deltas.append(delta[:, :LROWS])
        ml = jnp.concatenate(tops, axis=1)
        il = jnp.concatenate(invs, axis=1)
        delta_ref[RING + ii, pl.ds(0, 1), :] = jnp.concatenate(deltas, axis=1)
        for c in range(PAIRS):
            st_ref[base + c, pl.ds(3, 1), :] = jnp.exp2((lst[c][0:1] - ml) * EXP_SCALE) * il
        return 0

    lax.fori_loop(0, PAIRS, join, 0)

    def back(p, t, v, q, do, kt, delta):
        pr = p.astype(jnp.float32) * st_ref[t, pl.ds(3, 1), :]
        dp = dot(v, do, NT)
        ds = (pr * (dp - delta)).astype(jnp.bfloat16)
        return dot(ds, q, NN), dot(pr.astype(jnp.bfloat16), do, NN), dot(kt, ds, NN)

    def back_pair(kp, first):
        cols = pl.ds(pl.multiple_of(lax.rem(kp, 2) * ROWS, ROWS), ROWS)

        def one(ii, _):
            dk, dv, dq = back(
                lp_ref[ii, kp],
                RING + ii * PAIRS + kp // 2,
                lkv_ref[kp, 1],
                lq_ref[ii, 0],
                lq_ref[ii, 1],
                lkt_ref[kp // 2, 0, :, cols],
                delta_ref[RING + ii, pl.ds(0, 1), :],
            )
            for e in range(2):
                part = slice(e * LROWS, (e + 1) * LROWS)
                acc[2 * kp + e, 0, pl.ds(0, LROWS), :] += dk[part]
                acc[2 * kp + e, 1, pl.ds(0, LROWS), :] += dv[part]
                dq_acc[2 * ii + e, :, pl.ds(0, LROWS)] += dq[:, part]
            return 0

        lax.fori_loop(first, PAIRS, one, 0)

    def back_block(g, first, last):
        def one(i, _):
            dk, dv, dq = back(
                p_ref[i, RING + i - g],
                i,
                kvo_ref[g, 1],
                qo_ref[i],
                do_ref[i],
                kt_ref[g, 0],
                delta_ref[i, pl.ds(0, 1), :],
            )
            acc[g, 0] += dk
            acc[g, 1] += dv
            dq_acc[i] += dq
            return 0

        lax.fori_loop(first, last, one, 0)

    def give(s):
        return pltpu.make_async_remote_copy(
            src_ref=far_stage.at[s],
            dst_ref=near.at[s],
            send_sem=fsend.at[s],
            recv_sem=frecv.at[s],
            device_id={"seq": me - RING},
        )

    def give_long(s):
        return pltpu.make_async_remote_copy(
            src_ref=far_stage.at[s, :, pl.ds(0, LROWS)],
            dst_ref=near.at[s, :, pl.ds(0, LROWS)],
            send_sem=fsend.at[s],
            recv_sem=frecv.at[s],
            device_id={"seq": me - RING},
        )

    def home(s, what):
        if what == 0:
            src, dst = dq_stage.at[s], got_q.at[pos]
        else:
            src, dst = kv_stage.at[s], got_kv.at[pos]
        return pltpu.make_async_remote_copy(
            src_ref=src,
            dst_ref=dst,
            send_sem=bsend.at[what, s],
            recv_sem=brecv.at[what, pos],
            device_id={"seq": line * RING + s},
        )

    def landed(s, what):
        dst = got_q.at[s] if what == 0 else got_kv.at[s]
        src = dq_stage.at[s] if what == 0 else kv_stage.at[s]
        return pltpu.make_async_remote_copy(
            src_ref=src,
            dst_ref=dst,
            send_sem=bsend.at[what, s],
            recv_sem=brecv.at[what, s],
            device_id={"seq": line * RING + lax.rem(pos + 1, RING)},
        )

    def far_pair(kp, _):
        @pl.when(odd == 1)
        def _():
            back_pair(kp, 0)

        for e in range(2):
            g = 2 * kp + e

            @pl.when(kp >= PAIRS // 2)
            def _(g=g):
                back_block(g, 0, g - (RING - NEAR))

            far_stage[g, 0] = (acc[g, 0] * SCALE).astype(jnp.bfloat16)
            far_stage[g, 1] = acc[g, 1].astype(jnp.bfloat16)

            @pl.when(kp >= PAIRS // 2)
            def _(g=g):
                give(g).start()

            @pl.when(kp < PAIRS // 2)
            def _(g=g):
                give_long(g).start()

        return 0

    first_far = jnp.where(odd == 1, 0, jnp.where(line > 0, PAIRS // 2, PAIRS))
    lax.fori_loop(first_far, PAIRS, far_pair, 0)

    def own_pair(kp, _):
        back_pair(PAIRS + kp, kp)
        for e in range(2):
            b = 2 * kp + e
            back_block(RING + b, b, jnp.minimum(b + NEAR, RING))
            dq_stage[b] = (dq_acc[b].T * SCALE).astype(jnp.bfloat16)

            @pl.when(b != pos)
            def _(b=b):
                home(b, 0).start()

        for e in range(2):
            b = 2 * kp + e
            full = (line < ROW_LINES - 1) & (b >= RING // 2)
            half = (odd == 0) & (b < RING // 2)

            @pl.when(full)
            def _(b=b):
                give(b).wait_recv()

            @pl.when(half)
            def _(b=b):
                give_long(b).wait_recv()
                near[b, :, pl.ds(LROWS, LROWS)] = jnp.zeros((2, LROWS, HS), jnp.bfloat16)

            @pl.when(jnp.logical_not(full | half))
            def _(b=b):
                near[b] = jnp.zeros((2, ROWS, HS), jnp.bfloat16)

            kv_stage[b, 0] = (acc[RING + b, 0] * SCALE + near[b, 0].astype(jnp.float32)).astype(
                jnp.bfloat16
            )
            kv_stage[b, 1] = (acc[RING + b, 1] + near[b, 1].astype(jnp.float32)).astype(jnp.bfloat16)

            @pl.when(b != pos)
            def _(b=b):
                home(b, 1).start()

        return 0

    lax.fori_loop(0, PAIRS, own_pair, 0)
    got_q[pos] = dq_stage[pos]
    got_kv[pos] = kv_stage[pos]

    def unpack(o, _):
        h = lax.rem(pos + RING - o, RING)

        @pl.when(o > 0)
        def _():
            landed(h, 0).wait_recv()
            landed(h, 1).wait_recv()

        spread = spread_matrix(phase_ref[h])
        cols = pl.ds(pl.multiple_of(h * HS, HS), HS)
        gq_ref[:, cols] = dot(spread, got_q[h], NN).astype(jnp.bfloat16)
        gk_ref[:, cols] = dot(spread, got_kv[h, 0], NN).astype(jnp.bfloat16)
        gv_ref[:, cols] = dot(spread, got_kv[h, 1], NN).astype(jnp.bfloat16)
        return 0

    lax.fori_loop(0, RING, unpack, 0)

    def finish(o, _):
        s = lax.rem(pos + o, RING)
        home(s, 0).wait_send()
        home(s, 1).wait_send()
        return 0

    lax.fori_loop(1, RING, finish, 0)

    def finish_far(s, _):
        @pl.when((line > 0) & (s >= RING // 2))
        def _():
            give(s).wait_send()

        @pl.when((odd == 1) & (s < RING // 2))
        def _():
            give_long(s).wait_send()

        return 0

    lax.fori_loop(0, RING, finish_far, 0)

    def sent(o, _):
        to_peer(o, 0).wait_send()
        to_peer(o, 1).wait_send()
        return 0

    lax.fori_loop(1, RING, sent, 0)

    def sent_grad(j, _):
        h = slot(j)

        @pl.when(h != pos)
        def _():
            to_head(j, h).wait_send()

        return 0

    lax.fori_loop(0, RING, sent_grad, 0)

    def sent_far(s, _):
        @pl.when((line < ROW_LINES - 1) & (s >= RING // 2))
        def _():
            far(s).wait_send()

        @pl.when((lax.rem(line, 2) == 0) & (s < RING // 2))
        def _():
            far_long(s).wait_send()

        return 0

    lax.fori_loop(0, RING, sent_far, 0)
    to_mate.wait_send()
    for o in range(1, ROW_LINES):
        along_y(o).wait_send()
    for j in range(2, 8):
        along_x(j, True).wait_send()
    for j in range(1, 8):
        to_core(j).wait_send()


VM = pl.BlockSpec(memory_space=pltpu.VMEM)
SM = pl.BlockSpec(memory_space=pltpu.SMEM)
DMA = pltpu.SemaphoreType.DMA
BF = jnp.bfloat16


def shaped(*dims, dtype=BF):
    return jax.ShapeDtypeStruct(dims, dtype)


def shards(q, k, v, grad_mixed, out_weight, head_phase, segments_short, segments_long):
    me = lax.axis_index("seq")
    line, pos = me // RING, lax.rem(me, RING)
    f32, i32 = jnp.float32, jnp.int32
    gq, gk, gv = pl.pallas_call(
        layer,
        out_shape=(shaped(TOK, HEADS * HS),) * 3,
        in_specs=[SM, SM, SM, VM, VM, VM, VM, VM],
        out_specs=(VM,) * 3,
        scratch_shapes=[
            pltpu.VMEM((RING, 3, ROWS, HS), BF),
            pltpu.VMEM((RING, ROWS, HS), BF),
            pltpu.VMEM((HEADS, HS, grad_mixed.shape[2]), BF),
            pltpu.VMEM((RING, ROWS, HS), BF),
            pltpu.VMEM((2 * RING, 2, ROWS, HS), BF),
            pltpu.VMEM((RING, ROWS, HS), BF),
            pltpu.VMEM((2 * RING, 2, HS, ROWS), BF),
            pltpu.VMEM((2 * PAIRS, 2, ROWS, HS), BF),
            pltpu.VMEM((PAIRS, 2, HS, 2 * ROWS), BF),
            pltpu.VMEM((PAIRS, 2, ROWS, HS), BF),
            pltpu.VMEM((2, ROWS, LROWS), i32),
            pltpu.VMEM((RING + PAIRS, 8, ROWS), i32),
            pltpu.VMEM((NEAR, ROWS, ROWS), f32),
            pltpu.VMEM((RING, NEAR, ROWS, ROWS), BF),
            pltpu.VMEM((PAIRS, 2 * PAIRS, ROWS, ROWS), BF),
            pltpu.VMEM((RING, HS, ROWS), f32),
            pltpu.VMEM((PAIRS, PAIRS, HS, ROWS), f32),
            pltpu.VMEM((STATS, 8, ROWS), f32),
            pltpu.VMEM((RING + PAIRS, 8, ROWS), f32),
            pltpu.VMEM((2 * RING, 2, ROWS, HS), f32),
            pltpu.VMEM((RING, HS, ROWS), f32),
            pltpu.VMEM((RING, 2, ROWS, HS), BF),
            pltpu.VMEM((RING, 2, ROWS, HS), BF),
            pltpu.VMEM((RING, ROWS, HS), BF),
            pltpu.VMEM((RING, 2, ROWS, HS), BF),
            pltpu.VMEM((RING, ROWS, HS), BF),
            pltpu.VMEM((RING, 2, ROWS, HS), BF),
            DMA((2, RING)),
            DMA((2, RING)),
            DMA((RING,)),
            DMA((RING,)),
            DMA((RING,)),
            DMA((RING,)),
            DMA,
            DMA,
            DMA((ROW_LINES,)),
            DMA((ROW_LINES,)),
            DMA((RING,)),
            DMA((RING,)),
            DMA((RING,)),
            DMA((RING,)),
            DMA((2, RING)),
            DMA((2, RING)),
            DMA((RING,)),
            DMA((RING,)),
        ],
        compiler_params=pltpu.CompilerParams(
            collective_id=0, has_side_effects=True, vmem_limit_bytes=VMEM_LIMIT
        ),
        name="layer",
    )(
        head_phase,
        segments_short,
        segments_long,
        q[0],
        k[0],
        v[0],
        grad_mixed[0],
        out_weight,
    )
    return gq[None], gk[None], gv[None]


def solution(mesh):
    placed = (
        P("fsdp", "seq", None),
        P("fsdp", "seq", None),
        P("fsdp", "seq", None),
        P("fsdp", "seq", None),
        P("fsdp", None),
        P(),
        P(),
        P(),
    )
    return jax.shard_map(
        shards,
        mesh=mesh,
        in_specs=placed,
        out_specs=(P("fsdp", "seq", None), P("fsdp", "seq", None), P("fsdp", "seq", None)),
        check_vma=False,
    )
```

```python
import functools
import math

import jax
import jax.numpy as jnp
from jax import lax
from jax.experimental import pallas as pl
from jax.experimental.pallas import tpu as pltpu
from jax.sharding import PartitionSpec as P

HEADS = 8
HS = 128
TOK = 512
ROWS = 256
LROWS = 128
RING = 8
ROW_LINES = 4
XS = 4
PAIRS = 4
NEAR = 5
STATS = RING + PAIRS * PAIRS
NEG = -1e30
SCALE = 1.0 / math.sqrt(HS)
EXP_SCALE = SCALE * math.log2(math.e)
NT = (((1,), (1,)), ((), ()))
NN = (((1,), (0,)), ((), ()))
TN = (((0,), (0,)), ((), ()))
VMEM_LIMIT = 60 * 1024 * 1024


def dot(a, b, dims):
    return lax.dot_general(a, b, dims, preferred_element_type=jnp.float32)


def token_of(row, phase):
    other = jnp.where(phase < 2, phase + 2, phase - 2)
    return 4 * (row & (LROWS - 1)) + jnp.where(row < LROWS, phase, other)


def pick_matrix(phase):
    row = lax.broadcasted_iota(jnp.int32, (ROWS, TOK), 0)
    tok = lax.broadcasted_iota(jnp.int32, (ROWS, TOK), 1)
    return (tok == token_of(row, phase)).astype(jnp.float32).astype(jnp.bfloat16)


def spread_matrix(phase):
    row = lax.broadcasted_iota(jnp.int32, (TOK, ROWS), 1)
    tok = lax.broadcasted_iota(jnp.int32, (TOK, ROWS), 0)
    return (tok == token_of(row, phase)).astype(jnp.float32).astype(jnp.bfloat16)


def place():
    me = lax.axis_index("seq")
    return me, me // RING, lax.rem(me, RING)


def greet(line, pos, columns, gather):
    barrier = pltpu.get_barrier_semaphore()
    for o in range(1, RING):
        pl.semaphore_signal(
            barrier, inc=1, device_id={"seq": line * RING + lax.rem(pos + o, RING)}
        )
    for o in columns:
        pl.semaphore_signal(
            barrier, inc=1, device_id={"seq": lax.rem(line + o, ROW_LINES) * RING + pos}
        )
    total = RING - 1 + len(columns)
    if gather:
        f = lax.axis_index("fsdp")
        x, hi = f // 2, lax.rem(f, 2)
        pl.semaphore_signal(barrier, inc=1, device_id={"fsdp": 2 * x + 1 - hi})
        for o in range(1, XS):
            pl.semaphore_signal(barrier, inc=1, device_id={"fsdp": 2 * lax.rem(x + o, XS) + hi})
        total += XS
    pl.semaphore_wait(barrier, total)


def layer(
    phase_ref,
    short_ref,
    long_ref,
    q_ref,
    k_ref,
    v_ref,
    g_ref,
    w_ref,
    gq_ref,
    gk_ref,
    gv_ref,
    stage,
    gstage,
    w_all,
    qo_ref,
    kvo_ref,
    do_ref,
    kt_ref,
    lkv_ref,
    lkt_ref,
    lq_ref,
    off_ref,
    rows_ref,
    s_ref,
    p_ref,
    lp_ref,
    o_ref,
    lo_ref,
    st_ref,
    delta_ref,
    acc,
    dq_acc,
    far_stage,
    near,
    dq_stage,
    kv_stage,
    got_q,
    got_kv,
    send_sem,
    recv_sem,
    hsend,
    hrecv,
    gsend,
    grecv,
    zsend,
    zrecv,
    ysend,
    yrecv,
    xsend,
    xrecv,
    csend,
    crecv,
    bsend,
    brecv,
    fsend,
    frecv,
):
    me, line, pos = place()
    core = lax.rem(me, 2)
    f = lax.axis_index("fsdp")
    x, hi = f // 2, lax.rem(f, 2)
    mate = 2 * x + 1 - hi
    greet(line, pos, (1, 2, 3), True)
    half = pl.ds(pl.multiple_of(core * 64, 64), 64)
    piece = pl.ds(pl.multiple_of(core * 64 + line * 16, 16), 16)

    to_mate = pltpu.make_async_remote_copy(
        src_ref=w_ref.at[piece],
        dst_ref=w_all.at[f, piece],
        send_sem=zsend,
        recv_sem=zrecv,
        device_id={"fsdp": mate},
    )

    def along_y(o):
        return pltpu.make_async_remote_copy(
            src_ref=w_all.at[mate, piece],
            dst_ref=w_all.at[mate, piece],
            send_sem=ysend.at[o],
            recv_sem=yrecv.at[o],
            device_id={"seq": lax.rem(line + o, ROW_LINES) * RING + pos},
        )

    def along_x(j, own):
        m = jnp.maximum(j - 2, 0)
        src = w_ref.at[half] if own else w_all.at[mate, half]
        return pltpu.make_async_remote_copy(
            src_ref=src,
            dst_ref=w_all.at[f if own else mate, half],
            send_sem=xsend.at[j],
            recv_sem=xrecv.at[j],
            device_id={"fsdp": 2 * lax.rem(x + lax.rem(m, 3) + 1, XS) + hi},
        )

    def slot(j):
        m = jnp.maximum(j - 2, 0)
        other = 2 * lax.rem(x + XS - 1 - lax.rem(m, 3), XS) + jnp.where(m < 3, hi, 1 - hi)
        return jnp.where(j == 0, f, jnp.where(j == 1, mate, other))

    def to_core(j):
        return pltpu.make_async_remote_copy(
            src_ref=w_all.at[slot(j), half],
            dst_ref=w_all.at[slot(j), half],
            send_sem=csend.at[j],
            recv_sem=crecv.at[j],
            device_id={"seq": me + 1 - 2 * core},
        )

    to_mate.start()
    for j in range(2, 5):
        along_x(j, True).start()

    def packed(h):
        pick = pick_matrix(phase_ref[h])
        cols = pl.ds(pl.multiple_of(h * HS, HS), HS)
        return [dot(pick, ref[:, cols], NN).astype(jnp.bfloat16) for ref in (q_ref, k_ref, v_ref)]

    def to_peer(o, what):
        peer = line * RING + lax.rem(pos + o, RING)
        if what == 0:
            src, dst = stage.at[o, 0], qo_ref.at[pos]
        else:
            src, dst = stage.at[o, pl.ds(1, 2)], kvo_ref.at[RING + pos]
        return pltpu.make_async_remote_copy(
            src_ref=src,
            dst_ref=dst,
            send_sem=send_sem.at[what, o],
            recv_sem=recv_sem.at[what, o],
            device_id={"seq": peer},
        )

    def far(s):
        return pltpu.make_async_remote_copy(
            src_ref=kvo_ref.at[RING + s],
            dst_ref=kvo_ref.at[s],
            send_sem=hsend.at[s],
            recv_sem=hrecv.at[s],
            device_id={"seq": me + RING},
        )

    def far_long(s):
        return pltpu.make_async_remote_copy(
            src_ref=kvo_ref.at[RING + s, :, pl.ds(0, LROWS)],
            dst_ref=kvo_ref.at[s, :, pl.ds(0, LROWS)],
            send_sem=hsend.at[s],
            recv_sem=hrecv.at[s],
            device_id={"seq": me + RING},
        )

    def start(o, _):
        for i, rows in enumerate(packed(lax.rem(pos + o, RING))):
            stage[o, i] = rows
        to_peer(o, 1).start()
        return 0

    lax.fori_loop(1, RING, start, 0)

    def start_query(o, _):
        to_peer(o, 0).start()
        return 0

    lax.fori_loop(1, RING, start_query, 0)

    to_mate.wait_recv()
    for o in range(1, ROW_LINES):
        along_y(o).start()
    own = packed(pos)
    qo_ref[pos] = own[0]
    kvo_ref[RING + pos, 0] = own[1]
    kvo_ref[RING + pos, 1] = own[2]
    w_all[f] = w_ref[...]
    for o in range(1, ROW_LINES):
        along_y(o).wait_recv()
    for j in range(5, 8):
        along_x(j, False).start()
    to_core(1).start()

    def to_head(j, h):
        return pltpu.make_async_remote_copy(
            src_ref=gstage.at[j],
            dst_ref=do_ref.at[pos],
            send_sem=gsend.at[j],
            recv_sem=grecv.at[pos],
            device_id={"seq": line * RING + h},
        )

    def grad_head(j, _):
        h = slot(j)

        @pl.when((j >= 1) & (j < RING - 1))
        def _():
            along_x(j + 1, True).wait_recv()
            to_core(j + 1).start()

        @pl.when(j >= 1)
        def _():
            to_core(j).wait_recv()

        full = dot(g_ref[...], w_all[h], NT).astype(jnp.bfloat16)
        rows = dot(pick_matrix(phase_ref[h]), full, NN).astype(jnp.bfloat16)

        @pl.when(h == pos)
        def _():
            do_ref[pos] = rows

        @pl.when(h != pos)
        def _():
            gstage[j] = rows
            to_head(j, h).start()

        return 0

    lax.fori_loop(0, RING, grad_head, 0)

    def forward(o, _):
        s = lax.rem(pos + RING - o, RING)

        @pl.when(o > 0)
        def _():
            to_peer(o, 1).wait_recv()

        @pl.when((line < ROW_LINES - 1) & (s >= RING // 2))
        def _():
            far(s).start()

        @pl.when((lax.rem(line, 2) == 0) & (s < RING // 2))
        def _():
            far_long(s).start()

        return 0

    lax.fori_loop(0, RING, forward, 0)


    phase = phase_ref[pos]
    odd = lax.rem(line, 2)
    origin = (line - 1) * (RING * TOK)
    row = lax.broadcasted_iota(jnp.int32, (ROWS, LROWS), 0)
    off_ref[0] = token_of(row, phase)
    off_ref[1] = (row // LROWS) * TOK + 4 * (row & (LROWS - 1)) + phase

    def low_of(tok, lengths, count):
        low = jnp.full_like(tok, -origin)
        end = -origin
        for n in range(count):
            end = end + lengths[n]
            low = jnp.where(tok >= end, jnp.maximum(low, end), low)
        return low

    lane = lax.broadcasted_iota(jnp.int32, (1, ROWS), 1)
    query_off = token_of(lane, phase)
    pair_off = (lane // LROWS) * TOK + 4 * (lane & (LROWS - 1)) + phase

    def prepare_query(i, _):
        tok = (RING + i) * TOK + query_off
        rows_ref[i, pl.ds(0, 1), :] = tok
        rows_ref[i, pl.ds(1, 1), :] = low_of(tok, short_ref, short_ref.shape[0])
        return 0

    lax.fori_loop(0, RING, prepare_query, 0)

    def prepare_pair(ii, _):
        tok = (RING + 2 * ii) * TOK + pair_off
        rows_ref[RING + ii, pl.ds(0, 1), :] = tok
        rows_ref[RING + ii, pl.ds(1, 1), :] = low_of(tok, long_ref, long_ref.shape[0])
        return 0

    lax.fori_loop(0, PAIRS, prepare_pair, 0)

    st_ref[:, pl.ds(0, 1), :] = jnp.full((STATS, 1, ROWS), NEG, jnp.float32)
    st_ref[:, pl.ds(1, 3), :] = jnp.zeros((STATS, 3, ROWS), jnp.float32)
    acc[...] = jnp.zeros_like(acc)
    dq_acc[...] = jnp.zeros_like(dq_acc)
    lo_ref[...] = jnp.zeros_like(lo_ref)

    @pl.when(line == 0)
    def _():
        kvo_ref[pl.ds(0, RING)] = jnp.zeros((RING, 2, ROWS, HS), jnp.bfloat16)

    def got_query(o, _):
        to_peer(o, 0).wait_recv()
        return 0

    lax.fori_loop(1, RING, got_query, 0)

    def prepare_key(g, _):
        kt_ref[g, 0] = kvo_ref[g, 0].T
        kt_ref[g, 1] = kvo_ref[g, 1].T
        return 0

    def prepare_key_pair(kp, _):
        for e in range(2):
            for w in range(2):
                lkv_ref[kp, w, pl.ds(e * LROWS, LROWS), :] = kvo_ref[
                    2 * kp + e, w, pl.ds(0, LROWS), :
                ]
        cols = pl.ds(pl.multiple_of(lax.rem(kp, 2) * ROWS, ROWS), ROWS)
        lkt_ref[kp // 2, 0, :, cols] = lkv_ref[kp, 0].T
        lkt_ref[kp // 2, 1, :, cols] = lkv_ref[kp, 1].T
        return 0

    def prepare_long_query(ii, _):
        for e in range(2):
            lq_ref[ii, 0, pl.ds(e * LROWS, LROWS), :] = qo_ref[2 * ii + e, pl.ds(0, LROWS), :]
        return 0

    lax.fori_loop(0, PAIRS, prepare_long_query, 0)
    lax.fori_loop(RING, 2 * RING, prepare_key, 0)
    lax.fori_loop(PAIRS, 2 * PAIRS, prepare_key_pair, 0)

    def strip(i, _):
        tok = rows_ref[i, pl.ds(0, 1), :]
        low = rows_ref[i, pl.ds(1, 1), :]
        q = qo_ref[i]
        off = jnp.concatenate([off_ref[0], off_ref[0]], axis=1)
        tops = []
        for d in range(NEAR):
            g = RING + i - d
            s = dot(kvo_ref[g, 0], q, NT)
            live = off >= low - g * TOK
            if d == 0:
                live = live & (off <= tok - g * TOK)
            s = jnp.where(live, s, NEG)
            s_ref[d] = s
            tops.append(jnp.max(s, axis=0, keepdims=True))
        m = functools.reduce(jnp.maximum, tops)
        l, o = jnp.zeros((1, ROWS), jnp.float32), jnp.zeros((HS, ROWS), jnp.float32)
        for d in range(NEAR):
            p = jnp.exp2((s_ref[d] - m) * EXP_SCALE)
            l = l + jnp.sum(p, axis=0, keepdims=True)
            w = p.astype(jnp.bfloat16)
            p_ref[i, d] = w
            o = o + dot(kt_ref[RING + i - d, 1], w, NN)
        st_ref[i, pl.ds(0, 1), :] = m
        st_ref[i, pl.ds(1, 1), :] = l
        o_ref[i] = o
        return 0

    def chunk(ii, c):
        tok = rows_ref[RING + ii, pl.ds(0, 1), :]
        low = rows_ref[RING + ii, pl.ds(1, 1), :]
        q = lq_ref[ii, 0]
        off = jnp.concatenate([off_ref[1], off_ref[1]], axis=1)
        scores = []
        for e in range(2):
            kp = 2 * c + e
            s = dot(lkv_ref[kp, 0], q, NT)
            at = kp * (2 * TOK)
            scores.append(jnp.where((off >= low - at) & (off <= tok - at), s, NEG))
        m = jnp.maximum(*[jnp.max(s, axis=0, keepdims=True) for s in scores])
        l = jnp.zeros((1, ROWS), jnp.float32)
        parts = []
        for e in range(2):
            p = jnp.exp2((scores[e] - m) * EXP_SCALE)
            l = l + jnp.sum(p, axis=0, keepdims=True)
            w = p.astype(jnp.bfloat16)
            lp_ref[ii, 2 * c + e] = w
            parts.append(w)
        t = RING + ii * PAIRS + c
        st_ref[t, pl.ds(0, 1), :] = m
        st_ref[t, pl.ds(1, 1), :] = l
        lo_ref[ii, c] = dot(lkt_ref[c, 1], jnp.concatenate(parts, axis=0), NN)

    def own_chunks(ii, _):
        chunk(ii, 2)

        @pl.when(ii >= 2)
        def _():
            chunk(ii, 3)

        return 0

    lax.fori_loop(0, PAIRS, own_chunks, 0)
    lax.fori_loop(RING // 2, RING, strip, 0)

    def got_far(s, _):
        @pl.when((line > 0) & (s >= RING // 2))
        def _():
            far(s).wait_recv()

        @pl.when((odd == 1) & (s < RING // 2))
        def _():
            far_long(s).wait_recv()

        return 0

    lax.fori_loop(0, RING, got_far, 0)
    lax.fori_loop(RING // 2, RING, prepare_key, 0)
    lax.fori_loop(0, RING // 2, strip, 0)

    @pl.when(odd == 1)
    def _():
        lax.fori_loop(0, PAIRS, prepare_key_pair, 0)

        def far_chunks(n, _):
            chunk(n // 2, lax.rem(n, 2))
            return 0

        lax.fori_loop(0, 2 * PAIRS, far_chunks, 0)

    def got_grad(j, _):
        @pl.when(j != pos)
        def _():
            pltpu.make_async_remote_copy(
                src_ref=gstage.at[j],
                dst_ref=do_ref.at[j],
                send_sem=gsend.at[j],
                recv_sem=grecv.at[j],
                device_id={"seq": line * RING + lax.rem(pos + 1, RING)},
            ).wait_recv()

        return 0

    lax.fori_loop(0, RING, got_grad, 0)

    def join(ii, _):
        base = RING + ii * PAIRS
        lst = [st_ref[base + c] for c in range(PAIRS)]
        tops, invs, deltas = [], [], []
        for e in range(2):
            i = 2 * ii + e
            lq_ref[ii, 1, pl.ds(e * LROWS, LROWS), :] = do_ref[i, pl.ds(0, LROWS), :]
            here = slice(e * LROWS, (e + 1) * LROWS)
            m = st_ref[i, pl.ds(0, 1), :]
            ml = functools.reduce(jnp.maximum, [a[0:1, here] for a in lst], m[:, :LROWS])
            w = jnp.exp2((m - jnp.concatenate([ml, m[:, LROWS:]], axis=1)) * EXP_SCALE)
            wl = [jnp.exp2((a[0:1, here] - ml) * EXP_SCALE) for a in lst]
            l = w * st_ref[i, pl.ds(1, 1), :]
            ll = sum((x * a[1:2, here] for x, a in zip(wl, lst)), l[:, :LROWS])
            inv = 1.0 / jnp.concatenate([ll, l[:, LROWS:]], axis=1)
            o = o_ref[i] * w
            ol = o[:, :LROWS]
            for c in range(PAIRS):
                ol = ol + lo_ref[ii, c, :, here] * wl[c]
            o = jnp.concatenate([ol, o[:, LROWS:]], axis=1)
            gt = do_ref[i].T.astype(jnp.float32)
            delta = jnp.sum(gt * (o * inv), axis=0, keepdims=True)
            delta_ref[i, pl.ds(0, 1), :] = delta
            st_ref[i, pl.ds(3, 1), :] = w * inv
            tops.append(ml)
            invs.append(inv[:, :LROWS])
            deltas.append(delta[:, :LROWS])
        ml = jnp.concatenate(tops, axis=1)
        il = jnp.concatenate(invs, axis=1)
        delta_ref[RING + ii, pl.ds(0, 1), :] = jnp.concatenate(deltas, axis=1)
        for c in range(PAIRS):
            st_ref[base + c, pl.ds(3, 1), :] = jnp.exp2((lst[c][0:1] - ml) * EXP_SCALE) * il
        return 0

    lax.fori_loop(0, PAIRS, join, 0)

    def back(weights, scales, deltas, v, kt, q, do):
        dp = dot(v, do, NT)
        pbs, dss = [], []
        for u, (w, a, delta) in enumerate(zip(weights, scales, deltas)):
            pr = w.astype(jnp.float32) * a
            dss.append((pr * (dp[:, u * ROWS : (u + 1) * ROWS] - delta)).astype(jnp.bfloat16))
            pbs.append(pr.astype(jnp.bfloat16))
        ds = jnp.concatenate(dss, axis=1)
        pb = jnp.concatenate(pbs, axis=1)
        return dot(ds, q, NN), dot(pb, do, NN), dot(kt, ds, NN)

    def back_pair(kp, first, count):
        cols = pl.ds(pl.multiple_of(lax.rem(kp, 2) * ROWS, ROWS), ROWS)
        dk, dv, dq = back(
            [lp_ref[first + u, kp] for u in range(count)],
            [
                st_ref[RING + (first + u) * PAIRS + kp // 2, pl.ds(3, 1), :]
                for u in range(count)
            ],
            [delta_ref[RING + first + u, pl.ds(0, 1), :] for u in range(count)],
            lkv_ref[kp, 1],
            lkt_ref[kp // 2, 0, :, cols],
            lq_ref[pl.ds(first, count), 0].reshape(count * ROWS, HS),
            lq_ref[pl.ds(first, count), 1].reshape(count * ROWS, HS),
        )
        for e in range(2):
            part = slice(e * LROWS, (e + 1) * LROWS)
            acc[2 * kp + e, 0, pl.ds(0, LROWS), :] += dk[part]
            acc[2 * kp + e, 1, pl.ds(0, LROWS), :] += dv[part]
        for u in range(count):
            for e in range(2):
                at = u * ROWS + e * LROWS
                dq_acc[2 * (first + u) + e, :, pl.ds(0, LROWS)] += dq[:, at : at + LROWS]

    def back_block(g, first, count):
        d = RING + first - g
        dk, dv, dq = back(
            [p_ref[first + u, d + u] for u in range(count)],
            [st_ref[first + u, pl.ds(3, 1), :] for u in range(count)],
            [delta_ref[first + u, pl.ds(0, 1), :] for u in range(count)],
            kvo_ref[g, 1],
            kt_ref[g, 0],
            qo_ref[pl.ds(first, count)].reshape(count * ROWS, HS),
            do_ref[pl.ds(first, count)].reshape(count * ROWS, HS),
        )
        acc[g, 0] += dk
        acc[g, 1] += dv
        for u in range(count):
            dq_acc[first + u] += dq[:, u * ROWS : (u + 1) * ROWS]

    def give(s):
        return pltpu.make_async_remote_copy(
            src_ref=far_stage.at[s],
            dst_ref=near.at[s],
            send_sem=fsend.at[s],
            recv_sem=frecv.at[s],
            device_id={"seq": me - RING},
        )

    def give_long(s):
        return pltpu.make_async_remote_copy(
            src_ref=far_stage.at[s, :, pl.ds(0, LROWS)],
            dst_ref=near.at[s, :, pl.ds(0, LROWS)],
            send_sem=fsend.at[s],
            recv_sem=frecv.at[s],
            device_id={"seq": me - RING},
        )

    def home(s, what):
        if what == 0:
            src, dst = dq_stage.at[s], got_q.at[pos]
        else:
            src, dst = kv_stage.at[s], got_kv.at[pos]
        return pltpu.make_async_remote_copy(
            src_ref=src,
            dst_ref=dst,
            send_sem=bsend.at[what, s],
            recv_sem=brecv.at[what, pos],
            device_id={"seq": line * RING + s},
        )

    def landed(s, what):
        dst = got_q.at[s] if what == 0 else got_kv.at[s]
        src = dq_stage.at[s] if what == 0 else kv_stage.at[s]
        return pltpu.make_async_remote_copy(
            src_ref=src,
            dst_ref=dst,
            send_sem=bsend.at[what, s],
            recv_sem=brecv.at[what, s],
            device_id={"seq": line * RING + lax.rem(pos + 1, RING)},
        )

    def emit_far(g):
        far_stage[g, 0] = (acc[g, 0] * SCALE).astype(jnp.bfloat16)
        far_stage[g, 1] = acc[g, 1].astype(jnp.bfloat16)

    @pl.when(odd == 1)
    def _():
        def far_pair(kp, _):
            back_pair(kp, 0, PAIRS)

            @pl.when(kp < PAIRS // 2)
            def _():
                for e in range(2):
                    emit_far(2 * kp + e)
                    give_long(2 * kp + e).start()

            return 0

        lax.fori_loop(0, PAIRS, far_pair, 0)

    @pl.when(line > 0)
    def _():
        for g in range(RING // 2, RING):
            back_block(g, 0, g - (RING - NEAR))
            emit_far(g)
            give(g).start()

    def joined(b):
        full = (line < ROW_LINES - 1) & (b >= RING // 2)
        half = (odd == 0) & (b < RING // 2)
        return full, half

    def own_block(b, count):
        back_block(RING + b, b, count)
        dq_stage[b] = (dq_acc[b].T * SCALE).astype(jnp.bfloat16)

        @pl.when(b != pos)
        def _():
            home(b, 0).start()

        full, half = joined(b)

        @pl.when(jnp.logical_not(full | half))
        def _():
            kv_stage[b, 0] = (acc[RING + b, 0] * SCALE).astype(jnp.bfloat16)
            kv_stage[b, 1] = acc[RING + b, 1].astype(jnp.bfloat16)

            @pl.when(b != pos)
            def _():
                home(b, 1).start()

    def own_block_near(b, _):
        own_block(b, NEAR)
        return 0

    for kp in range(PAIRS):
        back_pair(PAIRS + kp, kp, PAIRS - kp)
        if 2 * kp + NEAR < RING:
            lax.fori_loop(2 * kp, 2 * kp + 2, own_block_near, 0)
        else:
            for e in range(2):
                own_block(2 * kp + e, RING - 2 * kp - e)

    def add_near(b, _):
        full, half = joined(b)

        @pl.when(full)
        def _():
            give(b).wait_recv()

        @pl.when(half)
        def _():
            give_long(b).wait_recv()
            near[b, :, pl.ds(LROWS, LROWS)] = jnp.zeros((2, LROWS, HS), jnp.bfloat16)

        @pl.when(full | half)
        def _():
            kv_stage[b, 0] = (acc[RING + b, 0] * SCALE + near[b, 0].astype(jnp.float32)).astype(
                jnp.bfloat16
            )
            kv_stage[b, 1] = (acc[RING + b, 1] + near[b, 1].astype(jnp.float32)).astype(
                jnp.bfloat16
            )

            @pl.when(b != pos)
            def _():
                home(b, 1).start()

        return 0

    lax.fori_loop(0, RING, add_near, 0)
    got_q[pos] = dq_stage[pos]
    got_kv[pos] = kv_stage[pos]

    def unpack(o, _):
        h = lax.rem(pos + RING - o, RING)

        @pl.when(o > 0)
        def _():
            landed(h, 0).wait_recv()
            landed(h, 1).wait_recv()

        spread = spread_matrix(phase_ref[h])
        cols = pl.ds(pl.multiple_of(h * HS, HS), HS)
        gq_ref[:, cols] = dot(spread, got_q[h], NN).astype(jnp.bfloat16)
        gk_ref[:, cols] = dot(spread, got_kv[h, 0], NN).astype(jnp.bfloat16)
        gv_ref[:, cols] = dot(spread, got_kv[h, 1], NN).astype(jnp.bfloat16)
        return 0

    lax.fori_loop(0, RING, unpack, 0)

    def finish(o, _):
        s = lax.rem(pos + o, RING)
        home(s, 0).wait_send()
        home(s, 1).wait_send()
        return 0

    lax.fori_loop(1, RING, finish, 0)

    def finish_far(s, _):
        @pl.when((line > 0) & (s >= RING // 2))
        def _():
            give(s).wait_send()

        @pl.when((odd == 1) & (s < RING // 2))
        def _():
            give_long(s).wait_send()

        return 0

    lax.fori_loop(0, RING, finish_far, 0)

    def sent(o, _):
        to_peer(o, 0).wait_send()
        to_peer(o, 1).wait_send()
        return 0

    lax.fori_loop(1, RING, sent, 0)

    def sent_grad(j, _):
        h = slot(j)

        @pl.when(h != pos)
        def _():
            to_head(j, h).wait_send()

        return 0

    lax.fori_loop(0, RING, sent_grad, 0)

    def sent_far(s, _):
        @pl.when((line < ROW_LINES - 1) & (s >= RING // 2))
        def _():
            far(s).wait_send()

        @pl.when((lax.rem(line, 2) == 0) & (s < RING // 2))
        def _():
            far_long(s).wait_send()

        return 0

    lax.fori_loop(0, RING, sent_far, 0)
    to_mate.wait_send()
    for o in range(1, ROW_LINES):
        along_y(o).wait_send()
    for j in range(2, 8):
        along_x(j, True).wait_send()
    for j in range(1, 8):
        to_core(j).wait_send()


VM = pl.BlockSpec(memory_space=pltpu.VMEM)
SM = pl.BlockSpec(memory_space=pltpu.SMEM)
DMA = pltpu.SemaphoreType.DMA
BF = jnp.bfloat16


def shaped(*dims, dtype=BF):
    return jax.ShapeDtypeStruct(dims, dtype)


def shards(q, k, v, grad_mixed, out_weight, head_phase, segments_short, segments_long):
    me = lax.axis_index("seq")
    line, pos = me // RING, lax.rem(me, RING)
    f32, i32 = jnp.float32, jnp.int32
    gq, gk, gv = pl.pallas_call(
        layer,
        out_shape=(shaped(TOK, HEADS * HS),) * 3,
        in_specs=[SM, SM, SM, VM, VM, VM, VM, VM],
        out_specs=(VM,) * 3,
        scratch_shapes=[
            pltpu.VMEM((RING, 3, ROWS, HS), BF),
            pltpu.VMEM((RING, ROWS, HS), BF),
            pltpu.VMEM((HEADS, HS, grad_mixed.shape[2]), BF),
            pltpu.VMEM((RING, ROWS, HS), BF),
            pltpu.VMEM((2 * RING, 2, ROWS, HS), BF),
            pltpu.VMEM((RING, ROWS, HS), BF),
            pltpu.VMEM((2 * RING, 2, HS, ROWS), BF),
            pltpu.VMEM((2 * PAIRS, 2, ROWS, HS), BF),
            pltpu.VMEM((PAIRS, 2, HS, 2 * ROWS), BF),
            pltpu.VMEM((PAIRS, 2, ROWS, HS), BF),
            pltpu.VMEM((2, ROWS, LROWS), i32),
            pltpu.VMEM((RING + PAIRS, 8, ROWS), i32),
            pltpu.VMEM((NEAR, ROWS, ROWS), f32),
            pltpu.VMEM((RING, NEAR, ROWS, ROWS), BF),
            pltpu.VMEM((PAIRS, 2 * PAIRS, ROWS, ROWS), BF),
            pltpu.VMEM((RING, HS, ROWS), f32),
            pltpu.VMEM((PAIRS, PAIRS, HS, ROWS), f32),
            pltpu.VMEM((STATS, 8, ROWS), f32),
            pltpu.VMEM((RING + PAIRS, 8, ROWS), f32),
            pltpu.VMEM((2 * RING, 2, ROWS, HS), f32),
            pltpu.VMEM((RING, HS, ROWS), f32),
            pltpu.VMEM((RING, 2, ROWS, HS), BF),
            pltpu.VMEM((RING, 2, ROWS, HS), BF),
            pltpu.VMEM((RING, ROWS, HS), BF),
            pltpu.VMEM((RING, 2, ROWS, HS), BF),
            pltpu.VMEM((RING, ROWS, HS), BF),
            pltpu.VMEM((RING, 2, ROWS, HS), BF),
            DMA((2, RING)),
            DMA((2, RING)),
            DMA((RING,)),
            DMA((RING,)),
            DMA((RING,)),
            DMA((RING,)),
            DMA,
            DMA,
            DMA((ROW_LINES,)),
            DMA((ROW_LINES,)),
            DMA((RING,)),
            DMA((RING,)),
            DMA((RING,)),
            DMA((RING,)),
            DMA((2, RING)),
            DMA((2, RING)),
            DMA((RING,)),
            DMA((RING,)),
        ],
        compiler_params=pltpu.CompilerParams(
            collective_id=0, has_side_effects=True, vmem_limit_bytes=VMEM_LIMIT
        ),
        name="layer",
    )(
        head_phase,
        segments_short,
        segments_long,
        q[0],
        k[0],
        v[0],
        grad_mixed[0],
        out_weight,
    )
    return gq[None], gk[None], gv[None]


def solution(mesh):
    placed = (
        P("fsdp", "seq", None),
        P("fsdp", "seq", None),
        P("fsdp", "seq", None),
        P("fsdp", "seq", None),
        P("fsdp", None),
        P(),
        P(),
        P(),
    )
    return jax.shard_map(
        shards,
        mesh=mesh,
        in_specs=placed,
        out_specs=(P("fsdp", "seq", None), P("fsdp", "seq", None), P("fsdp", "seq", None)),
        check_vma=False,
    )
```

```python
import functools
import math

import jax
import jax.numpy as jnp
from jax import lax
from jax.experimental import pallas as pl
from jax.experimental.pallas import tpu as pltpu
from jax.sharding import PartitionSpec as P

HEADS = 8
HS = 128
TOK = 512
ROWS = 256
LROWS = 128
RING = 8
ROW_LINES = 4
XS = 4
PAIRS = 4
NEAR = 5
STATS = RING + PAIRS * PAIRS
NEG = -1e30
SCALE = 1.0 / math.sqrt(HS)
EXP_SCALE = SCALE * math.log2(math.e)
NT = (((1,), (1,)), ((), ()))
NN = (((1,), (0,)), ((), ()))
TN = (((0,), (0,)), ((), ()))
VMEM_LIMIT = 60 * 1024 * 1024


def dot(a, b, dims):
    return lax.dot_general(a, b, dims, preferred_element_type=jnp.float32)


def token_of(row, phase):
    other = jnp.where(phase < 2, phase + 2, phase - 2)
    return 4 * (row & (LROWS - 1)) + jnp.where(row < LROWS, phase, other)


def pick_matrix(phase):
    row = lax.broadcasted_iota(jnp.int32, (ROWS, TOK), 0)
    tok = lax.broadcasted_iota(jnp.int32, (ROWS, TOK), 1)
    return (tok == token_of(row, phase)).astype(jnp.float32).astype(jnp.bfloat16)


def spread_matrix(phase):
    row = lax.broadcasted_iota(jnp.int32, (TOK, ROWS), 1)
    tok = lax.broadcasted_iota(jnp.int32, (TOK, ROWS), 0)
    return (tok == token_of(row, phase)).astype(jnp.float32).astype(jnp.bfloat16)


def place():
    me = lax.axis_index("seq")
    return me, me // RING, lax.rem(me, RING)


def greet(line, pos, columns, gather):
    barrier = pltpu.get_barrier_semaphore()
    for o in range(1, RING):
        pl.semaphore_signal(
            barrier, inc=1, device_id={"seq": line * RING + lax.rem(pos + o, RING)}
        )
    for o in columns:
        pl.semaphore_signal(
            barrier, inc=1, device_id={"seq": lax.rem(line + o, ROW_LINES) * RING + pos}
        )
    total = RING - 1 + len(columns)
    if gather:
        f = lax.axis_index("fsdp")
        x, hi = f // 2, lax.rem(f, 2)
        pl.semaphore_signal(barrier, inc=1, device_id={"fsdp": 2 * x + 1 - hi})
        for o in range(1, XS):
            pl.semaphore_signal(barrier, inc=1, device_id={"fsdp": 2 * lax.rem(x + o, XS) + hi})
        total += XS
    pl.semaphore_wait(barrier, total)


def layer(
    phase_ref,
    short_ref,
    long_ref,
    q_ref,
    k_ref,
    v_ref,
    g_ref,
    w_ref,
    gq_ref,
    gk_ref,
    gv_ref,
    stage,
    gstage,
    w_all,
    qo_ref,
    kvo_ref,
    do_ref,
    kt_ref,
    lkv_ref,
    lkt_ref,
    lq_ref,
    off_ref,
    rows_ref,
    s_ref,
    p_ref,
    lp_ref,
    o_ref,
    lo_ref,
    st_ref,
    delta_ref,
    acc,
    dq_acc,
    far_stage,
    near,
    dq_stage,
    kv_stage,
    got_q,
    got_kv,
    send_sem,
    recv_sem,
    hsend,
    hrecv,
    gsend,
    grecv,
    zsend,
    zrecv,
    ysend,
    yrecv,
    xsend,
    xrecv,
    csend,
    crecv,
    bsend,
    brecv,
    fsend,
    frecv,
):
    me, line, pos = place()
    core = lax.rem(me, 2)
    f = lax.axis_index("fsdp")
    x, hi = f // 2, lax.rem(f, 2)
    mate = 2 * x + 1 - hi
    greet(line, pos, (1, 2, 3), True)
    half = pl.ds(pl.multiple_of(core * 64, 64), 64)
    piece = pl.ds(pl.multiple_of(core * 64 + line * 16, 16), 16)

    to_mate = pltpu.make_async_remote_copy(
        src_ref=w_ref.at[piece],
        dst_ref=w_all.at[f, piece],
        send_sem=zsend,
        recv_sem=zrecv,
        device_id={"fsdp": mate},
    )

    def along_y(o):
        return pltpu.make_async_remote_copy(
            src_ref=w_all.at[mate, piece],
            dst_ref=w_all.at[mate, piece],
            send_sem=ysend.at[o],
            recv_sem=yrecv.at[o],
            device_id={"seq": lax.rem(line + o, ROW_LINES) * RING + pos},
        )

    def along_x(step, kind, way):
        hop = 1 if way == 0 else XS - 1
        if step == 0:
            at = f if kind == 0 else mate
            rows = half
            src = w_ref.at[half] if kind == 0 else w_all.at[mate, half]
        else:
            at = 2 * lax.rem(x + XS - hop, XS) + (hi if kind == 0 else 1 - hi)
            rows = pl.ds(pl.multiple_of(core * 64 + way * 32, 32), 32)
            src = w_all.at[at, rows]
        return pltpu.make_async_remote_copy(
            src_ref=src,
            dst_ref=w_all.at[at, rows],
            send_sem=xsend.at[step, kind, way],
            recv_sem=xrecv.at[step, kind, way],
            device_id={"fsdp": 2 * lax.rem(x + hop, XS) + hi},
        )

    def slot(j):
        m = jnp.maximum(j - 2, 0)
        r = lax.rem(m, 3)
        hop = jnp.where(r == 0, XS - 1, r)
        other = 2 * lax.rem(x + hop, XS) + jnp.where(m < 3, hi, 1 - hi)
        return jnp.where(j == 0, f, jnp.where(j == 1, mate, other))

    def to_core(j):
        return pltpu.make_async_remote_copy(
            src_ref=w_all.at[slot(j), half],
            dst_ref=w_all.at[slot(j), half],
            send_sem=csend.at[j],
            recv_sem=crecv.at[j],
            device_id={"seq": me + 1 - 2 * core},
        )

    to_mate.start()
    for way in range(2):
        along_x(0, 0, way).start()

    def pass_on(kind):
        for way in range(2):
            along_x(0, kind, way).wait_recv()
            along_x(1, kind, way).start()
            to_core(2 + 3 * kind + way).start()

    def passed(kind):
        for way in range(2):
            along_x(1, kind, way).wait_recv()
        to_core(4 + 3 * kind).start()

    def packed(h):
        pick = pick_matrix(phase_ref[h])
        cols = pl.ds(pl.multiple_of(h * HS, HS), HS)
        return [dot(pick, ref[:, cols], NN).astype(jnp.bfloat16) for ref in (q_ref, k_ref, v_ref)]

    def to_peer(o, what):
        peer = line * RING + lax.rem(pos + o, RING)
        if what == 0:
            src, dst = stage.at[o, 0], qo_ref.at[pos]
        else:
            src, dst = stage.at[o, pl.ds(1, 2)], kvo_ref.at[RING + pos]
        return pltpu.make_async_remote_copy(
            src_ref=src,
            dst_ref=dst,
            send_sem=send_sem.at[what, o],
            recv_sem=recv_sem.at[what, o],
            device_id={"seq": peer},
        )

    def far(s):
        return pltpu.make_async_remote_copy(
            src_ref=kvo_ref.at[RING + s],
            dst_ref=kvo_ref.at[s],
            send_sem=hsend.at[s],
            recv_sem=hrecv.at[s],
            device_id={"seq": me + RING},
        )

    def far_long(s):
        return pltpu.make_async_remote_copy(
            src_ref=kvo_ref.at[RING + s, :, pl.ds(0, LROWS)],
            dst_ref=kvo_ref.at[s, :, pl.ds(0, LROWS)],
            send_sem=hsend.at[s],
            recv_sem=hrecv.at[s],
            device_id={"seq": me + RING},
        )

    def start(o, _):
        for i, rows in enumerate(packed(lax.rem(pos + o, RING))):
            stage[o, i] = rows
        to_peer(o, 1).start()
        return 0

    lax.fori_loop(1, RING, start, 0)

    def start_query(o, _):
        to_peer(o, 0).start()
        return 0

    lax.fori_loop(1, RING, start_query, 0)

    to_mate.wait_recv()
    for o in range(1, ROW_LINES):
        along_y(o).start()
    pass_on(0)
    own = packed(pos)
    qo_ref[pos] = own[0]
    kvo_ref[RING + pos, 0] = own[1]
    kvo_ref[RING + pos, 1] = own[2]
    w_all[f] = w_ref[...]
    for o in range(1, ROW_LINES):
        along_y(o).wait_recv()
    for way in range(2):
        along_x(0, 1, way).start()
    to_core(1).start()

    def to_head(j, h):
        return pltpu.make_async_remote_copy(
            src_ref=gstage.at[j],
            dst_ref=do_ref.at[pos],
            send_sem=gsend.at[j],
            recv_sem=grecv.at[pos],
            device_id={"seq": line * RING + h},
        )

    def grad_head(j, _):
        h = slot(j)

        @pl.when(j == 1)
        def _():
            passed(0)

        @pl.when(j == 2)
        def _():
            pass_on(1)

        @pl.when(j == 4)
        def _():
            passed(1)

        @pl.when(j >= 1)
        def _():
            to_core(j).wait_recv()

        full = dot(g_ref[...], w_all[h], NT).astype(jnp.bfloat16)
        rows = dot(pick_matrix(phase_ref[h]), full, NN).astype(jnp.bfloat16)

        @pl.when(h == pos)
        def _():
            do_ref[pos] = rows

        @pl.when(h != pos)
        def _():
            gstage[j] = rows
            to_head(j, h).start()

        return 0

    lax.fori_loop(0, RING, grad_head, 0)

    def forward(o, _):
        s = lax.rem(pos + RING - o, RING)

        @pl.when(o > 0)
        def _():
            to_peer(o, 1).wait_recv()

        @pl.when((line < ROW_LINES - 1) & (s >= RING // 2))
        def _():
            far(s).start()

        @pl.when((lax.rem(line, 2) == 0) & (s < RING // 2))
        def _():
            far_long(s).start()

        return 0

    lax.fori_loop(0, RING, forward, 0)


    phase = phase_ref[pos]
    odd = lax.rem(line, 2)
    origin = (line - 1) * (RING * TOK)
    row = lax.broadcasted_iota(jnp.int32, (ROWS, LROWS), 0)
    off_ref[0] = token_of(row, phase)
    off_ref[1] = (row // LROWS) * TOK + 4 * (row & (LROWS - 1)) + phase

    def low_of(tok, lengths, count):
        low = jnp.full_like(tok, -origin)
        end = -origin
        for n in range(count):
            end = end + lengths[n]
            low = jnp.where(tok >= end, jnp.maximum(low, end), low)
        return low

    lane = lax.broadcasted_iota(jnp.int32, (1, ROWS), 1)
    query_off = token_of(lane, phase)
    pair_off = (lane // LROWS) * TOK + 4 * (lane & (LROWS - 1)) + phase

    def prepare_query(i, _):
        tok = (RING + i) * TOK + query_off
        rows_ref[i, pl.ds(0, 1), :] = tok
        rows_ref[i, pl.ds(1, 1), :] = low_of(tok, short_ref, short_ref.shape[0])
        return 0

    lax.fori_loop(0, RING, prepare_query, 0)

    def prepare_pair(ii, _):
        tok = (RING + 2 * ii) * TOK + pair_off
        rows_ref[RING + ii, pl.ds(0, 1), :] = tok
        rows_ref[RING + ii, pl.ds(1, 1), :] = low_of(tok, long_ref, long_ref.shape[0])
        return 0

    lax.fori_loop(0, PAIRS, prepare_pair, 0)

    st_ref[:, pl.ds(0, 1), :] = jnp.full((STATS, 1, ROWS), NEG, jnp.float32)
    st_ref[:, pl.ds(1, 3), :] = jnp.zeros((STATS, 3, ROWS), jnp.float32)
    acc[...] = jnp.zeros_like(acc)
    dq_acc[...] = jnp.zeros_like(dq_acc)
    lo_ref[...] = jnp.zeros_like(lo_ref)

    @pl.when(line == 0)
    def _():
        kvo_ref[pl.ds(0, RING)] = jnp.zeros((RING, 2, ROWS, HS), jnp.bfloat16)

    def got_query(o, _):
        to_peer(o, 0).wait_recv()
        return 0

    lax.fori_loop(1, RING, got_query, 0)

    def prepare_key(g, _):
        kt_ref[g, 0] = kvo_ref[g, 0].T
        kt_ref[g, 1] = kvo_ref[g, 1].T
        return 0

    def prepare_key_pair(kp, _):
        for e in range(2):
            for w in range(2):
                lkv_ref[kp, w, pl.ds(e * LROWS, LROWS), :] = kvo_ref[
                    2 * kp + e, w, pl.ds(0, LROWS), :
                ]
        cols = pl.ds(pl.multiple_of(lax.rem(kp, 2) * ROWS, ROWS), ROWS)
        lkt_ref[kp // 2, 0, :, cols] = lkv_ref[kp, 0].T
        lkt_ref[kp // 2, 1, :, cols] = lkv_ref[kp, 1].T
        return 0

    def prepare_long_query(ii, _):
        for e in range(2):
            lq_ref[ii, 0, pl.ds(e * LROWS, LROWS), :] = qo_ref[2 * ii + e, pl.ds(0, LROWS), :]
        return 0

    lax.fori_loop(0, PAIRS, prepare_long_query, 0)
    lax.fori_loop(RING, 2 * RING, prepare_key, 0)
    lax.fori_loop(PAIRS, 2 * PAIRS, prepare_key_pair, 0)

    def strip(i, _):
        tok = rows_ref[i, pl.ds(0, 1), :]
        low = rows_ref[i, pl.ds(1, 1), :]
        q = qo_ref[i]
        off = jnp.concatenate([off_ref[0], off_ref[0]], axis=1)
        tops = []
        for d in range(NEAR):
            g = RING + i - d
            s = dot(kvo_ref[g, 0], q, NT)
            live = off >= low - g * TOK
            if d == 0:
                live = live & (off <= tok - g * TOK)
            s = jnp.where(live, s, NEG)
            s_ref[d] = s
            tops.append(jnp.max(s, axis=0, keepdims=True))
        m = functools.reduce(jnp.maximum, tops)
        l, o = jnp.zeros((1, ROWS), jnp.float32), jnp.zeros((HS, ROWS), jnp.float32)
        for d in range(NEAR):
            p = jnp.exp2((s_ref[d] - m) * EXP_SCALE)
            l = l + jnp.sum(p, axis=0, keepdims=True)
            w = p.astype(jnp.bfloat16)
            p_ref[i, d] = w
            o = o + dot(kt_ref[RING + i - d, 1], w, NN)
        st_ref[i, pl.ds(0, 1), :] = m
        st_ref[i, pl.ds(1, 1), :] = l
        o_ref[i] = o
        return 0

    def chunk(ii, c):
        tok = rows_ref[RING + ii, pl.ds(0, 1), :]
        low = rows_ref[RING + ii, pl.ds(1, 1), :]
        q = lq_ref[ii, 0]
        off = jnp.concatenate([off_ref[1], off_ref[1]], axis=1)
        scores = []
        for e in range(2):
            kp = 2 * c + e
            s = dot(lkv_ref[kp, 0], q, NT)
            at = kp * (2 * TOK)
            scores.append(jnp.where((off >= low - at) & (off <= tok - at), s, NEG))
        m = jnp.maximum(*[jnp.max(s, axis=0, keepdims=True) for s in scores])
        l = jnp.zeros((1, ROWS), jnp.float32)
        parts = []
        for e in range(2):
            p = jnp.exp2((scores[e] - m) * EXP_SCALE)
            l = l + jnp.sum(p, axis=0, keepdims=True)
            w = p.astype(jnp.bfloat16)
            lp_ref[ii, 2 * c + e] = w
            parts.append(w)
        t = RING + ii * PAIRS + c
        st_ref[t, pl.ds(0, 1), :] = m
        st_ref[t, pl.ds(1, 1), :] = l
        lo_ref[ii, c] = dot(lkt_ref[c, 1], jnp.concatenate(parts, axis=0), NN)

    def own_chunks(ii, _):
        chunk(ii, 2)

        @pl.when(ii >= 2)
        def _():
            chunk(ii, 3)

        return 0

    lax.fori_loop(0, PAIRS, own_chunks, 0)
    lax.fori_loop(RING // 2, RING, strip, 0)

    def got_far(s, _):
        @pl.when((line > 0) & (s >= RING // 2))
        def _():
            far(s).wait_recv()

        @pl.when((odd == 1) & (s < RING // 2))
        def _():
            far_long(s).wait_recv()

        return 0

    lax.fori_loop(0, RING, got_far, 0)
    lax.fori_loop(RING // 2, RING, prepare_key, 0)
    lax.fori_loop(0, RING // 2, strip, 0)

    @pl.when(odd == 1)
    def _():
        lax.fori_loop(0, PAIRS, prepare_key_pair, 0)

        def far_chunks(n, _):
            chunk(n // 2, lax.rem(n, 2))
            return 0

        lax.fori_loop(0, 2 * PAIRS, far_chunks, 0)

    def got_grad(j, _):
        @pl.when(j != pos)
        def _():
            pltpu.make_async_remote_copy(
                src_ref=gstage.at[j],
                dst_ref=do_ref.at[j],
                send_sem=gsend.at[j],
                recv_sem=grecv.at[j],
                device_id={"seq": line * RING + lax.rem(pos + 1, RING)},
            ).wait_recv()

        return 0

    lax.fori_loop(0, RING, got_grad, 0)

    def join(ii, _):
        base = RING + ii * PAIRS
        lst = [st_ref[base + c] for c in range(PAIRS)]
        tops, invs, deltas = [], [], []
        for e in range(2):
            i = 2 * ii + e
            lq_ref[ii, 1, pl.ds(e * LROWS, LROWS), :] = do_ref[i, pl.ds(0, LROWS), :]
            here = slice(e * LROWS, (e + 1) * LROWS)
            m = st_ref[i, pl.ds(0, 1), :]
            ml = functools.reduce(jnp.maximum, [a[0:1, here] for a in lst], m[:, :LROWS])
            w = jnp.exp2((m - jnp.concatenate([ml, m[:, LROWS:]], axis=1)) * EXP_SCALE)
            wl = [jnp.exp2((a[0:1, here] - ml) * EXP_SCALE) for a in lst]
            l = w * st_ref[i, pl.ds(1, 1), :]
            ll = sum((x * a[1:2, here] for x, a in zip(wl, lst)), l[:, :LROWS])
            inv = 1.0 / jnp.concatenate([ll, l[:, LROWS:]], axis=1)
            o = o_ref[i] * w
            ol = o[:, :LROWS]
            for c in range(PAIRS):
                ol = ol + lo_ref[ii, c, :, here] * wl[c]
            o = jnp.concatenate([ol, o[:, LROWS:]], axis=1)
            gt = do_ref[i].T.astype(jnp.float32)
            delta = jnp.sum(gt * (o * inv), axis=0, keepdims=True)
            delta_ref[i, pl.ds(0, 1), :] = delta
            st_ref[i, pl.ds(3, 1), :] = w * inv
            tops.append(ml)
            invs.append(inv[:, :LROWS])
            deltas.append(delta[:, :LROWS])
        ml = jnp.concatenate(tops, axis=1)
        il = jnp.concatenate(invs, axis=1)
        delta_ref[RING + ii, pl.ds(0, 1), :] = jnp.concatenate(deltas, axis=1)
        for c in range(PAIRS):
            st_ref[base + c, pl.ds(3, 1), :] = jnp.exp2((lst[c][0:1] - ml) * EXP_SCALE) * il
        return 0

    lax.fori_loop(0, PAIRS, join, 0)

    def back(weights, scales, deltas, v, kt, q, do):
        dp = dot(v, do, NT)
        pbs, dss = [], []
        for u, (w, a, delta) in enumerate(zip(weights, scales, deltas)):
            pr = w.astype(jnp.float32) * a
            dss.append((pr * (dp[:, u * ROWS : (u + 1) * ROWS] - delta)).astype(jnp.bfloat16))
            pbs.append(pr.astype(jnp.bfloat16))
        ds = jnp.concatenate(dss, axis=1)
        pb = jnp.concatenate(pbs, axis=1)
        return dot(ds, q, NN), dot(pb, do, NN), dot(kt, ds, NN)

    def back_pair(kp, first, count):
        cols = pl.ds(pl.multiple_of(lax.rem(kp, 2) * ROWS, ROWS), ROWS)
        dk, dv, dq = back(
            [lp_ref[first + u, kp] for u in range(count)],
            [
                st_ref[RING + (first + u) * PAIRS + kp // 2, pl.ds(3, 1), :]
                for u in range(count)
            ],
            [delta_ref[RING + first + u, pl.ds(0, 1), :] for u in range(count)],
            lkv_ref[kp, 1],
            lkt_ref[kp // 2, 0, :, cols],
            lq_ref[pl.ds(first, count), 0].reshape(count * ROWS, HS),
            lq_ref[pl.ds(first, count), 1].reshape(count * ROWS, HS),
        )
        for e in range(2):
            part = slice(e * LROWS, (e + 1) * LROWS)
            acc[2 * kp + e, 0, pl.ds(0, LROWS), :] += dk[part]
            acc[2 * kp + e, 1, pl.ds(0, LROWS), :] += dv[part]
        for u in range(count):
            for e in range(2):
                at = u * ROWS + e * LROWS
                dq_acc[2 * (first + u) + e, :, pl.ds(0, LROWS)] += dq[:, at : at + LROWS]

    def back_block(g, first, count):
        d = RING + first - g
        dk, dv, dq = back(
            [p_ref[first + u, d + u] for u in range(count)],
            [st_ref[first + u, pl.ds(3, 1), :] for u in range(count)],
            [delta_ref[first + u, pl.ds(0, 1), :] for u in range(count)],
            kvo_ref[g, 1],
            kt_ref[g, 0],
            qo_ref[pl.ds(first, count)].reshape(count * ROWS, HS),
            do_ref[pl.ds(first, count)].reshape(count * ROWS, HS),
        )
        acc[g, 0] += dk
        acc[g, 1] += dv
        for u in range(count):
            dq_acc[first + u] += dq[:, u * ROWS : (u + 1) * ROWS]

    def give(s):
        return pltpu.make_async_remote_copy(
            src_ref=far_stage.at[s],
            dst_ref=near.at[s],
            send_sem=fsend.at[s],
            recv_sem=frecv.at[s],
            device_id={"seq": me - RING},
        )

    def give_long(s):
        return pltpu.make_async_remote_copy(
            src_ref=far_stage.at[s, :, pl.ds(0, LROWS)],
            dst_ref=near.at[s, :, pl.ds(0, LROWS)],
            send_sem=fsend.at[s],
            recv_sem=frecv.at[s],
            device_id={"seq": me - RING},
        )

    def home(s, what):
        if what == 0:
            src, dst = dq_stage.at[s], got_q.at[pos]
        else:
            src, dst = kv_stage.at[s], got_kv.at[pos]
        return pltpu.make_async_remote_copy(
            src_ref=src,
            dst_ref=dst,
            send_sem=bsend.at[what, s],
            recv_sem=brecv.at[what, pos],
            device_id={"seq": line * RING + s},
        )

    def landed(s, what):
        dst = got_q.at[s] if what == 0 else got_kv.at[s]
        src = dq_stage.at[s] if what == 0 else kv_stage.at[s]
        return pltpu.make_async_remote_copy(
            src_ref=src,
            dst_ref=dst,
            send_sem=bsend.at[what, s],
            recv_sem=brecv.at[what, s],
            device_id={"seq": line * RING + lax.rem(pos + 1, RING)},
        )

    def emit_far(g):
        far_stage[g, 0] = (acc[g, 0] * SCALE).astype(jnp.bfloat16)
        far_stage[g, 1] = acc[g, 1].astype(jnp.bfloat16)

    @pl.when(odd == 1)
    def _():
        def far_pair(kp, _):
            back_pair(kp, 0, PAIRS)

            @pl.when(kp < PAIRS // 2)
            def _():
                for e in range(2):
                    emit_far(2 * kp + e)
                    give_long(2 * kp + e).start()

            return 0

        lax.fori_loop(0, PAIRS, far_pair, 0)

    @pl.when(line > 0)
    def _():
        for g in range(RING // 2, RING):
            back_block(g, 0, g - (RING - NEAR))
            emit_far(g)
            give(g).start()

    def joined(b):
        full = (line < ROW_LINES - 1) & (b >= RING // 2)
        half = (odd == 0) & (b < RING // 2)
        return full, half

    def own_block(b, count):
        back_block(RING + b, b, count)
        dq_stage[b] = (dq_acc[b].T * SCALE).astype(jnp.bfloat16)

        @pl.when(b != pos)
        def _():
            home(b, 0).start()

        full, half = joined(b)

        @pl.when(jnp.logical_not(full | half))
        def _():
            kv_stage[b, 0] = (acc[RING + b, 0] * SCALE).astype(jnp.bfloat16)
            kv_stage[b, 1] = acc[RING + b, 1].astype(jnp.bfloat16)

            @pl.when(b != pos)
            def _():
                home(b, 1).start()

    def own_block_near(b, _):
        own_block(b, NEAR)
        return 0

    for kp in range(PAIRS):
        back_pair(PAIRS + kp, kp, PAIRS - kp)
        if 2 * kp + NEAR < RING:
            lax.fori_loop(2 * kp, 2 * kp + 2, own_block_near, 0)
        else:
            for e in range(2):
                own_block(2 * kp + e, RING - 2 * kp - e)

    def add_near(b, _):
        full, half = joined(b)

        @pl.when(full)
        def _():
            give(b).wait_recv()

        @pl.when(half)
        def _():
            give_long(b).wait_recv()
            near[b, :, pl.ds(LROWS, LROWS)] = jnp.zeros((2, LROWS, HS), jnp.bfloat16)

        @pl.when(full | half)
        def _():
            kv_stage[b, 0] = (acc[RING + b, 0] * SCALE + near[b, 0].astype(jnp.float32)).astype(
                jnp.bfloat16
            )
            kv_stage[b, 1] = (acc[RING + b, 1] + near[b, 1].astype(jnp.float32)).astype(
                jnp.bfloat16
            )

            @pl.when(b != pos)
            def _():
                home(b, 1).start()

        return 0

    lax.fori_loop(0, RING, add_near, 0)
    got_q[pos] = dq_stage[pos]
    got_kv[pos] = kv_stage[pos]

    def unpack(o, _):
        h = lax.rem(pos + RING - o, RING)

        @pl.when(o > 0)
        def _():
            landed(h, 0).wait_recv()
            landed(h, 1).wait_recv()

        spread = spread_matrix(phase_ref[h])
        cols = pl.ds(pl.multiple_of(h * HS, HS), HS)
        gq_ref[:, cols] = dot(spread, got_q[h], NN).astype(jnp.bfloat16)
        gk_ref[:, cols] = dot(spread, got_kv[h, 0], NN).astype(jnp.bfloat16)
        gv_ref[:, cols] = dot(spread, got_kv[h, 1], NN).astype(jnp.bfloat16)
        return 0

    lax.fori_loop(0, RING, unpack, 0)

    def finish(o, _):
        s = lax.rem(pos + o, RING)
        home(s, 0).wait_send()
        home(s, 1).wait_send()
        return 0

    lax.fori_loop(1, RING, finish, 0)

    def finish_far(s, _):
        @pl.when((line > 0) & (s >= RING // 2))
        def _():
            give(s).wait_send()

        @pl.when((odd == 1) & (s < RING // 2))
        def _():
            give_long(s).wait_send()

        return 0

    lax.fori_loop(0, RING, finish_far, 0)

    def sent(o, _):
        to_peer(o, 0).wait_send()
        to_peer(o, 1).wait_send()
        return 0

    lax.fori_loop(1, RING, sent, 0)

    def sent_grad(j, _):
        h = slot(j)

        @pl.when(h != pos)
        def _():
            to_head(j, h).wait_send()

        return 0

    lax.fori_loop(0, RING, sent_grad, 0)

    def sent_far(s, _):
        @pl.when((line < ROW_LINES - 1) & (s >= RING // 2))
        def _():
            far(s).wait_send()

        @pl.when((lax.rem(line, 2) == 0) & (s < RING // 2))
        def _():
            far_long(s).wait_send()

        return 0

    lax.fori_loop(0, RING, sent_far, 0)
    to_mate.wait_send()
    for o in range(1, ROW_LINES):
        along_y(o).wait_send()
    for step in range(2):
        for kind in range(2):
            for way in range(2):
                along_x(step, kind, way).wait_send()
    for j in range(1, 8):
        to_core(j).wait_send()


VM = pl.BlockSpec(memory_space=pltpu.VMEM)
SM = pl.BlockSpec(memory_space=pltpu.SMEM)
DMA = pltpu.SemaphoreType.DMA
BF = jnp.bfloat16


def shaped(*dims, dtype=BF):
    return jax.ShapeDtypeStruct(dims, dtype)


def shards(q, k, v, grad_mixed, out_weight, head_phase, segments_short, segments_long):
    me = lax.axis_index("seq")
    line, pos = me // RING, lax.rem(me, RING)
    f32, i32 = jnp.float32, jnp.int32
    gq, gk, gv = pl.pallas_call(
        layer,
        out_shape=(shaped(TOK, HEADS * HS),) * 3,
        in_specs=[SM, SM, SM, VM, VM, VM, VM, VM],
        out_specs=(VM,) * 3,
        scratch_shapes=[
            pltpu.VMEM((RING, 3, ROWS, HS), BF),
            pltpu.VMEM((RING, ROWS, HS), BF),
            pltpu.VMEM((HEADS, HS, grad_mixed.shape[2]), BF),
            pltpu.VMEM((RING, ROWS, HS), BF),
            pltpu.VMEM((2 * RING, 2, ROWS, HS), BF),
            pltpu.VMEM((RING, ROWS, HS), BF),
            pltpu.VMEM((2 * RING, 2, HS, ROWS), BF),
            pltpu.VMEM((2 * PAIRS, 2, ROWS, HS), BF),
            pltpu.VMEM((PAIRS, 2, HS, 2 * ROWS), BF),
            pltpu.VMEM((PAIRS, 2, ROWS, HS), BF),
            pltpu.VMEM((2, ROWS, LROWS), i32),
            pltpu.VMEM((RING + PAIRS, 8, ROWS), i32),
            pltpu.VMEM((NEAR, ROWS, ROWS), f32),
            pltpu.VMEM((RING, NEAR, ROWS, ROWS), BF),
            pltpu.VMEM((PAIRS, 2 * PAIRS, ROWS, ROWS), BF),
            pltpu.VMEM((RING, HS, ROWS), f32),
            pltpu.VMEM((PAIRS, PAIRS, HS, ROWS), f32),
            pltpu.VMEM((STATS, 8, ROWS), f32),
            pltpu.VMEM((RING + PAIRS, 8, ROWS), f32),
            pltpu.VMEM((2 * RING, 2, ROWS, HS), f32),
            pltpu.VMEM((RING, HS, ROWS), f32),
            pltpu.VMEM((RING, 2, ROWS, HS), BF),
            pltpu.VMEM((RING, 2, ROWS, HS), BF),
            pltpu.VMEM((RING, ROWS, HS), BF),
            pltpu.VMEM((RING, 2, ROWS, HS), BF),
            pltpu.VMEM((RING, ROWS, HS), BF),
            pltpu.VMEM((RING, 2, ROWS, HS), BF),
            DMA((2, RING)),
            DMA((2, RING)),
            DMA((RING,)),
            DMA((RING,)),
            DMA((RING,)),
            DMA((RING,)),
            DMA,
            DMA,
            DMA((ROW_LINES,)),
            DMA((ROW_LINES,)),
            DMA((2, 2, 2)),
            DMA((2, 2, 2)),
            DMA((RING,)),
            DMA((RING,)),
            DMA((2, RING)),
            DMA((2, RING)),
            DMA((RING,)),
            DMA((RING,)),
        ],
        compiler_params=pltpu.CompilerParams(
            collective_id=0, has_side_effects=True, vmem_limit_bytes=VMEM_LIMIT
        ),
        name="layer",
    )(
        head_phase,
        segments_short,
        segments_long,
        q[0],
        k[0],
        v[0],
        grad_mixed[0],
        out_weight,
    )
    return gq[None], gk[None], gv[None]


def solution(mesh):
    placed = (
        P("fsdp", "seq", None),
        P("fsdp", "seq", None),
        P("fsdp", "seq", None),
        P("fsdp", "seq", None),
        P("fsdp", None),
        P(),
        P(),
        P(),
    )
    return jax.shard_map(
        shards,
        mesh=mesh,
        in_specs=placed,
        out_specs=(P("fsdp", "seq", None), P("fsdp", "seq", None), P("fsdp", "seq", None)),
        check_vma=False,
    )
```

```python
import functools
import math

import jax
import jax.numpy as jnp
from jax import lax
from jax.experimental import pallas as pl
from jax.experimental.pallas import tpu as pltpu
from jax.sharding import PartitionSpec as P

HEADS = 8
HS = 128
TOK = 512
ROWS = 256
LROWS = 128
RING = 8
ROW_LINES = 4
XS = 4
PAIRS = 4
NEAR = 5
STATS = RING + PAIRS * PAIRS
NEG = -1e30
SCALE = 1.0 / math.sqrt(HS)
EXP_SCALE = SCALE * math.log2(math.e)
NT = (((1,), (1,)), ((), ()))
NN = (((1,), (0,)), ((), ()))
TN = (((0,), (0,)), ((), ()))
VMEM_LIMIT = 60 * 1024 * 1024


def dot(a, b, dims):
    return lax.dot_general(a, b, dims, preferred_element_type=jnp.float32)


def token_of(row, phase):
    other = jnp.where(phase < 2, phase + 2, phase - 2)
    return 4 * (row & (LROWS - 1)) + jnp.where(row < LROWS, phase, other)


def pick_matrix(phase):
    row = lax.broadcasted_iota(jnp.int32, (ROWS, TOK), 0)
    tok = lax.broadcasted_iota(jnp.int32, (ROWS, TOK), 1)
    return (tok == token_of(row, phase)).astype(jnp.float32).astype(jnp.bfloat16)


def spread_matrix(phase):
    row = lax.broadcasted_iota(jnp.int32, (TOK, ROWS), 1)
    tok = lax.broadcasted_iota(jnp.int32, (TOK, ROWS), 0)
    return (tok == token_of(row, phase)).astype(jnp.float32).astype(jnp.bfloat16)


def place():
    me = lax.axis_index("seq")
    return me, me // RING, lax.rem(me, RING)


def greet(line, pos, columns, gather):
    barrier = pltpu.get_barrier_semaphore()
    for o in range(1, RING):
        pl.semaphore_signal(
            barrier, inc=1, device_id={"seq": line * RING + lax.rem(pos + o, RING)}
        )
    for o in columns:
        pl.semaphore_signal(
            barrier, inc=1, device_id={"seq": lax.rem(line + o, ROW_LINES) * RING + pos}
        )
    total = RING - 1 + len(columns)
    if gather:
        f = lax.axis_index("fsdp")
        x, hi = f // 2, lax.rem(f, 2)
        pl.semaphore_signal(barrier, inc=1, device_id={"fsdp": 2 * x + 1 - hi})
        for o in range(1, XS):
            pl.semaphore_signal(barrier, inc=1, device_id={"fsdp": 2 * lax.rem(x + o, XS) + hi})
        total += XS
    pl.semaphore_wait(barrier, total)


def layer(
    phase_ref,
    short_ref,
    long_ref,
    q_ref,
    k_ref,
    v_ref,
    g_ref,
    w_ref,
    got_q,
    got_kv,
    stage,
    gstage,
    w_all,
    qo_ref,
    kvo_ref,
    do_ref,
    kt_ref,
    lkv_ref,
    lkt_ref,
    lq_ref,
    off_ref,
    rows_ref,
    s_ref,
    p_ref,
    lp_ref,
    o_ref,
    lo_ref,
    st_ref,
    delta_ref,
    acc,
    dq_acc,
    far_stage,
    near,
    dq_stage,
    kv_stage,
    send_sem,
    recv_sem,
    hsend,
    hrecv,
    gsend,
    grecv,
    zsend,
    zrecv,
    ysend,
    yrecv,
    xsend,
    xrecv,
    csend,
    crecv,
    bsend,
    brecv,
    fsend,
    frecv,
):
    me, line, pos = place()
    core = lax.rem(me, 2)
    f = lax.axis_index("fsdp")
    x, hi = f // 2, lax.rem(f, 2)
    mate = 2 * x + 1 - hi
    greet(line, pos, (1, 2, 3), True)
    half = pl.ds(pl.multiple_of(core * 64, 64), 64)
    piece = pl.ds(pl.multiple_of(core * 64 + line * 16, 16), 16)

    to_mate = pltpu.make_async_remote_copy(
        src_ref=w_ref.at[piece],
        dst_ref=w_all.at[f, piece],
        send_sem=zsend,
        recv_sem=zrecv,
        device_id={"fsdp": mate},
    )

    def along_y(o):
        return pltpu.make_async_remote_copy(
            src_ref=w_all.at[mate, piece],
            dst_ref=w_all.at[mate, piece],
            send_sem=ysend.at[o],
            recv_sem=yrecv.at[o],
            device_id={"seq": lax.rem(line + o, ROW_LINES) * RING + pos},
        )

    def along_x(step, kind, way):
        hop = 1 if way == 0 else XS - 1
        if step == 0:
            at = f if kind == 0 else mate
            rows = half
            src = w_ref.at[half] if kind == 0 else w_all.at[mate, half]
        else:
            at = 2 * lax.rem(x + XS - hop, XS) + (hi if kind == 0 else 1 - hi)
            rows = pl.ds(pl.multiple_of(core * 64 + way * 32, 32), 32)
            src = w_all.at[at, rows]
        return pltpu.make_async_remote_copy(
            src_ref=src,
            dst_ref=w_all.at[at, rows],
            send_sem=xsend.at[step, kind, way],
            recv_sem=xrecv.at[step, kind, way],
            device_id={"fsdp": 2 * lax.rem(x + hop, XS) + hi},
        )

    def slot(j):
        m = jnp.maximum(j - 2, 0)
        r = lax.rem(m, 3)
        hop = jnp.where(r == 0, XS - 1, r)
        other = 2 * lax.rem(x + hop, XS) + jnp.where(m < 3, hi, 1 - hi)
        return jnp.where(j == 0, f, jnp.where(j == 1, mate, other))

    def to_core(j):
        return pltpu.make_async_remote_copy(
            src_ref=w_all.at[slot(j), half],
            dst_ref=w_all.at[slot(j), half],
            send_sem=csend.at[j],
            recv_sem=crecv.at[j],
            device_id={"seq": me + 1 - 2 * core},
        )

    to_mate.start()
    for way in range(2):
        along_x(0, 0, way).start()

    def pass_on(kind):
        for way in range(2):
            along_x(0, kind, way).wait_recv()
            along_x(1, kind, way).start()
            to_core(2 + 3 * kind + way).start()

    def passed(kind):
        for way in range(2):
            along_x(1, kind, way).wait_recv()
        to_core(4 + 3 * kind).start()

    def packed(h):
        pick = pick_matrix(phase_ref[h])
        cols = pl.ds(pl.multiple_of(h * HS, HS), HS)
        return [dot(pick, ref[:, cols], NN).astype(jnp.bfloat16) for ref in (q_ref, k_ref, v_ref)]

    def to_peer(o, what):
        peer = line * RING + lax.rem(pos + o, RING)
        if what == 0:
            src, dst = stage.at[o, 0], qo_ref.at[pos]
        else:
            src, dst = stage.at[o, pl.ds(1, 2)], kvo_ref.at[RING + pos]
        return pltpu.make_async_remote_copy(
            src_ref=src,
            dst_ref=dst,
            send_sem=send_sem.at[what, o],
            recv_sem=recv_sem.at[what, o],
            device_id={"seq": peer},
        )

    def far(s):
        return pltpu.make_async_remote_copy(
            src_ref=kvo_ref.at[RING + s],
            dst_ref=kvo_ref.at[s],
            send_sem=hsend.at[s],
            recv_sem=hrecv.at[s],
            device_id={"seq": me + RING},
        )

    def far_long(s):
        return pltpu.make_async_remote_copy(
            src_ref=kvo_ref.at[RING + s, :, pl.ds(0, LROWS)],
            dst_ref=kvo_ref.at[s, :, pl.ds(0, LROWS)],
            send_sem=hsend.at[s],
            recv_sem=hrecv.at[s],
            device_id={"seq": me + RING},
        )

    def start(o, _):
        for i, rows in enumerate(packed(lax.rem(pos + o, RING))):
            stage[o, i] = rows
        to_peer(o, 1).start()
        return 0

    lax.fori_loop(1, RING, start, 0)

    def start_query(o, _):
        to_peer(o, 0).start()
        return 0


    to_mate.wait_recv()
    for o in range(1, ROW_LINES):
        along_y(o).start()
    pass_on(0)
    own = packed(pos)
    qo_ref[pos] = own[0]
    kvo_ref[RING + pos, 0] = own[1]
    kvo_ref[RING + pos, 1] = own[2]
    w_all[f] = w_ref[...]
    for o in range(1, ROW_LINES):
        along_y(o).wait_recv()
    for way in range(2):
        along_x(0, 1, way).start()
    to_core(1).start()

    def to_head(j, h):
        return pltpu.make_async_remote_copy(
            src_ref=gstage.at[j],
            dst_ref=do_ref.at[pos],
            send_sem=gsend.at[j],
            recv_sem=grecv.at[pos],
            device_id={"seq": line * RING + h},
        )

    def grad_head(j, _):
        h = slot(j)

        @pl.when(j == 1)
        def _():
            passed(0)

        @pl.when(j == 2)
        def _():
            pass_on(1)
            lax.fori_loop(1, RING, start_query, 0)

        @pl.when(j == 4)
        def _():
            passed(1)

        @pl.when(j >= 1)
        def _():
            to_core(j).wait_recv()

        full = dot(g_ref[...], w_all[h], NT).astype(jnp.bfloat16)
        rows = dot(pick_matrix(phase_ref[h]), full, NN).astype(jnp.bfloat16)

        @pl.when(h == pos)
        def _():
            do_ref[pos] = rows

        @pl.when(h != pos)
        def _():
            gstage[j] = rows

        return 0

    lax.fori_loop(0, RING, grad_head, 0)

    def start_grad(j, _):
        h = slot(j)

        @pl.when(h != pos)
        def _():
            to_head(j, h).start()

        return 0

    lax.fori_loop(0, RING, start_grad, 0)

    def forward(o, _):
        s = lax.rem(pos + RING - o, RING)

        @pl.when(o > 0)
        def _():
            to_peer(o, 1).wait_recv()

        @pl.when((line < ROW_LINES - 1) & (s >= RING // 2))
        def _():
            far(s).start()

        @pl.when((lax.rem(line, 2) == 0) & (s < RING // 2))
        def _():
            far_long(s).start()

        return 0

    lax.fori_loop(0, RING, forward, 0)


    phase = phase_ref[pos]
    odd = lax.rem(line, 2)
    origin = (line - 1) * (RING * TOK)
    row = lax.broadcasted_iota(jnp.int32, (ROWS, LROWS), 0)
    off_ref[0] = token_of(row, phase)
    off_ref[1] = (row // LROWS) * TOK + 4 * (row & (LROWS - 1)) + phase

    def low_of(tok, lengths, count):
        low = jnp.full_like(tok, -origin)
        end = -origin
        for n in range(count):
            end = end + lengths[n]
            low = jnp.where(tok >= end, jnp.maximum(low, end), low)
        return low

    lane = lax.broadcasted_iota(jnp.int32, (1, ROWS), 1)
    query_off = token_of(lane, phase)
    pair_off = (lane // LROWS) * TOK + 4 * (lane & (LROWS - 1)) + phase

    def prepare_query(i, _):
        tok = (RING + i) * TOK + query_off
        rows_ref[i, pl.ds(0, 1), :] = tok
        rows_ref[i, pl.ds(1, 1), :] = low_of(tok, short_ref, short_ref.shape[0])
        return 0

    lax.fori_loop(0, RING, prepare_query, 0)

    def prepare_pair(ii, _):
        tok = (RING + 2 * ii) * TOK + pair_off
        rows_ref[RING + ii, pl.ds(0, 1), :] = tok
        rows_ref[RING + ii, pl.ds(1, 1), :] = low_of(tok, long_ref, long_ref.shape[0])
        return 0

    lax.fori_loop(0, PAIRS, prepare_pair, 0)

    st_ref[:, pl.ds(0, 1), :] = jnp.full((STATS, 1, ROWS), NEG, jnp.float32)
    st_ref[:, pl.ds(1, 3), :] = jnp.zeros((STATS, 3, ROWS), jnp.float32)
    acc[...] = jnp.zeros_like(acc)
    dq_acc[...] = jnp.zeros_like(dq_acc)
    lo_ref[...] = jnp.zeros_like(lo_ref)

    @pl.when(line == 0)
    def _():
        kvo_ref[pl.ds(0, RING)] = jnp.zeros((RING, 2, ROWS, HS), jnp.bfloat16)

    def got_query(o, _):
        to_peer(o, 0).wait_recv()
        return 0

    lax.fori_loop(1, RING, got_query, 0)

    def prepare_key(g, _):
        kt_ref[g, 0] = kvo_ref[g, 0].T
        kt_ref[g, 1] = kvo_ref[g, 1].T
        return 0

    def prepare_key_pair(kp, _):
        for e in range(2):
            for w in range(2):
                lkv_ref[kp, w, pl.ds(e * LROWS, LROWS), :] = kvo_ref[
                    2 * kp + e, w, pl.ds(0, LROWS), :
                ]
        cols = pl.ds(pl.multiple_of(lax.rem(kp, 2) * ROWS, ROWS), ROWS)
        lkt_ref[kp // 2, 0, :, cols] = lkv_ref[kp, 0].T
        lkt_ref[kp // 2, 1, :, cols] = lkv_ref[kp, 1].T
        return 0

    def prepare_long_query(ii, _):
        for e in range(2):
            lq_ref[ii, 0, pl.ds(e * LROWS, LROWS), :] = qo_ref[2 * ii + e, pl.ds(0, LROWS), :]
        return 0

    lax.fori_loop(0, PAIRS, prepare_long_query, 0)
    lax.fori_loop(RING, 2 * RING, prepare_key, 0)
    lax.fori_loop(PAIRS, 2 * PAIRS, prepare_key_pair, 0)

    def strip(i, _):
        tok = rows_ref[i, pl.ds(0, 1), :]
        low = rows_ref[i, pl.ds(1, 1), :]
        q = qo_ref[i]
        off = jnp.concatenate([off_ref[0], off_ref[0]], axis=1)
        tops = []
        for d in range(NEAR):
            g = RING + i - d
            s = dot(kvo_ref[g, 0], q, NT)
            live = off >= low - g * TOK
            if d == 0:
                live = live & (off <= tok - g * TOK)
            s = jnp.where(live, s, NEG)
            s_ref[d] = s
            tops.append(jnp.max(s, axis=0, keepdims=True))
        m = functools.reduce(jnp.maximum, tops)
        l, o = jnp.zeros((1, ROWS), jnp.float32), jnp.zeros((HS, ROWS), jnp.float32)
        for d in range(NEAR):
            p = jnp.exp2((s_ref[d] - m) * EXP_SCALE)
            l = l + jnp.sum(p, axis=0, keepdims=True)
            w = p.astype(jnp.bfloat16)
            p_ref[i, d] = w
            o = o + dot(kt_ref[RING + i - d, 1], w, NN)
        st_ref[i, pl.ds(0, 1), :] = m
        st_ref[i, pl.ds(1, 1), :] = l
        o_ref[i] = o
        return 0

    def chunk(ii, c):
        tok = rows_ref[RING + ii, pl.ds(0, 1), :]
        low = rows_ref[RING + ii, pl.ds(1, 1), :]
        q = lq_ref[ii, 0]
        off = jnp.concatenate([off_ref[1], off_ref[1]], axis=1)
        scores = []
        for e in range(2):
            kp = 2 * c + e
            s = dot(lkv_ref[kp, 0], q, NT)
            at = kp * (2 * TOK)
            scores.append(jnp.where((off >= low - at) & (off <= tok - at), s, NEG))
        m = jnp.maximum(*[jnp.max(s, axis=0, keepdims=True) for s in scores])
        l = jnp.zeros((1, ROWS), jnp.float32)
        parts = []
        for e in range(2):
            p = jnp.exp2((scores[e] - m) * EXP_SCALE)
            l = l + jnp.sum(p, axis=0, keepdims=True)
            w = p.astype(jnp.bfloat16)
            lp_ref[ii, 2 * c + e] = w
            parts.append(w)
        t = RING + ii * PAIRS + c
        st_ref[t, pl.ds(0, 1), :] = m
        st_ref[t, pl.ds(1, 1), :] = l
        lo_ref[ii, c] = dot(lkt_ref[c, 1], jnp.concatenate(parts, axis=0), NN)

    def own_chunks(ii, _):
        chunk(ii, 2)

        @pl.when(ii >= 2)
        def _():
            chunk(ii, 3)

        return 0

    lax.fori_loop(0, PAIRS, own_chunks, 0)
    lax.fori_loop(RING // 2, RING, strip, 0)

    def got_far(s, _):
        @pl.when((line > 0) & (s >= RING // 2))
        def _():
            far(s).wait_recv()

        @pl.when((odd == 1) & (s < RING // 2))
        def _():
            far_long(s).wait_recv()

        return 0

    lax.fori_loop(0, RING, got_far, 0)
    lax.fori_loop(RING // 2, RING, prepare_key, 0)
    lax.fori_loop(0, RING // 2, strip, 0)

    @pl.when(odd == 1)
    def _():
        lax.fori_loop(0, PAIRS, prepare_key_pair, 0)

        def far_chunks(n, _):
            chunk(n // 2, lax.rem(n, 2))
            return 0

        lax.fori_loop(0, 2 * PAIRS, far_chunks, 0)

    def got_grad(j, _):
        @pl.when(j != pos)
        def _():
            pltpu.make_async_remote_copy(
                src_ref=gstage.at[j],
                dst_ref=do_ref.at[j],
                send_sem=gsend.at[j],
                recv_sem=grecv.at[j],
                device_id={"seq": line * RING + lax.rem(pos + 1, RING)},
            ).wait_recv()

        return 0

    lax.fori_loop(0, RING, got_grad, 0)

    def join(ii, _):
        base = RING + ii * PAIRS
        lst = [st_ref[base + c] for c in range(PAIRS)]
        tops, invs, deltas = [], [], []
        for e in range(2):
            i = 2 * ii + e
            lq_ref[ii, 1, pl.ds(e * LROWS, LROWS), :] = do_ref[i, pl.ds(0, LROWS), :]
            here = slice(e * LROWS, (e + 1) * LROWS)
            m = st_ref[i, pl.ds(0, 1), :]
            ml = functools.reduce(jnp.maximum, [a[0:1, here] for a in lst], m[:, :LROWS])
            w = jnp.exp2((m - jnp.concatenate([ml, m[:, LROWS:]], axis=1)) * EXP_SCALE)
            wl = [jnp.exp2((a[0:1, here] - ml) * EXP_SCALE) for a in lst]
            l = w * st_ref[i, pl.ds(1, 1), :]
            ll = sum((x * a[1:2, here] for x, a in zip(wl, lst)), l[:, :LROWS])
            inv = 1.0 / jnp.concatenate([ll, l[:, LROWS:]], axis=1)
            o = o_ref[i] * w
            ol = o[:, :LROWS]
            for c in range(PAIRS):
                ol = ol + lo_ref[ii, c, :, here] * wl[c]
            o = jnp.concatenate([ol, o[:, LROWS:]], axis=1)
            gt = do_ref[i].T.astype(jnp.float32)
            delta = jnp.sum(gt * (o * inv), axis=0, keepdims=True)
            delta_ref[i, pl.ds(0, 1), :] = delta
            st_ref[i, pl.ds(3, 1), :] = w * inv
            tops.append(ml)
            invs.append(inv[:, :LROWS])
            deltas.append(delta[:, :LROWS])
        ml = jnp.concatenate(tops, axis=1)
        il = jnp.concatenate(invs, axis=1)
        delta_ref[RING + ii, pl.ds(0, 1), :] = jnp.concatenate(deltas, axis=1)
        for c in range(PAIRS):
            st_ref[base + c, pl.ds(3, 1), :] = jnp.exp2((lst[c][0:1] - ml) * EXP_SCALE) * il
        return 0

    lax.fori_loop(0, PAIRS, join, 0)

    def back(weights, scales, deltas, v, kt, q, do):
        dp = dot(v, do, NT)
        pbs, dss = [], []
        for u, (w, a, delta) in enumerate(zip(weights, scales, deltas)):
            pr = w.astype(jnp.float32) * a
            dss.append((pr * (dp[:, u * ROWS : (u + 1) * ROWS] - delta)).astype(jnp.bfloat16))
            pbs.append(pr.astype(jnp.bfloat16))
        ds = jnp.concatenate(dss, axis=1)
        pb = jnp.concatenate(pbs, axis=1)
        return dot(ds, q, NN), dot(pb, do, NN), dot(kt, ds, NN)

    def back_pair(kp, first, count):
        cols = pl.ds(pl.multiple_of(lax.rem(kp, 2) * ROWS, ROWS), ROWS)
        dk, dv, dq = back(
            [lp_ref[first + u, kp] for u in range(count)],
            [
                st_ref[RING + (first + u) * PAIRS + kp // 2, pl.ds(3, 1), :]
                for u in range(count)
            ],
            [delta_ref[RING + first + u, pl.ds(0, 1), :] for u in range(count)],
            lkv_ref[kp, 1],
            lkt_ref[kp // 2, 0, :, cols],
            lq_ref[pl.ds(first, count), 0].reshape(count * ROWS, HS),
            lq_ref[pl.ds(first, count), 1].reshape(count * ROWS, HS),
        )
        for e in range(2):
            part = slice(e * LROWS, (e + 1) * LROWS)
            acc[2 * kp + e, 0, pl.ds(0, LROWS), :] += dk[part]
            acc[2 * kp + e, 1, pl.ds(0, LROWS), :] += dv[part]
        for u in range(count):
            for e in range(2):
                at = u * ROWS + e * LROWS
                dq_acc[2 * (first + u) + e, :, pl.ds(0, LROWS)] += dq[:, at : at + LROWS]

    def back_block(g, first, count):
        d = RING + first - g
        dk, dv, dq = back(
            [p_ref[first + u, d + u] for u in range(count)],
            [st_ref[first + u, pl.ds(3, 1), :] for u in range(count)],
            [delta_ref[first + u, pl.ds(0, 1), :] for u in range(count)],
            kvo_ref[g, 1],
            kt_ref[g, 0],
            qo_ref[pl.ds(first, count)].reshape(count * ROWS, HS),
            do_ref[pl.ds(first, count)].reshape(count * ROWS, HS),
        )
        acc[g, 0] += dk
        acc[g, 1] += dv
        for u in range(count):
            dq_acc[first + u] += dq[:, u * ROWS : (u + 1) * ROWS]

    def give(s):
        return pltpu.make_async_remote_copy(
            src_ref=far_stage.at[s],
            dst_ref=near.at[s],
            send_sem=fsend.at[s],
            recv_sem=frecv.at[s],
            device_id={"seq": me - RING},
        )

    def give_long(s):
        return pltpu.make_async_remote_copy(
            src_ref=far_stage.at[s, :, pl.ds(0, LROWS)],
            dst_ref=near.at[s, :, pl.ds(0, LROWS)],
            send_sem=fsend.at[s],
            recv_sem=frecv.at[s],
            device_id={"seq": me - RING},
        )

    def home(s, what):
        if what == 0:
            src, dst = dq_stage.at[s], got_q.at[pos]
        else:
            src, dst = kv_stage.at[s], got_kv.at[pos]
        return pltpu.make_async_remote_copy(
            src_ref=src,
            dst_ref=dst,
            send_sem=bsend.at[what, s],
            recv_sem=brecv.at[what, pos],
            device_id={"seq": line * RING + s},
        )

    def landed(s, what):
        dst = got_q.at[s] if what == 0 else got_kv.at[s]
        src = dq_stage.at[s] if what == 0 else kv_stage.at[s]
        return pltpu.make_async_remote_copy(
            src_ref=src,
            dst_ref=dst,
            send_sem=bsend.at[what, s],
            recv_sem=brecv.at[what, s],
            device_id={"seq": line * RING + lax.rem(pos + 1, RING)},
        )

    def emit_far(g):
        far_stage[g, 0] = (acc[g, 0] * SCALE).astype(jnp.bfloat16)
        far_stage[g, 1] = acc[g, 1].astype(jnp.bfloat16)

    @pl.when(odd == 1)
    def _():
        def far_pair(kp, _):
            back_pair(kp, 0, PAIRS)

            @pl.when(kp < PAIRS // 2)
            def _():
                for e in range(2):
                    emit_far(2 * kp + e)
                    give_long(2 * kp + e).start()

            return 0

        lax.fori_loop(0, PAIRS, far_pair, 0)

    @pl.when(line > 0)
    def _():
        for g in range(RING // 2, RING):
            back_block(g, 0, g - (RING - NEAR))
            emit_far(g)
            give(g).start()

    def joined(b):
        full = (line < ROW_LINES - 1) & (b >= RING // 2)
        half = (odd == 0) & (b < RING // 2)
        return full, half

    def own_block(b, count):
        back_block(RING + b, b, count)
        dq_stage[b] = (dq_acc[b].T * SCALE).astype(jnp.bfloat16)

        @pl.when(b != pos)
        def _():
            home(b, 0).start()

        full, half = joined(b)

        @pl.when(jnp.logical_not(full | half))
        def _():
            kv_stage[b, 0] = (acc[RING + b, 0] * SCALE).astype(jnp.bfloat16)
            kv_stage[b, 1] = acc[RING + b, 1].astype(jnp.bfloat16)

            @pl.when(b != pos)
            def _():
                home(b, 1).start()

    def own_block_near(b, _):
        own_block(b, NEAR)
        return 0

    for kp in range(PAIRS):
        back_pair(PAIRS + kp, kp, PAIRS - kp)
        if 2 * kp + NEAR < RING:
            lax.fori_loop(2 * kp, 2 * kp + 2, own_block_near, 0)
        else:
            for e in range(2):
                own_block(2 * kp + e, RING - 2 * kp - e)

    def add_near(b, _):
        full, half = joined(b)

        @pl.when(full)
        def _():
            give(b).wait_recv()

        @pl.when(half)
        def _():
            give_long(b).wait_recv()
            near[b, :, pl.ds(LROWS, LROWS)] = jnp.zeros((2, LROWS, HS), jnp.bfloat16)

        @pl.when(full | half)
        def _():
            kv_stage[b, 0] = (acc[RING + b, 0] * SCALE + near[b, 0].astype(jnp.float32)).astype(
                jnp.bfloat16
            )
            kv_stage[b, 1] = (acc[RING + b, 1] + near[b, 1].astype(jnp.float32)).astype(
                jnp.bfloat16
            )

            @pl.when(b != pos)
            def _():
                home(b, 1).start()

        return 0

    lax.fori_loop(0, RING, add_near, 0)
    got_q[pos] = dq_stage[pos]
    got_kv[pos] = kv_stage[pos]

    def arrived(o, _):
        h = lax.rem(pos + RING - o, RING)
        landed(h, 0).wait_recv()
        landed(h, 1).wait_recv()
        return 0

    lax.fori_loop(1, RING, arrived, 0)

    def finish(o, _):
        s = lax.rem(pos + o, RING)
        home(s, 0).wait_send()
        home(s, 1).wait_send()
        return 0

    lax.fori_loop(1, RING, finish, 0)

    def finish_far(s, _):
        @pl.when((line > 0) & (s >= RING // 2))
        def _():
            give(s).wait_send()

        @pl.when((odd == 1) & (s < RING // 2))
        def _():
            give_long(s).wait_send()

        return 0

    lax.fori_loop(0, RING, finish_far, 0)

    def sent(o, _):
        to_peer(o, 0).wait_send()
        to_peer(o, 1).wait_send()
        return 0

    lax.fori_loop(1, RING, sent, 0)

    def sent_grad(j, _):
        h = slot(j)

        @pl.when(h != pos)
        def _():
            to_head(j, h).wait_send()

        return 0

    lax.fori_loop(0, RING, sent_grad, 0)

    def sent_far(s, _):
        @pl.when((line < ROW_LINES - 1) & (s >= RING // 2))
        def _():
            far(s).wait_send()

        @pl.when((lax.rem(line, 2) == 0) & (s < RING // 2))
        def _():
            far_long(s).wait_send()

        return 0

    lax.fori_loop(0, RING, sent_far, 0)
    to_mate.wait_send()
    for o in range(1, ROW_LINES):
        along_y(o).wait_send()
    for step in range(2):
        for kind in range(2):
            for way in range(2):
                along_x(step, kind, way).wait_send()
    for j in range(1, 8):
        to_core(j).wait_send()


def spread(phase_ref, q_ref, kv_ref, gq_ref, gk_ref, gv_ref):
    put = spread_matrix(phase_ref[pl.program_id(0)])
    gq_ref[...] = dot(put, q_ref[0], NN).astype(jnp.bfloat16)
    gk_ref[...] = dot(put, kv_ref[0, 0], NN).astype(jnp.bfloat16)
    gv_ref[...] = dot(put, kv_ref[0, 1], NN).astype(jnp.bfloat16)


VM = pl.BlockSpec(memory_space=pltpu.VMEM)
SM = pl.BlockSpec(memory_space=pltpu.SMEM)
DMA = pltpu.SemaphoreType.DMA
BF = jnp.bfloat16


def shaped(*dims, dtype=BF):
    return jax.ShapeDtypeStruct(dims, dtype)


def shards(q, k, v, grad_mixed, out_weight, head_phase, segments_short, segments_long):
    me = lax.axis_index("seq")
    line, pos = me // RING, lax.rem(me, RING)
    f32, i32 = jnp.float32, jnp.int32
    got_q, got_kv = pl.pallas_call(
        layer,
        out_shape=(shaped(RING, ROWS, HS), shaped(RING, 2, ROWS, HS)),
        in_specs=[SM, SM, SM, VM, VM, VM, VM, VM],
        out_specs=(VM, VM),
        scratch_shapes=[
            pltpu.VMEM((RING, 3, ROWS, HS), BF),
            pltpu.VMEM((RING, ROWS, HS), BF),
            pltpu.VMEM((HEADS, HS, grad_mixed.shape[2]), BF),
            pltpu.VMEM((RING, ROWS, HS), BF),
            pltpu.VMEM((2 * RING, 2, ROWS, HS), BF),
            pltpu.VMEM((RING, ROWS, HS), BF),
            pltpu.VMEM((2 * RING, 2, HS, ROWS), BF),
            pltpu.VMEM((2 * PAIRS, 2, ROWS, HS), BF),
            pltpu.VMEM((PAIRS, 2, HS, 2 * ROWS), BF),
            pltpu.VMEM((PAIRS, 2, ROWS, HS), BF),
            pltpu.VMEM((2, ROWS, LROWS), i32),
            pltpu.VMEM((RING + PAIRS, 8, ROWS), i32),
            pltpu.VMEM((NEAR, ROWS, ROWS), f32),
            pltpu.VMEM((RING, NEAR, ROWS, ROWS), BF),
            pltpu.VMEM((PAIRS, 2 * PAIRS, ROWS, ROWS), BF),
            pltpu.VMEM((RING, HS, ROWS), f32),
            pltpu.VMEM((PAIRS, PAIRS, HS, ROWS), f32),
            pltpu.VMEM((STATS, 8, ROWS), f32),
            pltpu.VMEM((RING + PAIRS, 8, ROWS), f32),
            pltpu.VMEM((2 * RING, 2, ROWS, HS), f32),
            pltpu.VMEM((RING, HS, ROWS), f32),
            pltpu.VMEM((RING, 2, ROWS, HS), BF),
            pltpu.VMEM((RING, 2, ROWS, HS), BF),
            pltpu.VMEM((RING, ROWS, HS), BF),
            pltpu.VMEM((RING, 2, ROWS, HS), BF),
            DMA((2, RING)),
            DMA((2, RING)),
            DMA((RING,)),
            DMA((RING,)),
            DMA((RING,)),
            DMA((RING,)),
            DMA,
            DMA,
            DMA((ROW_LINES,)),
            DMA((ROW_LINES,)),
            DMA((2, 2, 2)),
            DMA((2, 2, 2)),
            DMA((RING,)),
            DMA((RING,)),
            DMA((2, RING)),
            DMA((2, RING)),
            DMA((RING,)),
            DMA((RING,)),
        ],
        compiler_params=pltpu.CompilerParams(
            collective_id=0, has_side_effects=True, vmem_limit_bytes=VMEM_LIMIT
        ),
        name="layer",
    )(
        head_phase,
        segments_short,
        segments_long,
        q[0],
        k[0],
        v[0],
        grad_mixed[0],
        out_weight,
    )
    block = pl.BlockSpec((TOK, HS), lambda h: (0, h))
    gq, gk, gv = pl.pallas_call(
        spread,
        grid=(HEADS,),
        out_shape=(shaped(TOK, HEADS * HS),) * 3,
        in_specs=[
            SM,
            pl.BlockSpec((1, ROWS, HS), lambda h: (h, 0, 0)),
            pl.BlockSpec((1, 2, ROWS, HS), lambda h: (h, 0, 0, 0)),
        ],
        out_specs=(block,) * 3,
        name="spread",
    )(head_phase, got_q, got_kv)
    return gq[None], gk[None], gv[None]


def solution(mesh):
    placed = (
        P("fsdp", "seq", None),
        P("fsdp", "seq", None),
        P("fsdp", "seq", None),
        P("fsdp", "seq", None),
        P("fsdp", None),
        P(),
        P(),
        P(),
    )
    return jax.shard_map(
        shards,
        mesh=mesh,
        in_specs=placed,
        out_specs=(P("fsdp", "seq", None), P("fsdp", "seq", None), P("fsdp", "seq", None)),
        check_vma=False,
    )
```

```python
import functools
import math

import jax
import jax.numpy as jnp
from jax import lax
from jax.experimental import pallas as pl
from jax.experimental.pallas import tpu as pltpu
from jax.sharding import PartitionSpec as P

HEADS = 8
HS = 128
TOK = 512
ROWS = 256
LROWS = 128
RING = 8
ROW_LINES = 4
XS = 4
PAIRS = 4
NEAR = 5
STATS = RING + PAIRS * PAIRS
NEG = -1e30
SCALE = 1.0 / math.sqrt(HS)
EXP_SCALE = SCALE * math.log2(math.e)
NT = (((1,), (1,)), ((), ()))
NN = (((1,), (0,)), ((), ()))
TN = (((0,), (0,)), ((), ()))
VMEM_LIMIT = 60 * 1024 * 1024


def dot(a, b, dims):
    return lax.dot_general(a, b, dims, preferred_element_type=jnp.float32)


def token_of(row, phase):
    other = jnp.where(phase < 2, phase + 2, phase - 2)
    return 4 * (row & (LROWS - 1)) + jnp.where(row < LROWS, phase, other)


def pick_matrix(phase):
    row = lax.broadcasted_iota(jnp.int32, (ROWS, TOK), 0)
    tok = lax.broadcasted_iota(jnp.int32, (ROWS, TOK), 1)
    return (tok == token_of(row, phase)).astype(jnp.float32).astype(jnp.bfloat16)


def spread_matrix(phase):
    row = lax.broadcasted_iota(jnp.int32, (TOK, ROWS), 1)
    tok = lax.broadcasted_iota(jnp.int32, (TOK, ROWS), 0)
    return (tok == token_of(row, phase)).astype(jnp.float32).astype(jnp.bfloat16)


def place():
    me = lax.axis_index("seq")
    return me, me // RING, lax.rem(me, RING)


def greet(line, pos, columns, gather):
    barrier = pltpu.get_barrier_semaphore()
    for o in range(1, RING):
        pl.semaphore_signal(
            barrier, inc=1, device_id={"seq": line * RING + lax.rem(pos + o, RING)}
        )
    for o in columns:
        pl.semaphore_signal(
            barrier, inc=1, device_id={"seq": lax.rem(line + o, ROW_LINES) * RING + pos}
        )
    total = RING - 1 + len(columns)
    if gather:
        f = lax.axis_index("fsdp")
        x, hi = f // 2, lax.rem(f, 2)
        pl.semaphore_signal(barrier, inc=1, device_id={"fsdp": 2 * x + 1 - hi})
        for o in range(1, XS):
            pl.semaphore_signal(barrier, inc=1, device_id={"fsdp": 2 * lax.rem(x + o, XS) + hi})
        total += XS
    pl.semaphore_wait(barrier, total)


def layer(
    phase_ref,
    short_ref,
    long_ref,
    q_ref,
    k_ref,
    v_ref,
    g_ref,
    w_ref,
    got_q,
    got_kv,
    stage,
    gstage,
    w_all,
    qo_ref,
    kvo_ref,
    do_ref,
    kt_ref,
    lkv_ref,
    lkt_ref,
    lq_ref,
    off_ref,
    rows_ref,
    s_ref,
    p_ref,
    lp_ref,
    o_ref,
    lo_ref,
    st_ref,
    delta_ref,
    acc,
    dq_acc,
    far_stage,
    near,
    dq_stage,
    kv_stage,
    send_sem,
    recv_sem,
    hsend,
    hrecv,
    gsend,
    grecv,
    zsend,
    zrecv,
    ysend,
    yrecv,
    xsend,
    xrecv,
    csend,
    crecv,
    bsend,
    brecv,
    fsend,
    frecv,
):
    me, line, pos = place()
    core = lax.rem(me, 2)
    f = lax.axis_index("fsdp")
    x, hi = f // 2, lax.rem(f, 2)
    mate = 2 * x + 1 - hi
    greet(line, pos, (1, 2, 3), True)
    half = pl.ds(pl.multiple_of(core * 64, 64), 64)
    piece = pl.ds(pl.multiple_of(core * 64 + line * 16, 16), 16)

    to_mate = pltpu.make_async_remote_copy(
        src_ref=w_ref.at[piece],
        dst_ref=w_all.at[f, piece],
        send_sem=zsend,
        recv_sem=zrecv,
        device_id={"fsdp": mate},
    )

    def along_y(o):
        return pltpu.make_async_remote_copy(
            src_ref=w_all.at[mate, piece],
            dst_ref=w_all.at[mate, piece],
            send_sem=ysend.at[o],
            recv_sem=yrecv.at[o],
            device_id={"seq": lax.rem(line + o, ROW_LINES) * RING + pos},
        )

    def along_x(step, kind, way):
        hop = 1 if way == 0 else XS - 1
        if step == 0:
            at = f if kind == 0 else mate
            rows = half
            src = w_ref.at[half] if kind == 0 else w_all.at[mate, half]
        else:
            at = 2 * lax.rem(x + XS - hop, XS) + (hi if kind == 0 else 1 - hi)
            rows = pl.ds(pl.multiple_of(core * 64 + way * 32, 32), 32)
            src = w_all.at[at, rows]
        return pltpu.make_async_remote_copy(
            src_ref=src,
            dst_ref=w_all.at[at, rows],
            send_sem=xsend.at[step, kind, way],
            recv_sem=xrecv.at[step, kind, way],
            device_id={"fsdp": 2 * lax.rem(x + hop, XS) + hi},
        )

    def slot(j):
        m = jnp.maximum(j - 2, 0)
        r = lax.rem(m, 3)
        hop = jnp.where(r == 0, XS - 1, r)
        other = 2 * lax.rem(x + hop, XS) + jnp.where(m < 3, hi, 1 - hi)
        return jnp.where(j == 0, f, jnp.where(j == 1, mate, other))

    def to_core(j):
        return pltpu.make_async_remote_copy(
            src_ref=w_all.at[slot(j), half],
            dst_ref=w_all.at[slot(j), half],
            send_sem=csend.at[j],
            recv_sem=crecv.at[j],
            device_id={"seq": me + 1 - 2 * core},
        )

    to_mate.start()
    for way in range(2):
        along_x(0, 0, way).start()

    def pass_on(kind):
        for way in range(2):
            along_x(0, kind, way).wait_recv()
            along_x(1, kind, way).start()
            to_core(2 + 3 * kind + way).start()

    def passed(kind):
        for way in range(2):
            along_x(1, kind, way).wait_recv()
        to_core(4 + 3 * kind).start()

    def packed(h):
        pick = pick_matrix(phase_ref[h])
        cols = pl.ds(pl.multiple_of(h * HS, HS), HS)
        return [dot(pick, ref[:, cols], NN).astype(jnp.bfloat16) for ref in (q_ref, k_ref, v_ref)]

    def to_peer(o, what):
        peer = line * RING + lax.rem(pos + o, RING)
        if what == 0:
            src, dst = stage.at[o, 0], qo_ref.at[pos]
        else:
            src, dst = stage.at[o, pl.ds(1, 2)], kvo_ref.at[RING + pos]
        return pltpu.make_async_remote_copy(
            src_ref=src,
            dst_ref=dst,
            send_sem=send_sem.at[what, o],
            recv_sem=recv_sem.at[what, o],
            device_id={"seq": peer},
        )

    def far(s):
        return pltpu.make_async_remote_copy(
            src_ref=kvo_ref.at[RING + s],
            dst_ref=kvo_ref.at[s],
            send_sem=hsend.at[s],
            recv_sem=hrecv.at[s],
            device_id={"seq": me + RING},
        )

    def far_long(s):
        return pltpu.make_async_remote_copy(
            src_ref=kvo_ref.at[RING + s, :, pl.ds(0, LROWS)],
            dst_ref=kvo_ref.at[s, :, pl.ds(0, LROWS)],
            send_sem=hsend.at[s],
            recv_sem=hrecv.at[s],
            device_id={"seq": me + RING},
        )

    def start(o, _):
        for i, rows in enumerate(packed(lax.rem(pos + o, RING))):
            stage[o, i] = rows
        to_peer(o, 1).start()
        return 0

    lax.fori_loop(1, RING, start, 0)

    def start_query(o, _):
        to_peer(o, 0).start()
        return 0

    lax.fori_loop(1, RING, start_query, 0)

    to_mate.wait_recv()
    for o in range(1, ROW_LINES):
        along_y(o).start()
    pass_on(0)
    own = packed(pos)
    qo_ref[pos] = own[0]
    kvo_ref[RING + pos, 0] = own[1]
    kvo_ref[RING + pos, 1] = own[2]
    w_all[f] = w_ref[...]
    for o in range(1, ROW_LINES):
        along_y(o).wait_recv()
    for way in range(2):
        along_x(0, 1, way).start()
    to_core(1).start()

    def to_head(j, h):
        return pltpu.make_async_remote_copy(
            src_ref=gstage.at[j],
            dst_ref=do_ref.at[pos],
            send_sem=gsend.at[j],
            recv_sem=grecv.at[pos],
            device_id={"seq": line * RING + h},
        )

    def grad_head(j, _):
        h = slot(j)

        @pl.when(j == 1)
        def _():
            passed(0)

        @pl.when(j == 2)
        def _():
            pass_on(1)

        @pl.when(j == 4)
        def _():
            passed(1)

        @pl.when(j >= 1)
        def _():
            to_core(j).wait_recv()

        full = dot(g_ref[...], w_all[h], NT).astype(jnp.bfloat16)
        rows = dot(pick_matrix(phase_ref[h]), full, NN).astype(jnp.bfloat16)

        @pl.when(h == pos)
        def _():
            do_ref[pos] = rows

        @pl.when(h != pos)
        def _():
            gstage[j] = rows
            to_head(j, h).start()

        return 0

    lax.fori_loop(0, RING, grad_head, 0)

    def forward(o, _):
        s = lax.rem(pos + RING - o, RING)

        @pl.when(o > 0)
        def _():
            to_peer(o, 1).wait_recv()

        @pl.when((line < ROW_LINES - 1) & (s >= RING // 2))
        def _():
            far(s).start()

        @pl.when((lax.rem(line, 2) == 0) & (s < RING // 2))
        def _():
            far_long(s).start()

        return 0

    lax.fori_loop(0, RING, forward, 0)


    phase = phase_ref[pos]
    odd = lax.rem(line, 2)
    origin = (line - 1) * (RING * TOK)
    row = lax.broadcasted_iota(jnp.int32, (ROWS, LROWS), 0)
    off_ref[0] = token_of(row, phase)
    off_ref[1] = (row // LROWS) * TOK + 4 * (row & (LROWS - 1)) + phase

    def low_of(tok, lengths, count):
        low = jnp.full_like(tok, -origin)
        end = -origin
        for n in range(count):
            end = end + lengths[n]
            low = jnp.where(tok >= end, jnp.maximum(low, end), low)
        return low

    lane = lax.broadcasted_iota(jnp.int32, (1, ROWS), 1)
    query_off = token_of(lane, phase)
    pair_off = (lane // LROWS) * TOK + 4 * (lane & (LROWS - 1)) + phase

    def prepare_query(i, _):
        tok = (RING + i) * TOK + query_off
        rows_ref[i, pl.ds(0, 1), :] = tok
        rows_ref[i, pl.ds(1, 1), :] = low_of(tok, short_ref, short_ref.shape[0])
        return 0

    lax.fori_loop(0, RING, prepare_query, 0)

    def prepare_pair(ii, _):
        tok = (RING + 2 * ii) * TOK + pair_off
        rows_ref[RING + ii, pl.ds(0, 1), :] = tok
        rows_ref[RING + ii, pl.ds(1, 1), :] = low_of(tok, long_ref, long_ref.shape[0])
        return 0

    lax.fori_loop(0, PAIRS, prepare_pair, 0)

    st_ref[:, pl.ds(0, 1), :] = jnp.full((STATS, 1, ROWS), NEG, jnp.float32)
    st_ref[:, pl.ds(1, 3), :] = jnp.zeros((STATS, 3, ROWS), jnp.float32)
    acc[...] = jnp.zeros_like(acc)
    dq_acc[...] = jnp.zeros_like(dq_acc)
    lo_ref[...] = jnp.zeros_like(lo_ref)

    @pl.when(line == 0)
    def _():
        kvo_ref[pl.ds(0, RING)] = jnp.zeros((RING, 2, ROWS, HS), jnp.bfloat16)

    def prepare_key(g, _):
        kt_ref[g, 0] = kvo_ref[g, 0].T
        kt_ref[g, 1] = kvo_ref[g, 1].T
        return 0

    def prepare_key_pair(kp, _):
        for e in range(2):
            for w in range(2):
                lkv_ref[kp, w, pl.ds(e * LROWS, LROWS), :] = kvo_ref[
                    2 * kp + e, w, pl.ds(0, LROWS), :
                ]
        cols = pl.ds(pl.multiple_of(lax.rem(kp, 2) * ROWS, ROWS), ROWS)
        lkt_ref[kp // 2, 0, :, cols] = lkv_ref[kp, 0].T
        lkt_ref[kp // 2, 1, :, cols] = lkv_ref[kp, 1].T
        return 0

    def prepare_long_query(ii, _):
        for e in range(2):
            lq_ref[ii, 0, pl.ds(e * LROWS, LROWS), :] = qo_ref[2 * ii + e, pl.ds(0, LROWS), :]
        return 0

    lax.fori_loop(RING, 2 * RING, prepare_key, 0)
    lax.fori_loop(PAIRS, 2 * PAIRS, prepare_key_pair, 0)

    def got_query(o, _):
        to_peer(o, 0).wait_recv()
        return 0

    lax.fori_loop(1, RING, got_query, 0)

    lax.fori_loop(0, PAIRS, prepare_long_query, 0)

    def strip(i, _):
        tok = rows_ref[i, pl.ds(0, 1), :]
        low = rows_ref[i, pl.ds(1, 1), :]
        q = qo_ref[i]
        off = jnp.concatenate([off_ref[0], off_ref[0]], axis=1)
        tops = []
        for d in range(NEAR):
            g = RING + i - d
            s = dot(kvo_ref[g, 0], q, NT)
            live = off >= low - g * TOK
            if d == 0:
                live = live & (off <= tok - g * TOK)
            s = jnp.where(live, s, NEG)
            s_ref[d] = s
            tops.append(jnp.max(s, axis=0, keepdims=True))
        m = functools.reduce(jnp.maximum, tops)
        l, o = jnp.zeros((1, ROWS), jnp.float32), jnp.zeros((HS, ROWS), jnp.float32)
        for d in range(NEAR):
            p = jnp.exp2((s_ref[d] - m) * EXP_SCALE)
            l = l + jnp.sum(p, axis=0, keepdims=True)
            w = p.astype(jnp.bfloat16)
            p_ref[i, d] = w
            o = o + dot(kt_ref[RING + i - d, 1], w, NN)
        st_ref[i, pl.ds(0, 1), :] = m
        st_ref[i, pl.ds(1, 1), :] = l
        o_ref[i] = o
        return 0

    def chunk(ii, c):
        tok = rows_ref[RING + ii, pl.ds(0, 1), :]
        low = rows_ref[RING + ii, pl.ds(1, 1), :]
        q = lq_ref[ii, 0]
        off = jnp.concatenate([off_ref[1], off_ref[1]], axis=1)
        scores = []
        for e in range(2):
            kp = 2 * c + e
            s = dot(lkv_ref[kp, 0], q, NT)
            at = kp * (2 * TOK)
            scores.append(jnp.where((off >= low - at) & (off <= tok - at), s, NEG))
        m = jnp.maximum(*[jnp.max(s, axis=0, keepdims=True) for s in scores])
        l = jnp.zeros((1, ROWS), jnp.float32)
        parts = []
        for e in range(2):
            p = jnp.exp2((scores[e] - m) * EXP_SCALE)
            l = l + jnp.sum(p, axis=0, keepdims=True)
            w = p.astype(jnp.bfloat16)
            lp_ref[ii, 2 * c + e] = w
            parts.append(w)
        t = RING + ii * PAIRS + c
        st_ref[t, pl.ds(0, 1), :] = m
        st_ref[t, pl.ds(1, 1), :] = l
        lo_ref[ii, c] = dot(lkt_ref[c, 1], jnp.concatenate(parts, axis=0), NN)

    def own_chunks(ii, _):
        chunk(ii, 2)

        @pl.when(ii >= 2)
        def _():
            chunk(ii, 3)

        return 0

    lax.fori_loop(0, PAIRS, own_chunks, 0)
    lax.fori_loop(RING // 2, RING, strip, 0)

    def got_far(s, _):
        @pl.when((line > 0) & (s >= RING // 2))
        def _():
            far(s).wait_recv()

        @pl.when((odd == 1) & (s < RING // 2))
        def _():
            far_long(s).wait_recv()

        return 0

    lax.fori_loop(0, RING, got_far, 0)
    lax.fori_loop(RING // 2, RING, prepare_key, 0)
    lax.fori_loop(0, RING // 2, strip, 0)

    @pl.when(odd == 1)
    def _():
        lax.fori_loop(0, PAIRS, prepare_key_pair, 0)

        def far_chunks(n, _):
            chunk(n // 2, lax.rem(n, 2))
            return 0

        lax.fori_loop(0, 2 * PAIRS, far_chunks, 0)

    def got_grad(j, _):
        @pl.when(j != pos)
        def _():
            pltpu.make_async_remote_copy(
                src_ref=gstage.at[j],
                dst_ref=do_ref.at[j],
                send_sem=gsend.at[j],
                recv_sem=grecv.at[j],
                device_id={"seq": line * RING + lax.rem(pos + 1, RING)},
            ).wait_recv()

        return 0

    lax.fori_loop(0, RING, got_grad, 0)

    def join(ii, _):
        base = RING + ii * PAIRS
        lst = [st_ref[base + c] for c in range(PAIRS)]
        tops, invs, deltas = [], [], []
        for e in range(2):
            i = 2 * ii + e
            lq_ref[ii, 1, pl.ds(e * LROWS, LROWS), :] = do_ref[i, pl.ds(0, LROWS), :]
            here = slice(e * LROWS, (e + 1) * LROWS)
            m = st_ref[i, pl.ds(0, 1), :]
            ml = functools.reduce(jnp.maximum, [a[0:1, here] for a in lst], m[:, :LROWS])
            w = jnp.exp2((m - jnp.concatenate([ml, m[:, LROWS:]], axis=1)) * EXP_SCALE)
            wl = [jnp.exp2((a[0:1, here] - ml) * EXP_SCALE) for a in lst]
            l = w * st_ref[i, pl.ds(1, 1), :]
            ll = sum((x * a[1:2, here] for x, a in zip(wl, lst)), l[:, :LROWS])
            inv = 1.0 / jnp.concatenate([ll, l[:, LROWS:]], axis=1)
            o = o_ref[i] * w
            ol = o[:, :LROWS]
            for c in range(PAIRS):
                ol = ol + lo_ref[ii, c, :, here] * wl[c]
            o = jnp.concatenate([ol, o[:, LROWS:]], axis=1)
            gt = do_ref[i].T.astype(jnp.float32)
            delta = jnp.sum(gt * (o * inv), axis=0, keepdims=True)
            delta_ref[i, pl.ds(0, 1), :] = delta
            st_ref[i, pl.ds(3, 1), :] = w * inv
            tops.append(ml)
            invs.append(inv[:, :LROWS])
            deltas.append(delta[:, :LROWS])
        ml = jnp.concatenate(tops, axis=1)
        il = jnp.concatenate(invs, axis=1)
        delta_ref[RING + ii, pl.ds(0, 1), :] = jnp.concatenate(deltas, axis=1)
        for c in range(PAIRS):
            st_ref[base + c, pl.ds(3, 1), :] = jnp.exp2((lst[c][0:1] - ml) * EXP_SCALE) * il
        return 0

    lax.fori_loop(0, PAIRS, join, 0)

    def back(weights, scales, deltas, v, kt, q, do):
        dp = dot(v, do, NT)
        pbs, dss = [], []
        for u, (w, a, delta) in enumerate(zip(weights, scales, deltas)):
            pr = w.astype(jnp.float32) * a
            dss.append((pr * (dp[:, u * ROWS : (u + 1) * ROWS] - delta)).astype(jnp.bfloat16))
            pbs.append(pr.astype(jnp.bfloat16))
        ds = jnp.concatenate(dss, axis=1)
        pb = jnp.concatenate(pbs, axis=1)
        return dot(ds, q, NN), dot(pb, do, NN), dot(kt, ds, NN)

    def back_pair(kp, first, count):
        cols = pl.ds(pl.multiple_of(lax.rem(kp, 2) * ROWS, ROWS), ROWS)
        dk, dv, dq = back(
            [lp_ref[first + u, kp] for u in range(count)],
            [
                st_ref[RING + (first + u) * PAIRS + kp // 2, pl.ds(3, 1), :]
                for u in range(count)
            ],
            [delta_ref[RING + first + u, pl.ds(0, 1), :] for u in range(count)],
            lkv_ref[kp, 1],
            lkt_ref[kp // 2, 0, :, cols],
            lq_ref[pl.ds(first, count), 0].reshape(count * ROWS, HS),
            lq_ref[pl.ds(first, count), 1].reshape(count * ROWS, HS),
        )
        for e in range(2):
            part = slice(e * LROWS, (e + 1) * LROWS)
            acc[2 * kp + e, 0, pl.ds(0, LROWS), :] += dk[part]
            acc[2 * kp + e, 1, pl.ds(0, LROWS), :] += dv[part]
        for u in range(count):
            for e in range(2):
                at = u * ROWS + e * LROWS
                dq_acc[2 * (first + u) + e, :, pl.ds(0, LROWS)] += dq[:, at : at + LROWS]

    def back_block(g, first, count):
        d = RING + first - g
        dk, dv, dq = back(
            [p_ref[first + u, d + u] for u in range(count)],
            [st_ref[first + u, pl.ds(3, 1), :] for u in range(count)],
            [delta_ref[first + u, pl.ds(0, 1), :] for u in range(count)],
            kvo_ref[g, 1],
            kt_ref[g, 0],
            qo_ref[pl.ds(first, count)].reshape(count * ROWS, HS),
            do_ref[pl.ds(first, count)].reshape(count * ROWS, HS),
        )
        acc[g, 0] += dk
        acc[g, 1] += dv
        for u in range(count):
            dq_acc[first + u] += dq[:, u * ROWS : (u + 1) * ROWS]

    def give(s):
        return pltpu.make_async_remote_copy(
            src_ref=far_stage.at[s],
            dst_ref=near.at[s],
            send_sem=fsend.at[s],
            recv_sem=frecv.at[s],
            device_id={"seq": me - RING},
        )

    def give_long(s):
        return pltpu.make_async_remote_copy(
            src_ref=far_stage.at[s, :, pl.ds(0, LROWS)],
            dst_ref=near.at[s, :, pl.ds(0, LROWS)],
            send_sem=fsend.at[s],
            recv_sem=frecv.at[s],
            device_id={"seq": me - RING},
        )

    def home(s, what):
        if what == 0:
            src, dst = dq_stage.at[s], got_q.at[pos]
        else:
            src, dst = kv_stage.at[s], got_kv.at[pos]
        return pltpu.make_async_remote_copy(
            src_ref=src,
            dst_ref=dst,
            send_sem=bsend.at[what, s],
            recv_sem=brecv.at[what, pos],
            device_id={"seq": line * RING + s},
        )

    def landed(s, what):
        dst = got_q.at[s] if what == 0 else got_kv.at[s]
        src = dq_stage.at[s] if what == 0 else kv_stage.at[s]
        return pltpu.make_async_remote_copy(
            src_ref=src,
            dst_ref=dst,
            send_sem=bsend.at[what, s],
            recv_sem=brecv.at[what, s],
            device_id={"seq": line * RING + lax.rem(pos + 1, RING)},
        )

    def emit_far(g):
        far_stage[g, 0] = (acc[g, 0] * SCALE).astype(jnp.bfloat16)
        far_stage[g, 1] = acc[g, 1].astype(jnp.bfloat16)

    @pl.when(odd == 1)
    def _():
        def far_pair(kp, _):
            back_pair(kp, 0, PAIRS)

            @pl.when(kp < PAIRS // 2)
            def _():
                for e in range(2):
                    emit_far(2 * kp + e)
                    give_long(2 * kp + e).start()

            return 0

        lax.fori_loop(0, PAIRS, far_pair, 0)

    @pl.when(line > 0)
    def _():
        for g in range(RING // 2, RING):
            back_block(g, 0, g - (RING - NEAR))
            emit_far(g)
            give(g).start()

    def joined(b):
        full = (line < ROW_LINES - 1) & (b >= RING // 2)
        half = (odd == 0) & (b < RING // 2)
        return full, half

    def own_block(b, count):
        back_block(RING + b, b, count)
        dq_stage[b] = (dq_acc[b].T * SCALE).astype(jnp.bfloat16)

        @pl.when(b != pos)
        def _():
            home(b, 0).start()

        full, half = joined(b)

        @pl.when(jnp.logical_not(full | half))
        def _():
            kv_stage[b, 0] = (acc[RING + b, 0] * SCALE).astype(jnp.bfloat16)
            kv_stage[b, 1] = acc[RING + b, 1].astype(jnp.bfloat16)

            @pl.when(b != pos)
            def _():
                home(b, 1).start()

    def own_block_near(b, _):
        own_block(b, NEAR)
        return 0

    for kp in range(PAIRS):
        back_pair(PAIRS + kp, kp, PAIRS - kp)
        if 2 * kp + NEAR < RING:
            lax.fori_loop(2 * kp, 2 * kp + 2, own_block_near, 0)
        else:
            for e in range(2):
                own_block(2 * kp + e, RING - 2 * kp - e)

    def add_near(b, _):
        full, half = joined(b)

        @pl.when(full)
        def _():
            give(b).wait_recv()

        @pl.when(half)
        def _():
            give_long(b).wait_recv()
            near[b, :, pl.ds(LROWS, LROWS)] = jnp.zeros((2, LROWS, HS), jnp.bfloat16)

        @pl.when(full | half)
        def _():
            kv_stage[b, 0] = (acc[RING + b, 0] * SCALE + near[b, 0].astype(jnp.float32)).astype(
                jnp.bfloat16
            )
            kv_stage[b, 1] = (acc[RING + b, 1] + near[b, 1].astype(jnp.float32)).astype(
                jnp.bfloat16
            )

            @pl.when(b != pos)
            def _():
                home(b, 1).start()

        return 0

    lax.fori_loop(0, RING, add_near, 0)
    got_q[pos] = dq_stage[pos]
    got_kv[pos] = kv_stage[pos]

    def arrived(o, _):
        h = lax.rem(pos + RING - o, RING)
        landed(h, 0).wait_recv()
        landed(h, 1).wait_recv()
        return 0

    lax.fori_loop(1, RING, arrived, 0)

    def finish(o, _):
        s = lax.rem(pos + o, RING)
        home(s, 0).wait_send()
        home(s, 1).wait_send()
        return 0

    lax.fori_loop(1, RING, finish, 0)

    def finish_far(s, _):
        @pl.when((line > 0) & (s >= RING // 2))
        def _():
            give(s).wait_send()

        @pl.when((odd == 1) & (s < RING // 2))
        def _():
            give_long(s).wait_send()

        return 0

    lax.fori_loop(0, RING, finish_far, 0)

    def sent(o, _):
        to_peer(o, 0).wait_send()
        to_peer(o, 1).wait_send()
        return 0

    lax.fori_loop(1, RING, sent, 0)

    def sent_grad(j, _):
        h = slot(j)

        @pl.when(h != pos)
        def _():
            to_head(j, h).wait_send()

        return 0

    lax.fori_loop(0, RING, sent_grad, 0)

    def sent_far(s, _):
        @pl.when((line < ROW_LINES - 1) & (s >= RING // 2))
        def _():
            far(s).wait_send()

        @pl.when((lax.rem(line, 2) == 0) & (s < RING // 2))
        def _():
            far_long(s).wait_send()

        return 0

    lax.fori_loop(0, RING, sent_far, 0)
    to_mate.wait_send()
    for o in range(1, ROW_LINES):
        along_y(o).wait_send()
    for step in range(2):
        for kind in range(2):
            for way in range(2):
                along_x(step, kind, way).wait_send()
    for j in range(1, 8):
        to_core(j).wait_send()


def spread(phase_ref, q_ref, kv_ref, gq_ref, gk_ref, gv_ref):
    tok = lax.broadcasted_iota(jnp.int32, (TOK, ROWS), 0)
    row = lax.broadcasted_iota(jnp.int32, (1, ROWS), 1)
    for e in range(2):
        of_row = token_of(row, phase_ref[2 * pl.program_id(0) + e])
        put = jnp.where(tok == of_row, 1.0, 0.0).astype(jnp.bfloat16)
        rows = jnp.concatenate([q_ref[e], kv_ref[e, 0], kv_ref[e, 1]], axis=1)
        full = dot(put, rows, NN).astype(jnp.bfloat16)
        here = pl.ds(e * HS, HS)
        gq_ref[:, here] = full[:, :HS]
        gk_ref[:, here] = full[:, HS : 2 * HS]
        gv_ref[:, here] = full[:, 2 * HS :]


VM = pl.BlockSpec(memory_space=pltpu.VMEM)
SM = pl.BlockSpec(memory_space=pltpu.SMEM)
DMA = pltpu.SemaphoreType.DMA
BF = jnp.bfloat16


def shaped(*dims, dtype=BF):
    return jax.ShapeDtypeStruct(dims, dtype)


def shards(q, k, v, grad_mixed, out_weight, head_phase, segments_short, segments_long):
    me = lax.axis_index("seq")
    line, pos = me // RING, lax.rem(me, RING)
    f32, i32 = jnp.float32, jnp.int32
    got_q, got_kv = pl.pallas_call(
        layer,
        out_shape=(shaped(RING, ROWS, HS), shaped(RING, 2, ROWS, HS)),
        in_specs=[SM, SM, SM, VM, VM, VM, VM, VM],
        out_specs=(VM, VM),
        scratch_shapes=[
            pltpu.VMEM((RING, 3, ROWS, HS), BF),
            pltpu.VMEM((RING, ROWS, HS), BF),
            pltpu.VMEM((HEADS, HS, grad_mixed.shape[2]), BF),
            pltpu.VMEM((RING, ROWS, HS), BF),
            pltpu.VMEM((2 * RING, 2, ROWS, HS), BF),
            pltpu.VMEM((RING, ROWS, HS), BF),
            pltpu.VMEM((2 * RING, 2, HS, ROWS), BF),
            pltpu.VMEM((2 * PAIRS, 2, ROWS, HS), BF),
            pltpu.VMEM((PAIRS, 2, HS, 2 * ROWS), BF),
            pltpu.VMEM((PAIRS, 2, ROWS, HS), BF),
            pltpu.VMEM((2, ROWS, LROWS), i32),
            pltpu.VMEM((RING + PAIRS, 8, ROWS), i32),
            pltpu.VMEM((NEAR, ROWS, ROWS), f32),
            pltpu.VMEM((RING, NEAR, ROWS, ROWS), BF),
            pltpu.VMEM((PAIRS, 2 * PAIRS, ROWS, ROWS), BF),
            pltpu.VMEM((RING, HS, ROWS), f32),
            pltpu.VMEM((PAIRS, PAIRS, HS, ROWS), f32),
            pltpu.VMEM((STATS, 8, ROWS), f32),
            pltpu.VMEM((RING + PAIRS, 8, ROWS), f32),
            pltpu.VMEM((2 * RING, 2, ROWS, HS), f32),
            pltpu.VMEM((RING, HS, ROWS), f32),
            pltpu.VMEM((RING, 2, ROWS, HS), BF),
            pltpu.VMEM((RING, 2, ROWS, HS), BF),
            pltpu.VMEM((RING, ROWS, HS), BF),
            pltpu.VMEM((RING, 2, ROWS, HS), BF),
            DMA((2, RING)),
            DMA((2, RING)),
            DMA((RING,)),
            DMA((RING,)),
            DMA((RING,)),
            DMA((RING,)),
            DMA,
            DMA,
            DMA((ROW_LINES,)),
            DMA((ROW_LINES,)),
            DMA((2, 2, 2)),
            DMA((2, 2, 2)),
            DMA((RING,)),
            DMA((RING,)),
            DMA((2, RING)),
            DMA((2, RING)),
            DMA((RING,)),
            DMA((RING,)),
        ],
        compiler_params=pltpu.CompilerParams(
            collective_id=0, has_side_effects=True, vmem_limit_bytes=VMEM_LIMIT
        ),
        name="layer",
    )(
        head_phase,
        segments_short,
        segments_long,
        q[0],
        k[0],
        v[0],
        grad_mixed[0],
        out_weight,
    )
    block = pl.BlockSpec((TOK, 2 * HS), lambda h: (0, h))
    gq, gk, gv = pl.pallas_call(
        spread,
        grid=(HEADS // 2,),
        out_shape=(shaped(TOK, HEADS * HS),) * 3,
        in_specs=[
            SM,
            pl.BlockSpec((2, ROWS, HS), lambda h: (h, 0, 0)),
            pl.BlockSpec((2, 2, ROWS, HS), lambda h: (h, 0, 0, 0)),
        ],
        out_specs=(block,) * 3,
        name="spread",
    )(head_phase, got_q, got_kv)
    return gq[None], gk[None], gv[None]


def solution(mesh):
    placed = (
        P("fsdp", "seq", None),
        P("fsdp", "seq", None),
        P("fsdp", "seq", None),
        P("fsdp", "seq", None),
        P("fsdp", None),
        P(),
        P(),
        P(),
    )
    return jax.shard_map(
        shards,
        mesh=mesh,
        in_specs=placed,
        out_specs=(P("fsdp", "seq", None), P("fsdp", "seq", None), P("fsdp", "seq", None)),
        check_vma=False,
    )
```
